512 devices in a mesh: row: 32 (over x, y, core), col: 16 (over z).
Axes of the slice: x: 4, y: 4, z: 16, core: 2. Of those that a mesh axis runs over, the one named last changes fastest.
Arguments:
- src_embed: float32 [32, 32768], P(None, 'row'), may hold values from -20 to 20, as said below
- tgt_embed: float32 [32, 24576], P(None, 'col'), may hold values from -20 to 20, as said below
Outputs:
- src_potential: float32 [32768], P('row')
- tgt_potential: float32 [24576], P('col')
- src_image: float32 [32, 32768], P(None, 'row')
- tgt_image: float32 [32, 24576], P(None, 'col')
The draws below stay inside these ranges and needn't reach their ends.
Inputs may be any that keep to these rules, and one draw needn't show every extreme that they name: `src_embed`: real-valued coordinates of order one to a few units. `tgt_embed`: real-valued coordinates of order one to a few units.
All inputs are finite; a program needn't handle non-finite values.
Results may differ from the reference program's by a relative error of at most 0.0003.
Values sent between devices are 32-bit elements; how exact they have to be, the bound alone decides.
No kernel may reach another device: no remote copies, remote signals or barrier semaphores. Data moves between devices by JAX's collectives and lax.ppermute only.
A program may use at most 64 MiB of HBM per device.

```python
import math
import jax
import jax.numpy as jnp
from jax import lax

DIM = 32
SR_DEV = 1024
ITERS = 3
NS = 32768
NT = 24576
N_ROW = 32


def shared_noise(key):
    return jax.random.normal(jax.random.fold_in(key, 11), (DIM, NS), jnp.float32)


def draw_src_embed(key, part):
    base = shared_noise(key)
    return 0.5 * base


def draw_tgt_embed(key, part):
    key = jax.random.fold_in(key, 2)
    own = jax.random.normal(jax.random.fold_in(key, 5), (DIM, NT), jnp.float32)
    return 0.5 * own


def setup_inputs(seed: int = 0) -> dict:
    arg_keys = jax.random.split(jax.random.key(seed), 3)
    src_embed = draw_src_embed(jax.random.fold_in(arg_keys[2], 71), 0)
    tgt_embed = draw_tgt_embed(jax.random.fold_in(arg_keys[2], 71), 0)
    return dict(src_embed=src_embed, tgt_embed=tgt_embed)


epsilon = 1.0


def cost_rows(src_embed, sq_src, tgt_embed, sq_tgt, index):
    start = (index * SR_DEV).astype(jnp.int32)
    block = lax.dynamic_slice_in_dim(src_embed, start, SR_DEV, 1)
    sq_block = lax.dynamic_slice_in_dim(sq_src, start, SR_DEV, 0)
    cross = lax.dot_general(block, tgt_embed, (((0,), (0,)), ((), ())), precision=lax.Precision.HIGHEST, preferred_element_type=jnp.float32)
    return sq_block[:, None] + sq_tgt[None, :] - 2.0 * cross


def reference(src_embed, tgt_embed):
    sq_src = jnp.sum(src_embed * src_embed, axis=0)
    sq_tgt = jnp.sum(tgt_embed * tgt_embed, axis=0)
    indices = jnp.arange(N_ROW, dtype=jnp.int32)
    tgt_potential = jnp.zeros((NT,), jnp.float32)
    src_potential = jnp.zeros((NS,), jnp.float32)
    for step in range(ITERS):
        def row_lse(index):
            scores = (tgt_potential[None, :] - cost_rows(src_embed, sq_src, tgt_embed, sq_tgt, index)) / epsilon
            peak = jnp.max(scores, axis=1)
            return peak + jnp.log(jnp.sum(jnp.exp(scores - peak[:, None]), axis=1))
        lse_rows = lax.map(row_lse, indices).reshape(NS)
        src_potential = -epsilon * (lse_rows - math.log(NT))

        def col_step(carry, index):
            peak, total = carry
            start = (index * SR_DEV).astype(jnp.int32)
            fblock = lax.dynamic_slice_in_dim(src_potential, start, SR_DEV, 0)
            scores = (fblock[:, None] - cost_rows(src_embed, sq_src, tgt_embed, sq_tgt, index)) / epsilon
            new_peak = jnp.maximum(peak, jnp.max(scores, axis=0))
            total = total * jnp.exp(peak - new_peak) + jnp.sum(jnp.exp(scores - new_peak[None, :]), axis=0)
            return (new_peak, total), None
        start_carry = (jnp.full((NT,), -jnp.inf, jnp.float32), jnp.zeros((NT,), jnp.float32))
        (peak, total), unused = lax.scan(col_step, start_carry, indices)
        tgt_potential = -epsilon * (peak + jnp.log(total) - math.log(NS))

    def src_map(index):
        scores = (tgt_potential[None, :] - cost_rows(src_embed, sq_src, tgt_embed, sq_tgt, index)) / epsilon
        peak = jnp.max(scores, axis=1)
        weights = jnp.exp(scores - peak[:, None])
        total = jnp.sum(weights, axis=1)
        moved = lax.dot_general(tgt_embed, weights, (((1,), (1,)), ((), ())), precision=lax.Precision.HIGHEST, preferred_element_type=jnp.float32)
        return moved / total[None, :]
    src_image = jnp.transpose(lax.map(src_map, indices), (1, 0, 2)).reshape(DIM, NS)

    def tgt_step(carry, index):
        peak, total, moved = carry
        start = (index * SR_DEV).astype(jnp.int32)
        fblock = lax.dynamic_slice_in_dim(src_potential, start, SR_DEV, 0)
        xblock = lax.dynamic_slice_in_dim(src_embed, start, SR_DEV, 1)
        scores = (fblock[:, None] - cost_rows(src_embed, sq_src, tgt_embed, sq_tgt, index)) / epsilon
        new_peak = jnp.maximum(peak, jnp.max(scores, axis=0))
        weights = jnp.exp(scores - new_peak[None, :])
        factor = jnp.exp(peak - new_peak)
        total = total * factor + jnp.sum(weights, axis=0)
        moved = moved * factor[None, :] + jnp.dot(xblock, weights, precision=lax.Precision.HIGHEST, preferred_element_type=jnp.float32)
        return (new_peak, total, moved), None
    start_carry = (jnp.full((NT,), -jnp.inf, jnp.float32), jnp.zeros((NT,), jnp.float32), jnp.zeros((DIM, NT), jnp.float32))
    (peak, total, moved), unused = lax.scan(tgt_step, start_carry, indices)
    tgt_image = moved / total[None, :]
    return src_potential, tgt_potential, src_image, tgt_image
```

```python
import functools
import math

import jax
import jax.numpy as jnp
from jax import lax
from jax.experimental import pallas as pl
from jax.experimental.pallas import tpu as pltpu
from jax.sharding import PartitionSpec as P

ITERS = 3
LOG2E = math.log2(math.e)
LN2 = math.log(2.0)
DEPTH = 256
HALF = 128
TILE = 256
CHUNK = 256
PROBE = 256
LOW, HIGH = 2.0**-90, 2.0**100
BF, F32 = jnp.bfloat16, jnp.float32
VMEM = pl.BlockSpec(memory_space=pltpu.VMEM)


def rounded(v):
    return v.astype(BF).astype(F32)


def split(v):
    a = rounded(v)
    b = rounded(v - a)
    return a, b, rounded(v - a - b)


def as_row(v):
    return jnp.concatenate([v[r : r + 1, :] for r in range(v.shape[0])], axis=1)


def as_dense(v):
    return jnp.concatenate(
        [v[:, HALF * r : HALF * (r + 1)] for r in range(v.shape[1] // HALF)], axis=0
    )


def potential_rows(v, first):
    a, b, c = split(v)
    row = lax.broadcasted_iota(jnp.int32, (8, v.shape[1]), 0)
    ones = jnp.where((row < 6) & ((row < first) | (row >= first + 3)), 1.0, 0.0).astype(F32)
    out = jnp.where(row == first, a, ones)
    out = jnp.where(row == first + 1, b, out)
    return jnp.where(row == first + 2, c, out)


def row_block(v, first):
    rows = potential_rows(v, first)
    return jnp.concatenate([rows, jnp.zeros_like(rows)], axis=0).astype(BF)


def operand(v, order1, order2, first):
    pieces = split(v)
    n = v.shape[1]
    zero = jnp.zeros((32, n), F32)
    rows = potential_rows(jnp.zeros((1, n), F32), first)
    return jnp.concatenate(
        [pieces[k] for k in order1]
        + [zero, rows, zero[:8]]
        + [pieces[k] for k in order2]
        + [zero[:16]],
        axis=0,
    )


SRC = dict(order1=(0, 0, 1), order2=(0, 2, 1), first=0)
TGT = dict(order1=(0, 1, 0), order2=(2, 0, 1), first=3)


def column_half(v, first, static_ref):
    rows = potential_rows(v, first)
    n = v.shape[1]
    keep = lax.broadcasted_iota(jnp.int32, (8, n), 0)
    rows = jnp.where((keep >= first) & (keep < first + 3), rows, 0.0)
    wide = jnp.concatenate([rows, jnp.zeros((HALF - 8, n), F32)], axis=0)
    return static_ref[:, HALF:] + jnp.transpose(wide).astype(BF)


def tile_of(row_ref, block, start):
    cols = pl.ds(start, TILE)
    return jnp.concatenate(
        [row_ref[:HALF, cols], block, row_ref[HALF + 16 :, cols]], axis=0
    )


def scores(col_ref, half_ref, start, rhs):
    rows = pl.ds(start, CHUNK)
    lhs = jnp.concatenate([col_ref[rows, :HALF], half_ref[rows, :]], axis=1)
    return jnp.dot(lhs, rhs, preferred_element_type=F32)


def sums(col_ref, half_ref, row_ref, shift_ref, s_ref, first):
    count, n = col_ref.shape[0], row_ref.shape[1]
    for t in range(n // TILE):
        cols = slice(t * TILE, (t + 1) * TILE)
        rhs = tile_of(row_ref, row_block(shift_ref[:, cols], first), t * TILE)
        acc = jnp.zeros((8, TILE), F32)
        for c in range(count // CHUNK):
            s = scores(col_ref, half_ref, c * CHUNK, rhs)
            acc += jnp.sum(jnp.exp2(s).reshape(CHUNK // 8, 8, TILE), axis=0)
        s_ref[:, cols] = jnp.sum(acc, axis=0, keepdims=True)


def peaks(col_ref, half_ref, row_ref, shift_ref, first, count):
    n = row_ref.shape[1]

    @pl.loop(0, n // TILE)
    def _(t):
        start = pl.multiple_of(t * TILE, TILE)
        rhs = tile_of(row_ref, row_block(jnp.zeros((1, TILE), F32), first), start)

        def step(c, acc):
            s = scores(col_ref, half_ref, pl.multiple_of(c * CHUNK, CHUNK), rhs)
            return jnp.maximum(acc, jnp.max(s.reshape(CHUNK // 8, 8, TILE), axis=0))

        acc = lax.fori_loop(0, count // CHUNK, step, jnp.full((8, TILE), -jnp.inf, F32))
        shift_ref[:, pl.ds(start, TILE)] = -jnp.max(acc, axis=0, keepdims=True)


def outside(s):
    return jnp.any(jnp.logical_not((s > LOW) & (s < HIGH)))


def local_lse(col_ref, half_ref, row_ref, shift_ref, s_ref, first):
    args = (col_ref, half_ref, row_ref, shift_ref)
    sums(*args, s_ref, first)

    @pl.when(outside(s_ref[...]))
    def _():
        peaks(*args, first, col_ref.shape[0])
        sums(*args, s_ref, first)

    return jnp.log2(s_ref[...]) - shift_ref[...]


def joined(parts):
    peak = jnp.max(parts, axis=0)
    return peak + jnp.log2(jnp.sum(jnp.exp2(parts - peak[None]), axis=0))


def send_all(out_ref, v):
    out_ref[...] = jnp.broadcast_to(v[None], out_ref.shape)


def start_kernel(
    x_ref, y_ref,
    xt_ref, yt_ref, xr_ref, yr_ref, xsq_ref, ysq_ref, out_ref,
    half_ref, shift_ref, s_ref,
):
    x, y = x_ref[...], y_ref[...]
    xr = operand(x * (2.0 * LOG2E), **SRC)
    yr = operand(y, **TGT)
    xr_ref[...] = xr.astype(BF)
    yr_ref[...] = yr.astype(BF)
    xt_ref[...] = jnp.transpose(xr).astype(BF)
    yt_ref[...] = jnp.transpose(yr).astype(BF)
    xsq_ref[...] = as_dense(jnp.sum(x * x, axis=0, keepdims=True))
    ysq = jnp.sum(y * y, axis=0, keepdims=True)
    ysq_ref[...] = as_dense(ysq)
    half_ref[...] = column_half(ysq * -LOG2E, 3, yt_ref)
    args = (yt_ref, half_ref, xr_ref, shift_ref)
    peaks(*args, 0, PROBE)
    send_all(out_ref, as_dense(local_lse(*args, s_ref, 0)))


def lse_kernel(
    total, col_first, row_first,
    parts_ref, col_ref, row_ref, old_ref,
    new_ref, out_ref,
    half_ref, shift_ref, s_ref,
):
    new = math.log2(total) - joined(parts_ref[...])
    new_ref[...] = new
    half_ref[...] = column_half(as_row(new), col_first, col_ref)
    args = (col_ref, half_ref, row_ref, shift_ref)
    if old_ref is None:
        peaks(*args, row_first, PROBE)
    else:
        shift_ref[...] = as_row(old_ref[...])
    send_all(out_ref, as_dense(local_lse(*args, s_ref, row_first)))


def maps(col_ref, half_ref, row_ref, block_ref, values_ref, moved_ref, exact):
    n = row_ref.shape[1]

    def chunk(c, unused):
        start = pl.multiple_of(c * CHUNK, CHUNK)
        if exact:
            peak = jnp.full((CHUNK, 1), -jnp.inf, F32)
            for t in range(n // TILE):
                cols = slice(t * TILE, (t + 1) * TILE)
                rhs = tile_of(row_ref, block_ref[:, cols], t * TILE)
                s = scores(col_ref, half_ref, start, rhs)
                peak = jnp.maximum(peak, jnp.max(s, axis=1, keepdims=True))
        total = jnp.zeros((CHUNK, HALF), F32)
        for t in range(n // TILE):
            cols = slice(t * TILE, (t + 1) * TILE)
            rhs = tile_of(row_ref, block_ref[:, cols], t * TILE)
            s = scores(col_ref, half_ref, start, rhs)
            w = jnp.exp2(s - peak) if exact else jnp.exp2(s)
            high = w.astype(BF)
            low = (w - high.astype(F32)).astype(BF)
            values = values_ref[cols, HALF:]
            total += jnp.dot(high, values, preferred_element_type=F32)
            total += jnp.dot(low, values, preferred_element_type=F32)
        if exact:
            lane = lax.broadcasted_iota(jnp.int32, (CHUNK, HALF), 1)
            total = jnp.where(lane == HALF - 1, peak, total)
        moved_ref[pl.ds(start, CHUNK), :] = total
        return unused

    chunks = col_ref.shape[0] // CHUNK
    if exact:
        lax.fori_loop(0, chunks, chunk, 0)
    else:
        for c in range(chunks):
            chunk(c, 0)


def image_kernel(
    total, col_first, row_first, dims, scale,
    parts_ref, col_ref, row_ref, values_ref, old_ref,
    *refs,
):
    new_ref, out_ref = refs[:2]
    half_ref, block_ref, moved_ref, across_ref, shift_ref, image_ref = refs[-6:]
    rows = old_ref.shape[0]
    if len(refs) > 8:
        share_ref = refs[2]
        parts = parts_ref[...]
        logs = parts[:, : new_ref.shape[0]]
        peak = jnp.max(logs, axis=0)
        weights = jnp.exp2(logs - peak[None])
        sum_w = jnp.sum(weights, axis=0)
        new = math.log2(total) - (peak + jnp.log2(sum_w))
        send_all(share_ref, share(parts, weights, sum_w))
    else:
        new = math.log2(total) - joined(parts_ref[...])
    new_ref[...] = new
    block_ref[...] = row_block(as_row(new), row_first)
    shift = as_row(old_ref[...])
    shift_ref[...] = shift
    half_ref[...] = column_half(shift, col_first, col_ref)
    args = (col_ref, half_ref, row_ref, block_ref, values_ref, moved_ref)
    maps(*args, False)
    across_ref[...] = jnp.transpose(moved_ref[...])
    one = 3 - row_first
    one = {0: 3, 3: 0}[row_first]

    @pl.when(outside(across_ref[one : one + 1, :]))
    def _():
        half_ref[...] = col_ref[:, HALF:]
        maps(*args, True)
        across_ref[...] = jnp.transpose(moved_ref[...])
        shift_ref[...] = jnp.zeros_like(shift)

    s = across_ref[one : one + 1, :]
    log = jnp.log2(s) + across_ref[HALF - 1 :, :] - shift_ref[...]
    image = across_ref[16:48, :] + across_ref[48:80, :] + across_ref[80:112, :]
    image = image * (scale / s)
    for r in range(rows):
        image_ref[:, r, :] = image[:, HALF * r : HALF * (r + 1)]
    n = out_ref.shape[0]
    out_ref[:, :rows, :] = jnp.broadcast_to(as_dense(log)[None], (n, rows, HALF))
    for d in range(dims):
        for k in range(n):
            out_ref[k, rows * (d + 1) : rows * (d + 2), :] = image_ref[k * dims + d]


def share(parts, weights, sum_w):
    rows = weights.shape[1]
    out = []
    for d in range(parts.shape[1] // rows - 1):
        part = parts[:, rows * (d + 1) : rows * (d + 2)]
        out.append(jnp.sum(part * weights, axis=0) / sum_w)
    return jnp.concatenate(out, axis=0)


def share_kernel(rows, parts_ref, out_ref):
    parts = parts_ref[...]
    logs = parts[:, :rows]
    weights = jnp.exp2(logs - jnp.max(logs, axis=0)[None])
    send_all(out_ref, share(parts, weights, jnp.sum(weights, axis=0)))


def end_kernel(
    e_ref, h_ref, xsq_ref, ysq_ref, src_ref, tgt_ref, f_ref, g_ref, si_ref, ti_ref
):
    f_ref[...] = LN2 * e_ref[...] + xsq_ref[...]
    g_ref[...] = LN2 * h_ref[...] + ysq_ref[...]
    for parts_ref, out_ref in ((src_ref, si_ref), (tgt_ref, ti_ref)):
        for r in range(parts_ref.shape[1]):
            out_ref[:, HALF * r : HALF * (r + 1)] = parts_ref[:, r, :]


def shape(*dims, dtype=F32):
    return jax.ShapeDtypeStruct(dims, dtype)


def call(kernel, ins, outs, scratch=(), name=None):
    return pl.pallas_call(
        kernel,
        out_shape=outs,
        in_specs=[VMEM] * len(ins),
        out_specs=jax.tree.map(lambda _: VMEM, outs),
        scratch_shapes=list(scratch),
        compiler_params=pltpu.CompilerParams(vmem_limit_bytes=32 * 2**20),
        name=name,
    )(*ins)


def local(x, y):
    ns, nt = x.shape[1], y.shape[1]
    n_row, n_col = lax.axis_size("row"), lax.axis_size("col")
    rs, rt = ns // HALF, nt // HALF
    all_src, all_tgt = ns * n_row, nt * n_col
    dim_src, dim_tgt = x.shape[0] // n_col, x.shape[0] // n_row

    def scratch(m, n):
        return (pltpu.VMEM((m, HALF), BF), pltpu.VMEM((1, n), F32), pltpu.VMEM((1, n), F32))

    def over(axis, v):
        return lax.all_to_all(v, axis, 0, 0)

    xt, yt, xr, yr, xsq, ysq, parts = call(
        start_kernel,
        (x, y),
        (
            shape(ns, DEPTH, dtype=BF),
            shape(nt, DEPTH, dtype=BF),
            shape(DEPTH, ns, dtype=BF),
            shape(DEPTH, nt, dtype=BF),
            shape(rs, HALF),
            shape(rt, HALF),
            shape(n_col, rs, HALF),
        ),
        scratch(nt, ns),
        name="start",
    )
    h = None
    for step in range(ITERS - 1):
        parts = over("col", parts)
        kernel = functools.partial(lse_kernel, all_tgt, 0, 3)
        ins = (parts, xt, yr)
        if h is None:
            base = kernel
            kernel = lambda p, c, r, *refs: base(p, c, r, None, *refs)
        else:
            ins += (h,)
        e, parts = call(
            kernel, ins, (shape(rs, HALF), shape(n_row, rt, HALF)), scratch(ns, nt), name="cols"
        )
        parts = over("row", parts)
        h, parts = call(
            functools.partial(lse_kernel, all_src, 3, 0),
            (parts, yt, xr, e),
            (shape(rt, HALF), shape(n_col, rs, HALF)),
            scratch(nt, ns),
            name="rows",
        )

    def image_scratch(m, n):
        return (
            pltpu.VMEM((m, HALF), BF),
            pltpu.VMEM((16, n), BF),
            pltpu.VMEM((m, HALF), F32),
            pltpu.VMEM((HALF, m), F32),
            pltpu.VMEM((1, m), F32),
            pltpu.VMEM((x.shape[0], m // HALF, HALF), F32),
        )

    parts = over("col", parts)
    e, parts = call(
        functools.partial(image_kernel, all_tgt, 3, 0, dim_tgt, 0.5 * LN2),
        (parts, yt, xr, xt, h),
        (shape(rs, HALF), shape(n_row, rt * (1 + dim_tgt), HALF)),
        image_scratch(nt, ns),
        name="tgt_part",
    )
    parts = over("row", parts)
    h, parts, tgt = call(
        functools.partial(image_kernel, all_src, 0, 3, dim_src, 1.0),
        (parts, xt, yr, yt, e),
        (
            shape(rt, HALF),
            shape(n_col, rs * (1 + dim_src), HALF),
            shape(n_row, rt * dim_tgt, HALF),
        ),
        image_scratch(ns, nt),
        name="src_part",
    )
    parts = over("col", parts)
    src = call(
        functools.partial(share_kernel, rs),
        (parts,),
        shape(n_col, rs * dim_src, HALF),
        name="src_share",
    )
    src = over("col", src).reshape(x.shape[0], rs, HALF)
    tgt = over("row", tgt).reshape(x.shape[0], rt, HALF)
    f, g, si, ti = call(
        end_kernel,
        (e, h, xsq, ysq, src, tgt),
        (shape(rs, HALF), shape(rt, HALF), shape(*x.shape), shape(*y.shape)),
        name="end",
    )
    return f.reshape(ns), g.reshape(nt), si, ti


def solution(mesh):
    in_specs = (P(None, "row"), P(None, "col"))
    out_specs = (P("row"), P("col"), P(None, "row"), P(None, "col"))
    return jax.shard_map(local, mesh=mesh, in_specs=in_specs, out_specs=out_specs, check_vma=False)
```

```python
import functools
import math

import jax
import jax.numpy as jnp
from jax import lax
from jax.experimental import pallas as pl
from jax.experimental.pallas import tpu as pltpu
from jax.sharding import PartitionSpec as P

ITERS = 3
LOG2E = math.log2(math.e)
LN2 = math.log(2.0)
DEPTH = 256
HALF = 128
TILE = 256
CHUNK = 256
PROBE = 64
LOW, HIGH = 2.0**-90, 2.0**100
BF, F32 = jnp.bfloat16, jnp.float32
VMEM = pl.BlockSpec(memory_space=pltpu.VMEM)


def rounded(v):
    return v.astype(BF).astype(F32)


def split(v):
    a = rounded(v)
    b = rounded(v - a)
    return a, b, rounded(v - a - b)


def as_row(v):
    return jnp.concatenate([v[r : r + 1, :] for r in range(v.shape[0])], axis=1)


def as_dense(v):
    return jnp.concatenate(
        [v[:, HALF * r : HALF * (r + 1)] for r in range(v.shape[1] // HALF)], axis=0
    )


def potential_rows(v, first):
    a, b, c = split(v)
    row = lax.broadcasted_iota(jnp.int32, (8, v.shape[1]), 0)
    ones = jnp.where((row < 6) & ((row < first) | (row >= first + 3)), 1.0, 0.0).astype(F32)
    out = jnp.where(row == first, a, ones)
    out = jnp.where(row == first + 1, b, out)
    return jnp.where(row == first + 2, c, out)


def row_block(v, first):
    rows = potential_rows(v, first)
    return jnp.concatenate([rows, jnp.zeros_like(rows)], axis=0).astype(BF)


def operand(v, order1, order2, first):
    pieces = split(v)
    n = v.shape[1]
    zero = jnp.zeros((32, n), F32)
    rows = potential_rows(jnp.zeros((1, n), F32), first)
    return jnp.concatenate(
        [pieces[k] for k in order1]
        + [zero, rows, zero[:8]]
        + [pieces[k] for k in order2]
        + [zero[:16]],
        axis=0,
    )


SRC = dict(order1=(0, 0, 1), order2=(0, 2, 1), first=0)
TGT = dict(order1=(0, 1, 0), order2=(2, 0, 1), first=3)


def column_half(v, first, static_ref):
    rows = potential_rows(v, first)
    n = v.shape[1]
    keep = lax.broadcasted_iota(jnp.int32, (8, n), 0)
    rows = jnp.where((keep >= first) & (keep < first + 3), rows, 0.0)
    wide = jnp.concatenate([rows, jnp.zeros((HALF - 8, n), F32)], axis=0)
    return static_ref[:, HALF:] + jnp.transpose(wide).astype(BF)


def tile_of(row_ref, block, start):
    cols = pl.ds(start, TILE)
    return jnp.concatenate(
        [row_ref[:HALF, cols], block, row_ref[HALF + 16 :, cols]], axis=0
    )


def scores(col_ref, half_ref, start, rhs, count=CHUNK):
    rows = pl.ds(start, count)
    lhs = jnp.concatenate([col_ref[rows, :HALF], half_ref[rows, :]], axis=1)
    return jnp.dot(lhs, rhs, preferred_element_type=F32)


def sums(col_ref, half_ref, row_ref, shift_ref, s_ref, first):
    count, n = col_ref.shape[0], row_ref.shape[1]
    for t in range(n // TILE):
        cols = slice(t * TILE, (t + 1) * TILE)
        rhs = tile_of(row_ref, row_block(shift_ref[:, cols], first), t * TILE)
        acc = jnp.zeros((8, TILE), F32)
        for c in range(count // CHUNK):
            s = scores(col_ref, half_ref, c * CHUNK, rhs)
            acc += jnp.sum(jnp.exp2(s).reshape(CHUNK // 8, 8, TILE), axis=0)
        s_ref[:, cols] = jnp.sum(acc, axis=0, keepdims=True)


def peaks(col_ref, half_ref, row_ref, shift_ref, first, count):
    n = row_ref.shape[1]

    @pl.loop(0, n // TILE)
    def _(t):
        start = pl.multiple_of(t * TILE, TILE)
        rhs = tile_of(row_ref, row_block(jnp.zeros((1, TILE), F32), first), start)

        def step(c, acc):
            s = scores(col_ref, half_ref, pl.multiple_of(c * CHUNK, CHUNK), rhs)
            return jnp.maximum(acc, jnp.max(s.reshape(CHUNK // 8, 8, TILE), axis=0))

        acc = lax.fori_loop(0, count // CHUNK, step, jnp.full((8, TILE), -jnp.inf, F32))
        shift_ref[:, pl.ds(start, TILE)] = -jnp.max(acc, axis=0, keepdims=True)


def probe(col_ref, half_ref, row_ref, shift_ref, first):
    for t in range(row_ref.shape[1] // TILE):
        cols = slice(t * TILE, (t + 1) * TILE)
        rhs = tile_of(row_ref, row_block(jnp.zeros((1, TILE), F32), first), t * TILE)
        s = scores(col_ref, half_ref, 0, rhs, PROBE)
        shift_ref[:, cols] = -jnp.max(s, axis=0, keepdims=True)


def outside(s):
    return jnp.any(jnp.logical_not((s > LOW) & (s < HIGH)))


def local_lse(col_ref, half_ref, row_ref, shift_ref, s_ref, first):
    args = (col_ref, half_ref, row_ref, shift_ref)
    sums(*args, s_ref, first)

    @pl.when(outside(s_ref[...]))
    def _():
        peaks(*args, first, col_ref.shape[0])
        sums(*args, s_ref, first)

    return jnp.log2(s_ref[...]) - shift_ref[...]


def joined(parts):
    peak = jnp.max(parts, axis=0)
    return peak + jnp.log2(jnp.sum(jnp.exp2(parts - peak[None]), axis=0))


def send_all(out_ref, v):
    out_ref[...] = jnp.broadcast_to(v[None], out_ref.shape)


def start_kernel(
    x_ref, y_ref,
    xt_ref, yt_ref, xr_ref, yr_ref, xsq_ref, ysq_ref, out_ref,
    half_ref, shift_ref, s_ref,
):
    x, y = x_ref[...], y_ref[...]
    xr = operand(x * (2.0 * LOG2E), **SRC)
    yr = operand(y, **TGT)
    xr_ref[...] = xr.astype(BF)
    yr_ref[...] = yr.astype(BF)
    xt_ref[...] = jnp.transpose(xr).astype(BF)
    yt_ref[...] = jnp.transpose(yr).astype(BF)
    xsq_ref[...] = as_dense(jnp.sum(x * x, axis=0, keepdims=True))
    ysq = jnp.sum(y * y, axis=0, keepdims=True)
    ysq_ref[...] = as_dense(ysq)
    half_ref[...] = column_half(ysq * -LOG2E, 3, yt_ref)
    args = (yt_ref, half_ref, xr_ref, shift_ref)
    probe(*args, 0)
    send_all(out_ref, as_dense(local_lse(*args, s_ref, 0)))


def lse_kernel(
    total, col_first, row_first,
    parts_ref, col_ref, row_ref, old_ref,
    new_ref, out_ref,
    half_ref, shift_ref, s_ref,
):
    new = math.log2(total) - joined(parts_ref[...])
    new_ref[...] = new
    half_ref[...] = column_half(as_row(new), col_first, col_ref)
    args = (col_ref, half_ref, row_ref, shift_ref)
    if old_ref is None:
        probe(*args, row_first)
    else:
        shift_ref[...] = as_row(old_ref[...])
    send_all(out_ref, as_dense(local_lse(*args, s_ref, row_first)))


def maps(col_ref, half_ref, row_ref, values_ref, shift_ref, moved_ref, first):
    count, n = col_ref.shape[0], row_ref.shape[1]
    for t in range(n // TILE):
        cols = slice(t * TILE, (t + 1) * TILE)
        rhs = tile_of(row_ref, row_block(shift_ref[:, cols], first), t * TILE)
        total = jnp.zeros((HALF, TILE), F32)
        for c in range(count // CHUNK):
            w = jnp.exp2(scores(col_ref, half_ref, c * CHUNK, rhs))
            high = w.astype(BF)
            low = (w - high.astype(F32)).astype(BF)
            values = values_ref[HALF:, c * CHUNK : (c + 1) * CHUNK]
            total += jnp.dot(values, high, preferred_element_type=F32)
            total += jnp.dot(values, low, preferred_element_type=F32)
        moved_ref[:, cols] = total


def potential_kernel(total, parts_ref, new_ref):
    new_ref[...] = math.log2(total) - joined(parts_ref[...])


def join_kernel(total, parts_ref, new_ref, share_ref):
    parts = parts_ref[...]
    logs = parts[:, : new_ref.shape[0]]
    peak = jnp.max(logs, axis=0)
    weights = jnp.exp2(logs - peak[None])
    sum_w = jnp.sum(weights, axis=0)
    new_ref[...] = math.log2(total) - (peak + jnp.log2(sum_w))
    send_all(share_ref, share(parts, weights, sum_w))


def image_kernel(
    dims, scale, col_first, row_first,
    new_ref, col_ref, row_ref, values_ref, old_ref,
    out_ref,
    half_ref, shift_ref, moved_ref, image_ref,
):
    rows = old_ref.shape[0]
    half_ref[...] = column_half(as_row(new_ref[...]), col_first, col_ref)
    shift_ref[...] = as_row(old_ref[...])
    args = (col_ref, half_ref, row_ref)
    maps(*args, values_ref, shift_ref, moved_ref, row_first)
    one = 3 - col_first

    @pl.when(outside(moved_ref[one : one + 1, :]))
    def _():
        peaks(*args, shift_ref, row_first, col_ref.shape[0])
        maps(*args, values_ref, shift_ref, moved_ref, row_first)

    s = moved_ref[one : one + 1, :]
    log = jnp.log2(s) - shift_ref[...]
    image = moved_ref[16:48, :] + moved_ref[48:80, :] + moved_ref[80:112, :]
    image = image * (scale / s)
    for r in range(rows):
        image_ref[:, r, :] = image[:, HALF * r : HALF * (r + 1)]
    n = out_ref.shape[0]
    out_ref[:, :rows, :] = jnp.broadcast_to(as_dense(log)[None], (n, rows, HALF))
    for d in range(dims):
        for k in range(n):
            out_ref[k, rows * (d + 1) : rows * (d + 2), :] = image_ref[k * dims + d]


def share(parts, weights, sum_w):
    rows = weights.shape[1]
    out = []
    for d in range(parts.shape[1] // rows - 1):
        part = parts[:, rows * (d + 1) : rows * (d + 2)]
        out.append(jnp.sum(part * weights, axis=0) / sum_w)
    return jnp.concatenate(out, axis=0)


def share_kernel(rows, parts_ref, out_ref):
    parts = parts_ref[...]
    logs = parts[:, :rows]
    weights = jnp.exp2(logs - jnp.max(logs, axis=0)[None])
    send_all(out_ref, share(parts, weights, jnp.sum(weights, axis=0)))


def end_kernel(
    e_ref, h_ref, xsq_ref, ysq_ref, src_ref, tgt_ref, f_ref, g_ref, si_ref, ti_ref
):
    f_ref[...] = LN2 * e_ref[...] + xsq_ref[...]
    g_ref[...] = LN2 * h_ref[...] + ysq_ref[...]
    for parts_ref, out_ref in ((src_ref, si_ref), (tgt_ref, ti_ref)):
        for r in range(parts_ref.shape[1]):
            out_ref[:, HALF * r : HALF * (r + 1)] = parts_ref[:, r, :]


def shape(*dims, dtype=F32):
    return jax.ShapeDtypeStruct(dims, dtype)


def call(kernel, ins, outs, scratch=(), name=None):
    return pl.pallas_call(
        kernel,
        out_shape=outs,
        in_specs=[VMEM] * len(ins),
        out_specs=jax.tree.map(lambda _: VMEM, outs),
        scratch_shapes=list(scratch),
        compiler_params=pltpu.CompilerParams(vmem_limit_bytes=32 * 2**20),
        name=name,
    )(*ins)


def local(x, y):
    ns, nt = x.shape[1], y.shape[1]
    n_row, n_col = lax.axis_size("row"), lax.axis_size("col")
    rs, rt = ns // HALF, nt // HALF
    all_src, all_tgt = ns * n_row, nt * n_col
    dim_src, dim_tgt = x.shape[0] // n_col, x.shape[0] // n_row

    def scratch(m, n):
        return (pltpu.VMEM((m, HALF), BF), pltpu.VMEM((1, n), F32), pltpu.VMEM((1, n), F32))

    def over(axis, v):
        return lax.all_to_all(v, axis, 0, 0)

    xt, yt, xr, yr, xsq, ysq, parts = call(
        start_kernel,
        (x, y),
        (
            shape(ns, DEPTH, dtype=BF),
            shape(nt, DEPTH, dtype=BF),
            shape(DEPTH, ns, dtype=BF),
            shape(DEPTH, nt, dtype=BF),
            shape(rs, HALF),
            shape(rt, HALF),
            shape(n_col, rs, HALF),
        ),
        scratch(nt, ns),
        name="start",
    )
    h = None
    for step in range(ITERS - 1):
        parts = over("col", parts)
        kernel = functools.partial(lse_kernel, all_tgt, 0, 3)
        ins = (parts, xt, yr)
        if h is None:
            base = kernel
            kernel = lambda p, c, r, *refs: base(p, c, r, None, *refs)
        else:
            ins += (h,)
        e, parts = call(
            kernel, ins, (shape(rs, HALF), shape(n_row, rt, HALF)), scratch(ns, nt), name="cols"
        )
        parts = over("row", parts)
        h, parts = call(
            functools.partial(lse_kernel, all_src, 3, 0),
            (parts, yt, xr, e),
            (shape(rt, HALF), shape(n_col, rs, HALF)),
            scratch(nt, ns),
            name="rows",
        )

    def image_scratch(m, n):
        return scratch(m, n)[:2] + (
            pltpu.VMEM((HALF, n), F32),
            pltpu.VMEM((x.shape[0], n // HALF, HALF), F32),
        )

    parts = over("col", parts)
    e = call(functools.partial(potential_kernel, all_tgt), (parts,), shape(rs, HALF), name="src_join")
    parts = call(
        functools.partial(image_kernel, dim_tgt, 0.5 * LN2, 0, 3),
        (e, xt, yr, xr, h),
        shape(n_row, rt * (1 + dim_tgt), HALF),
        image_scratch(ns, nt),
        name="tgt_part",
    )
    parts = over("row", parts)
    h, tgt = call(
        functools.partial(join_kernel, all_src),
        (parts,),
        (shape(rt, HALF), shape(n_row, rt * dim_tgt, HALF)),
        name="tgt_join",
    )
    tgt = over("row", tgt).reshape(x.shape[0], rt, HALF)
    parts = call(
        functools.partial(image_kernel, dim_src, 1.0, 3, 0),
        (h, yt, xr, yr, e),
        shape(n_col, rs * (1 + dim_src), HALF),
        image_scratch(nt, ns),
        name="src_part",
    )
    parts = over("col", parts)
    src = call(
        functools.partial(share_kernel, rs),
        (parts,),
        shape(n_col, rs * dim_src, HALF),
        name="src_share",
    )
    src = over("col", src).reshape(x.shape[0], rs, HALF)
    f, g, si, ti = call(
        end_kernel,
        (e, h, xsq, ysq, src, tgt),
        (shape(rs, HALF), shape(rt, HALF), shape(*x.shape), shape(*y.shape)),
        name="end",
    )
    return f.reshape(ns), g.reshape(nt), si, ti


def solution(mesh):
    in_specs = (P(None, "row"), P(None, "col"))
    out_specs = (P("row"), P("col"), P(None, "row"), P(None, "col"))
    return jax.shard_map(local, mesh=mesh, in_specs=in_specs, out_specs=out_specs, check_vma=False)
```

```python
import functools
import math

import jax
import jax.numpy as jnp
from jax import lax
from jax.experimental import pallas as pl
from jax.experimental.pallas import tpu as pltpu
from jax.sharding import PartitionSpec as P

ITERS = 3
LOG2E = math.log2(math.e)
LN2 = math.log(2.0)
DEPTH = 256
HALF = 128
DIM = 32
TILE = 256
CHUNK = 256
PROBE = 64
LOW, HIGH = 2.0**-90, 2.0**100
BF, F32 = jnp.bfloat16, jnp.float32
VMEM = pl.BlockSpec(memory_space=pltpu.VMEM)


def rounded(v):
    return v.astype(BF).astype(F32)


def split(v):
    a = rounded(v)
    b = rounded(v - a)
    return a, b, rounded(v - a - b)


def as_row(v):
    return jnp.concatenate([v[r : r + 1, :] for r in range(v.shape[0])], axis=1)


def as_dense(v):
    return jnp.concatenate(
        [v[:, HALF * r : HALF * (r + 1)] for r in range(v.shape[1] // HALF)], axis=0
    )


def potential_rows(v, first):
    a, b, c = split(v)
    row = lax.broadcasted_iota(jnp.int32, (8, v.shape[1]), 0)
    ones = jnp.where((row < 6) & ((row < first) | (row >= first + 3)), 1.0, 0.0).astype(F32)
    out = jnp.where(row == first, a, ones)
    out = jnp.where(row == first + 1, b, out)
    return jnp.where(row == first + 2, c, out)


def row_block(v, first):
    rows = potential_rows(v, first)
    return jnp.concatenate([rows, jnp.zeros_like(rows)], axis=0).astype(BF)


def operand(v, order1, order2, first):
    pieces = split(v)
    n = v.shape[1]
    zero = jnp.zeros((32, n), F32)
    rows = potential_rows(jnp.zeros((1, n), F32), first)
    return jnp.concatenate(
        [pieces[k] for k in order1]
        + [zero, rows, zero[:8]]
        + [pieces[k] for k in order2]
        + [zero[:16]],
        axis=0,
    )


SRC = dict(order1=(0, 0, 1), order2=(0, 2, 1), first=0)
TGT = dict(order1=(0, 1, 0), order2=(2, 0, 1), first=3)


def column_half(v, first, static_ref):
    rows = potential_rows(v, first)
    n = v.shape[1]
    keep = lax.broadcasted_iota(jnp.int32, (8, n), 0)
    rows = jnp.where((keep >= first) & (keep < first + 3), rows, 0.0)
    wide = jnp.concatenate([rows, jnp.zeros((HALF - 8, n), F32)], axis=0)
    return static_ref[:, HALF:] + jnp.transpose(wide.astype(BF))


def tile_of(row_ref, block, start):
    cols = pl.ds(start, TILE)
    return jnp.concatenate(
        [row_ref[:HALF, cols], block, row_ref[HALF + 16 :, cols]], axis=0
    )


def scores(col_ref, half_ref, start, rhs, count=CHUNK):
    rows = pl.ds(start, count)
    lhs = jnp.concatenate([col_ref[rows, :HALF], half_ref[rows, :]], axis=1)
    return jnp.dot(lhs, rhs, preferred_element_type=F32)


def sums(col_ref, half_ref, row_ref, shift_ref, s_ref, first):
    count, n = col_ref.shape[0], row_ref.shape[1]
    for t in range(n // TILE):
        cols = slice(t * TILE, (t + 1) * TILE)
        rhs = tile_of(row_ref, row_block(shift_ref[:, cols], first), t * TILE)
        acc = jnp.zeros((8, TILE), F32)
        for c in range(count // CHUNK):
            s = scores(col_ref, half_ref, c * CHUNK, rhs)
            acc += jnp.sum(jnp.exp2(s).reshape(CHUNK // 8, 8, TILE), axis=0)
        s_ref[:, cols] = jnp.sum(acc, axis=0, keepdims=True)


def peaks(col_ref, half_ref, row_ref, shift_ref, first):
    count, n = col_ref.shape[0], row_ref.shape[1]

    @pl.loop(0, n // TILE)
    def _(t):
        start = pl.multiple_of(t * TILE, TILE)
        rhs = tile_of(row_ref, row_block(jnp.zeros((1, TILE), F32), first), start)

        def step(c, acc):
            s = scores(col_ref, half_ref, pl.multiple_of(c * CHUNK, CHUNK), rhs)
            return jnp.maximum(acc, jnp.max(s.reshape(CHUNK // 8, 8, TILE), axis=0))

        acc = lax.fori_loop(0, count // CHUNK, step, jnp.full((8, TILE), -jnp.inf, F32))
        shift_ref[:, pl.ds(start, TILE)] = -jnp.max(acc, axis=0, keepdims=True)


def probe(col_ref, half_ref, row_ref, shift_ref, first):
    for t in range(row_ref.shape[1] // TILE):
        cols = slice(t * TILE, (t + 1) * TILE)
        rhs = tile_of(row_ref, row_block(jnp.zeros((1, TILE), F32), first), t * TILE)
        s = scores(col_ref, half_ref, 0, rhs, PROBE)
        shift_ref[:, cols] = -jnp.max(s, axis=0, keepdims=True)


def outside(s):
    return jnp.any(jnp.logical_not((s > LOW) & (s < HIGH)))


def guarded(compute, finish, sum_ref, col_ref, half_ref, row_ref, shift_ref, first):
    compute()
    s = as_dense(sum_ref[...])
    finish(s)

    @pl.when(outside(s))
    def _():
        peaks(col_ref, half_ref, row_ref, shift_ref, first)
        compute()
        finish(as_dense(sum_ref[...]))


def joined(parts):
    peak = jnp.max(parts, axis=0)
    return peak + jnp.log2(jnp.sum(jnp.exp2(parts - peak[None]), axis=0))


def joined_rows(total, parts_ref, new_ref):
    new = math.log2(total) - joined(parts_ref[...])
    step = new.shape[1]
    for k in range(new.shape[0]):
        new_ref[step * k : step * (k + 1), :] = new[k]


def send_logs(out_ref, log):
    n, step = out_ref.shape[0], out_ref.shape[2]
    for k in range(log.shape[0] // step):
        rows = log[step * k : step * (k + 1)]
        out_ref[:, k] = jnp.broadcast_to(rows[None], (n, step, HALF))


def start_kernel(
    xy_ref,
    xt_ref, yt_ref, xr_ref, yr_ref, xsq_ref, ysq_ref, out_ref,
    half_ref, shift_ref, s_ref,
):
    x = xy_ref[:, : xr_ref.shape[1]]
    xr = operand(x * (2.0 * LOG2E), **SRC)
    xr_ref[...] = xr.astype(BF)
    xt_ref[...] = jnp.transpose(xr.astype(BF))
    xsq_ref[...] = as_dense(jnp.sum(x * x, axis=0, keepdims=True))
    y = xy_ref[:, xr_ref.shape[1] :]
    yr = operand(y, **TGT)
    yr_ref[...] = yr.astype(BF)
    yt_ref[...] = jnp.transpose(yr.astype(BF))
    ysq = jnp.sum(y * y, axis=0, keepdims=True)
    ysq_ref[...] = as_dense(ysq)
    half_ref[...] = column_half(ysq * -LOG2E, 3, yt_ref)
    args = (yt_ref, half_ref, xr_ref, shift_ref)
    probe(*args, 0)
    lse(out_ref, *args, s_ref, 0)


def lse(out_ref, col_ref, half_ref, row_ref, shift_ref, s_ref, first):
    args = (col_ref, half_ref, row_ref, shift_ref)
    guarded(
        lambda: sums(*args, s_ref, first),
        lambda s: send_logs(out_ref, jnp.log2(s) - as_dense(shift_ref[...])),
        s_ref,
        *args,
        first,
    )


def lse_kernel(
    total, col_first, row_first,
    parts_ref, col_ref, row_ref, old_ref,
    new_ref, out_ref,
    half_ref, shift_ref, s_ref,
):
    joined_rows(total, parts_ref, new_ref)
    half_ref[...] = column_half(as_row(new_ref[...]), col_first, col_ref)
    args = (col_ref, half_ref, row_ref, shift_ref)
    if old_ref is None:
        probe(*args, row_first)
    else:
        shift_ref[...] = as_row(old_ref[...])
    lse(out_ref, *args, s_ref, row_first)


def maps(col_ref, half_ref, row_ref, values_ref, shift_ref, moved_ref, first):
    count, n = col_ref.shape[0], row_ref.shape[1]
    for t in range(n // TILE):
        cols = slice(t * TILE, (t + 1) * TILE)
        rhs = tile_of(row_ref, row_block(shift_ref[:, cols], first), t * TILE)
        total = jnp.zeros((HALF, TILE), F32)
        for c in range(count // CHUNK):
            w = jnp.exp2(scores(col_ref, half_ref, c * CHUNK, rhs))
            high = w.astype(BF)
            low = (w - high.astype(F32)).astype(BF)
            values = values_ref[HALF:, c * CHUNK : (c + 1) * CHUNK]
            total += jnp.dot(values, high, preferred_element_type=F32)
            total += jnp.dot(values, low, preferred_element_type=F32)
        moved_ref[:, cols] = total


def image(dims, scale, send, out_ref, col_ref, half_ref, row_ref, values_ref, shift_ref, moved_ref, first):
    one = first
    n, cells = out_ref.shape[0], row_ref.shape[1] // HALF
    groups = n * dims // DIM
    args = (col_ref, half_ref, row_ref, shift_ref)

    def finish(s):
        log = jnp.log2(s) - as_dense(shift_ref[...])
        base = send(out_ref, log, groups)
        part = moved_ref[16:48, :] + moved_ref[48:80, :] + moved_ref[80:112, :]
        part = part * (scale / as_row(s))
        for k in range(n):
            top, group = dims * (k // groups), k % groups
            at = base
            for cell in range(group, cells, groups):
                for d in range(top, top + dims, 4):
                    out_ref[k, at] = part[d : d + 4, HALF * cell : HALF * (cell + 1)]
                    at += 1

    guarded(
        lambda: maps(col_ref, half_ref, row_ref, values_ref, shift_ref, moved_ref, first),
        finish,
        moved_ref.at[one : one + 1, :],
        *args,
        first,
    )


def send_all_logs(out_ref, log, groups):
    send_logs(out_ref, log)
    return log.shape[0] // 4


def send_own_logs(out_ref, log, groups):
    n, each = out_ref.shape[0], log.shape[0] // groups
    blocks = -(-each // 4)
    for group in range(groups):
        rows = [log[c : c + 1] for c in range(group, log.shape[0], groups)]
        rows = rows + [jnp.zeros_like(rows[0])] * (4 * blocks - each)
        for b in range(blocks):
            block = jnp.concatenate(rows[4 * b : 4 * b + 4], axis=0)
            for k in range(group, n, groups):
                out_ref[k, b] = block
    return blocks


def tgt_part_kernel(
    total, dims,
    parts_ref, col_ref, row_ref, values_ref, old_ref,
    new_ref, out_ref,
    half_ref, shift_ref, moved_ref,
):
    joined_rows(total, parts_ref, new_ref)
    half_ref[...] = column_half(as_row(new_ref[...]), 0, col_ref)
    shift_ref[...] = as_row(old_ref[...])
    image(
        dims, 0.5 * LN2, send_all_logs, out_ref,
        col_ref, half_ref, row_ref, values_ref, shift_ref, moved_ref, 3,
    )


def src_part_kernel(
    dims,
    new_ref, col_ref, row_ref, values_ref, old_ref,
    out_ref,
    half_ref, shift_ref, moved_ref,
):
    half_ref[...] = column_half(as_row(new_ref[...]), 3, col_ref)
    shift_ref[...] = as_row(old_ref[...])
    image(
        dims, 1.0, send_own_logs, out_ref,
        col_ref, half_ref, row_ref, values_ref, shift_ref, moved_ref, 0,
    )


def share(parts_ref, out_ref, base, dims, logs_of):
    n, blocks = out_ref.shape[:2]
    each = dims // 4
    for c in range(blocks // each):
        logs = logs_of(c)
        weights = jnp.exp2(logs - jnp.max(logs, axis=0)[None])
        weights = weights / jnp.sum(weights, axis=0)[None]
        for u in range(each):
            at = c * each + u
            part = jnp.sum(parts_ref[:, base + at] * weights, axis=0)
            out_ref[:, at] = jnp.broadcast_to(part[None], (n, 4, HALF))


def tgt_join_kernel(total, dims, groups, parts_ref, new_ref, out_ref):
    logs_ref = parts_ref.at[:, : new_ref.shape[0] // 4]
    joined_rows(total, logs_ref, new_ref)
    group = lax.rem(lax.axis_index("row"), groups)

    def logs_of(c):
        cell = groups * c + group
        return logs_ref[:, cell // 4, pl.ds(lax.rem(cell, 4), 1), :]

    share(parts_ref, out_ref, new_ref.shape[0] // 4, dims, logs_of)


def src_share_kernel(dims, parts_ref, out_ref):
    base = parts_ref.shape[1] - out_ref.shape[1]
    share(
        parts_ref, out_ref, base, dims, lambda c: parts_ref[:, c // 4, c % 4 : c % 4 + 1, :]
    )


def end_kernel(
    dims_of, e_ref, h_ref, xsq_ref, ysq_ref, src_ref, tgt_ref, f_ref, g_ref, si_ref, ti_ref
):
    f_ref[...] = LN2 * e_ref[...] + xsq_ref[...]
    g_ref[...] = LN2 * h_ref[...] + ysq_ref[...]
    for parts_ref, out_ref in ((src_ref, si_ref), (tgt_ref, ti_ref)):
        n, blocks = parts_ref.shape[:2]
        cells = out_ref.shape[1] // HALF
        dims = dims_of[0] if out_ref is si_ref else dims_of[1]
        groups = n * dims // DIM
        for k in range(n):
            top, at = dims * (k // groups), 0
            for cell in range(k % groups, cells, groups):
                for d in range(top, top + dims, 4):
                    out_ref[d : d + 4, HALF * cell : HALF * (cell + 1)] = parts_ref[k, at]
                    at += 1


def shape(*dims, dtype=F32):
    return jax.ShapeDtypeStruct(dims, dtype)


def call(kernel, ins, outs, scratch=(), name=None):
    return pl.pallas_call(
        kernel,
        out_shape=outs,
        in_specs=[VMEM] * len(ins),
        out_specs=jax.tree.map(lambda _: VMEM, outs),
        scratch_shapes=list(scratch),
        compiler_params=pltpu.CompilerParams(vmem_limit_bytes=32 * 2**20),
        name=name,
    )(*ins)


def local(x, y):
    ns, nt = x.shape[1], y.shape[1]
    n_row, n_col = lax.axis_size("row"), lax.axis_size("col")
    rs, rt = ns // HALF, nt // HALF
    all_src, all_tgt = ns * n_row, nt * n_col
    dim_src, dim_tgt = DIM // min(n_col, 4), DIM // min(n_row, 8)
    grp_src, grp_tgt = n_col * dim_src // DIM, n_row * dim_tgt // DIM
    blk_src, blk_tgt = ns * DIM // n_col // 512, nt * DIM // n_row // 512
    log_src = -(-rs // grp_src // 4)

    def scratch(m, n, rows=1):
        return (pltpu.VMEM((m, HALF), BF), pltpu.VMEM((1, n), F32), pltpu.VMEM((rows, n), F32))

    def over(axis, v):
        return lax.all_to_all(v, axis, 0, 0)

    xt, yt, xr, yr, xsq, ysq, parts = call(
        start_kernel,
        (jnp.concatenate([x, y], axis=1),),
        (
            shape(ns, DEPTH, dtype=BF),
            shape(nt, DEPTH, dtype=BF),
            shape(DEPTH, ns, dtype=BF),
            shape(DEPTH, nt, dtype=BF),
            shape(rs, HALF),
            shape(rt, HALF),
            shape(n_col, rs // 8, 8, HALF),
        ),
        scratch(nt, ns),
        name="start",
    )
    h = None
    for step in range(ITERS - 1):
        parts = over("col", parts)
        kernel = functools.partial(lse_kernel, all_tgt, 0, 3)
        ins = (parts, xt, yr)
        if h is None:
            base = kernel
            kernel = lambda p, c, r, *refs: base(p, c, r, None, *refs)
        else:
            ins += (h,)
        e, parts = call(
            kernel,
            ins,
            (shape(rs, HALF), shape(n_row, rt // 4, 4, HALF)),
            scratch(ns, nt),
            name="cols",
        )
        parts = over("row", parts)
        h, parts = call(
            functools.partial(lse_kernel, all_src, 3, 0),
            (parts, yt, xr, e),
            (shape(rt, HALF), shape(n_col, rs // 8, 8, HALF)),
            scratch(nt, ns),
            name="rows",
        )
    parts = over("col", parts)
    e, parts = call(
        functools.partial(tgt_part_kernel, all_tgt, dim_tgt),
        (parts, xt, yr, xr, h),
        (shape(rs, HALF), shape(n_row, rt // 4 + blk_tgt, 4, HALF)),
        scratch(ns, nt, HALF),
        name="tgt_part",
    )
    parts = over("row", parts)
    h, tgt = call(
        functools.partial(tgt_join_kernel, all_src, dim_tgt, grp_tgt),
        (parts,),
        (shape(rt, HALF), shape(n_row, blk_tgt, 4, HALF)),
        name="tgt_join",
    )
    tgt = over("row", tgt)
    parts = call(
        functools.partial(src_part_kernel, dim_src),
        (h, yt, xr, yr, e),
        shape(n_col, log_src + blk_src, 4, HALF),
        scratch(nt, ns, HALF),
        name="src_part",
    )
    parts, tgt = lax.optimization_barrier((parts, tgt))
    parts = over("col", parts)
    src = call(
        functools.partial(src_share_kernel, dim_src),
        (parts,),
        shape(n_col, blk_src, 4, HALF),
        name="src_share",
    )
    src = over("col", src)
    f, g, si, ti = call(
        functools.partial(end_kernel, (dim_src, dim_tgt)),
        (e, h, xsq, ysq, src, tgt),
        (shape(rs, HALF), shape(rt, HALF), shape(*x.shape), shape(*y.shape)),
        name="end",
    )
    return f.reshape(ns), g.reshape(nt), si, ti


def solution(mesh):
    in_specs = (P(None, "row"), P(None, "col"))
    out_specs = (P("row"), P("col"), P(None, "row"), P(None, "col"))
    return jax.shard_map(local, mesh=mesh, in_specs=in_specs, out_specs=out_specs, check_vma=False)
```

```python
import functools
import math

import jax
import jax.numpy as jnp
from jax import lax
from jax.experimental import pallas as pl
from jax.experimental.pallas import tpu as pltpu
from jax.sharding import PartitionSpec as P

ITERS = 3
LOG2E = math.log2(math.e)
LN2 = math.log(2.0)
DEPTH = 256
HALF = 128
DIM = 32
TILE = 256
CHUNK = 256
UNROLL = 8
PROBE = 64
LOW, HIGH = 2.0**-90, 2.0**100
BF, F32 = jnp.bfloat16, jnp.float32
VMEM = pl.BlockSpec(memory_space=pltpu.VMEM)
HBM = pl.BlockSpec(memory_space=pltpu.HBM)


def rounded(v):
    return v.astype(BF).astype(F32)


def split(v):
    a = rounded(v)
    b = rounded(v - a)
    return a, b, rounded(v - a - b)


def as_row(v):
    return jnp.concatenate([v[r : r + 1, :] for r in range(v.shape[0])], axis=1)


def as_dense(v):
    return jnp.concatenate(
        [v[:, HALF * r : HALF * (r + 1)] for r in range(v.shape[1] // HALF)], axis=0
    )


def potential_rows(v, first):
    a, b, c = split(v)
    row = lax.broadcasted_iota(jnp.int32, (8, v.shape[1]), 0)
    ones = jnp.where((row < 6) & ((row < first) | (row >= first + 3)), 1.0, 0.0).astype(F32)
    out = jnp.where(row == first, a, ones)
    out = jnp.where(row == first + 1, b, out)
    return jnp.where(row == first + 2, c, out)


def row_block(v, first):
    rows = potential_rows(v, first)
    return jnp.concatenate([rows, jnp.zeros_like(rows)], axis=0).astype(BF)


def operand(v, order1, order2, first):
    pieces = split(v)
    n = v.shape[1]
    zero = jnp.zeros((32, n), F32)
    rows = potential_rows(jnp.zeros((1, n), F32), first)
    return jnp.concatenate(
        [pieces[k] for k in order1]
        + [zero, rows, zero[:8]]
        + [pieces[k] for k in order2]
        + [zero[:16]],
        axis=0,
    )


SRC = dict(order1=(0, 0, 1), order2=(0, 2, 1), first=0)
TGT = dict(order1=(0, 1, 0), order2=(2, 0, 1), first=3)


def column_part(v, first):
    rows = potential_rows(v, first)
    n = v.shape[1]
    keep = lax.broadcasted_iota(jnp.int32, (8, n), 0)
    rows = jnp.where((keep >= first) & (keep < first + 3), rows, 0.0)
    wide = jnp.concatenate([rows, jnp.zeros((HALF - 8, n), F32)], axis=0)
    return jnp.transpose(wide.astype(BF))


def column_half(v, first, static_ref):
    return static_ref[:, HALF:] + column_part(v, first)


def tile_of(row_ref, block, start):
    cols = pl.ds(start, TILE)
    return jnp.concatenate(
        [row_ref[:HALF, cols], block, row_ref[HALF + 16 :, cols]], axis=0
    )


def scores(col_ref, half_ref, start, rhs, count=CHUNK):
    rows = pl.ds(start, count)
    lhs = jnp.concatenate([col_ref[rows, :HALF], half_ref[rows, :]], axis=1)
    return jnp.dot(lhs, rhs, preferred_element_type=F32)


def sums(col_ref, half_ref, row_ref, shift_ref, s_ref, first):
    count, n = col_ref.shape[0], row_ref.shape[1]
    for t in range(n // TILE):
        cols = slice(t * TILE, (t + 1) * TILE)
        rhs = tile_of(row_ref, row_block(shift_ref[:, cols], first), t * TILE)
        acc = jnp.zeros((8, TILE), F32)
        for c in range(count // CHUNK):
            s = scores(col_ref, half_ref, c * CHUNK, rhs)
            acc += jnp.sum(jnp.exp2(s).reshape(CHUNK // 8, 8, TILE), axis=0)
        s_ref[:, cols] = jnp.sum(acc, axis=0, keepdims=True)


def fold(col_ref, half_ref, row_ref, shift_ref, out_ref, first, shifted, start, step, end):
    @pl.loop(0, row_ref.shape[1] // TILE)
    def _(t):
        at = pl.multiple_of(t * TILE, TILE)
        cols = pl.ds(at, TILE)
        shift = shift_ref[:, cols] if shifted else jnp.zeros((1, TILE), F32)
        rhs = tile_of(row_ref, row_block(shift, first), at)

        def chunk(c, acc):
            c = pl.multiple_of(c * CHUNK, CHUNK)
            return step(c, acc, scores(col_ref, half_ref, c, rhs))

        out_ref[:, cols] = end(lax.fori_loop(0, col_ref.shape[0] // CHUNK, chunk, start))


def peaks(col_ref, half_ref, row_ref, shift_ref, first):
    fold(
        col_ref, half_ref, row_ref, shift_ref, shift_ref, first, False,
        jnp.full((8, TILE), -jnp.inf, F32),
        lambda c, acc, s: jnp.maximum(acc, jnp.max(s.reshape(CHUNK // 8, 8, TILE), axis=0)),
        lambda acc: -jnp.max(acc, axis=0, keepdims=True),
    )


def slow_sums(col_ref, half_ref, row_ref, shift_ref, s_ref, first):
    fold(
        col_ref, half_ref, row_ref, shift_ref, s_ref, first, True,
        jnp.zeros((8, TILE), F32),
        lambda c, acc, s: acc + jnp.sum(jnp.exp2(s).reshape(CHUNK // 8, 8, TILE), axis=0),
        lambda acc: jnp.sum(acc, axis=0, keepdims=True),
    )


def probe(col_ref, half_ref, row_ref, shift_ref, first):
    for t in range(row_ref.shape[1] // TILE):
        cols = slice(t * TILE, (t + 1) * TILE)
        rhs = tile_of(row_ref, row_block(jnp.zeros((1, TILE), F32), first), t * TILE)
        s = scores(col_ref, half_ref, 0, rhs, PROBE)
        shift_ref[:, cols] = -jnp.max(s, axis=0, keepdims=True)


def outside(s):
    return jnp.any(jnp.logical_not((s > LOW) & (s < HIGH)))


def guarded(compute, redo, finish, sum_ref, col_ref, half_ref, row_ref, shift_ref, first):
    compute()
    s = as_dense(sum_ref[...])
    finish(s)

    @pl.when(outside(s))
    def _():
        peaks(col_ref, half_ref, row_ref, shift_ref, first)
        redo()
        finish(as_dense(sum_ref[...]))


def joined(parts):
    peak = jnp.max(parts, axis=0)
    return peak + jnp.log2(jnp.sum(jnp.exp2(parts - peak[None]), axis=0))


def joined_rows(total, parts_ref, new_ref):
    new = math.log2(total) - joined(parts_ref[...])
    step = new.shape[1]
    for k in range(new.shape[0]):
        new_ref[step * k : step * (k + 1), :] = new[k]


def send_logs(out_ref, log):
    n, step = out_ref.shape[0], out_ref.shape[2]
    for k in range(log.shape[0] // step):
        rows = log[step * k : step * (k + 1)]
        out_ref[:, k] = jnp.broadcast_to(rows[None], (n, step, HALF))


def start_kernel(
    xy_ref,
    xt_ref, yt_ref, xr_ref, yr_ref, xsq_ref, ysq_ref, out_ref,
    half_ref, shift_ref, s_ref,
):
    x = xy_ref[:, : xr_ref.shape[1]]
    xr = operand(x * (2.0 * LOG2E), **SRC)
    xr_ref[...] = xr.astype(BF)
    xt_ref[...] = jnp.transpose(xr.astype(BF))
    xsq_ref[...] = as_dense(jnp.sum(x * x, axis=0, keepdims=True))
    y = xy_ref[:, xr_ref.shape[1] :]
    yr = operand(y, **TGT)
    yr_ref[...] = yr.astype(BF)
    yt_ref[...] = jnp.transpose(yr.astype(BF))
    ysq = jnp.sum(y * y, axis=0, keepdims=True)
    ysq_ref[...] = as_dense(ysq)
    half_ref[...] = column_half(ysq * -LOG2E, 3, yt_ref)
    args = (yt_ref, half_ref, xr_ref, shift_ref)
    probe(*args, 0)
    lse(out_ref, *args, s_ref, 0)


def lse(out_ref, col_ref, half_ref, row_ref, shift_ref, s_ref, first):
    args = (col_ref, half_ref, row_ref, shift_ref)
    guarded(
        lambda: sums(*args, s_ref, first),
        lambda: slow_sums(*args, s_ref, first),
        lambda s: send_logs(out_ref, jnp.log2(s) - as_dense(shift_ref[...])),
        s_ref,
        *args,
        first,
    )


def lse_kernel(
    total, col_first, row_first,
    parts_ref, col_ref, row_ref, old_ref,
    new_ref, out_ref,
    half_ref, shift_ref, s_ref,
):
    joined_rows(total, parts_ref, new_ref)
    half_ref[...] = column_half(as_row(new_ref[...]), col_first, col_ref)
    args = (col_ref, half_ref, row_ref, shift_ref)
    if old_ref is None:
        probe(*args, row_first)
    else:
        shift_ref[...] = as_row(old_ref[...])
    lse(out_ref, *args, s_ref, row_first)


def weighted(score, values):
    w = jnp.exp2(score)
    high = w.astype(BF)
    low = (w - high.astype(F32)).astype(BF)
    return jnp.dot(values, high, preferred_element_type=F32) + jnp.dot(
        values, low, preferred_element_type=F32
    )


def maps(col_ref, half_ref, row_ref, shift_ref, values_ref, moved_ref, first):
    count, n = col_ref.shape[0], row_ref.shape[1]
    for t in range(n // TILE):
        cols = slice(t * TILE, (t + 1) * TILE)
        rhs = tile_of(row_ref, row_block(shift_ref[:, cols], first), t * TILE)
        total = jnp.zeros((HALF, TILE), F32)
        for c in range(count // CHUNK):
            values = values_ref[HALF:, c * CHUNK : (c + 1) * CHUNK]
            total += weighted(scores(col_ref, half_ref, c * CHUNK, rhs), values)
        moved_ref[:, cols] = total


def slow_maps(col_ref, half_ref, row_ref, shift_ref, values_ref, moved_ref, first):
    fold(
        col_ref, half_ref, row_ref, shift_ref, moved_ref, first, True,
        jnp.zeros((HALF, TILE), F32),
        lambda c, acc, s: acc + weighted(s, values_ref[HALF:, pl.ds(c, CHUNK)]),
        lambda acc: acc,
    )


def image(dims, scale, send, out_ref, col_ref, half_ref, row_ref, values_ref, shift_ref, moved_ref, first):
    one = first
    n, cells = out_ref.shape[0], row_ref.shape[1] // HALF
    groups = n * dims // DIM
    args = (col_ref, half_ref, row_ref, shift_ref)

    def finish(s):
        log = jnp.log2(s) - as_dense(shift_ref[...])
        base = send(out_ref, log, groups)
        part = moved_ref[16:48, :] + moved_ref[48:80, :] + moved_ref[80:112, :]
        part = part * (scale / as_row(s))
        for k in range(n):
            top, group = dims * (k // groups), k % groups
            at = base
            for cell in range(group, cells, groups):
                for d in range(top, top + dims, 4):
                    out_ref[k, at] = part[d : d + 4, HALF * cell : HALF * (cell + 1)]
                    at += 1

    guarded(
        lambda: maps(*args, values_ref, moved_ref, first),
        lambda: slow_maps(*args, values_ref, moved_ref, first),
        finish,
        moved_ref.at[one : one + 1, :],
        *args,
        first,
    )


def send_all_logs(out_ref, log, groups):
    send_logs(out_ref, log)
    return log.shape[0] // 4


def tgt_part_kernel(
    total, dims,
    parts_ref, col_ref, row_ref, values_ref, old_ref,
    new_ref, out_ref,
    half_ref, shift_ref, moved_ref,
):
    joined_rows(total, parts_ref, new_ref)
    half_ref[...] = column_half(as_row(new_ref[...]), 0, col_ref)
    shift_ref[...] = as_row(old_ref[...])
    image(
        dims, 0.5 * LN2, send_all_logs, out_ref,
        col_ref, half_ref, row_ref, values_ref, shift_ref, moved_ref, 3,
    )


def tgt_join_kernel(total, parts_ref, new_ref, out_ref):
    joined_rows(total, parts_ref.at[:, : new_ref.shape[0] // 4], new_ref)
    send_logs(out_ref, new_ref[...])


def tgt_share_kernel(dims, groups, parts_ref, out_ref):
    n, blocks = out_ref.shape[:2]
    each = dims // 4
    base = parts_ref.shape[1] - blocks
    group = lax.rem(lax.axis_index("row"), groups)
    for c in range(blocks // each):
        cell = groups * c + group
        logs = parts_ref[:, cell // 4, pl.ds(lax.rem(cell, 4), 1), :]
        weights = jnp.exp2(logs - jnp.max(logs, axis=0)[None])
        weights = weights / jnp.sum(weights, axis=0)[None]
        for u in range(each):
            at = c * each + u
            part = jnp.sum(parts_ref[:, base + at] * weights, axis=0)
            out_ref[:, at] = jnp.broadcast_to(part[None], (n, 4, HALF))


def src_scratch(count, n_blocks, width):
    return (
        pltpu.VMEM((DEPTH, count), BF),
        pltpu.VMEM((count // HALF, HALF), F32),
        pltpu.VMEM((HALF, count), F32),
    )


def src_map_kernel(
    h_ref, y_hbm, xr_ref, e_ref,
    out_ref,
    row_ref, shift_ref, moved_ref, y_ref, sems,
):
    n_blocks, _, width = y_ref.shape
    each = math.gcd(n_blocks, UNROLL)
    copies = [
        pltpu.make_async_copy(
            y_hbm.at[pl.ds(k, each)], y_ref.at[pl.ds(k, each)], sems.at[k // each]
        )
        for k in range(0, n_blocks, each)
    ]
    for copy in copies:
        copy.start()
    count = row_ref.shape[1]
    pieces = count // HALF
    group = lax.rem(lax.axis_index("col"), out_ref.shape[0])
    cols = pl.ds(pl.multiple_of(group * count, count), count)
    one, two, three = xr_ref[0:32, cols], xr_ref[64:96, cols], xr_ref[176:208, cols]
    zero = jnp.zeros((16, count), BF)
    row_ref[...] = jnp.concatenate(
        [one, one, one, zero, zero, two, two, three, zero, zero], axis=0
    )
    row_ref[96:112, :] = xr_ref[128:144, cols]

    def chunk_of(block, t):
        y = y_ref[block, :, TILE * t : TILE * (t + 1)]
        first = TILE // HALF * t
        h = jnp.concatenate(
            [h_ref[block, c // 4, c % 4 : c % 4 + 1, :] for c in range(first, first + TILE // HALF)],
            axis=1,
        )
        values = jnp.concatenate(
            [v.astype(BF) for v in split(y)] + [row_block(h, 3), jnp.zeros((16, TILE), BF)], axis=0
        )
        again = jnp.concatenate([values[:64], values[:64]], axis=0)
        return values, jnp.concatenate([jnp.transpose(values), jnp.transpose(again)], axis=1)

    def step(block, total):
        rhs = row_ref[...]
        for t in range(width // TILE):
            values, lhs = chunk_of(block, t)
            total += weighted(jnp.dot(lhs, rhs, preferred_element_type=F32), values)
        return total

    def maps(arrived):
        shift = as_row(shift_ref[...])
        row_ref[96:112, :] = row_block(shift, 0)
        moved_ref[...] = jnp.zeros((HALF, count), F32)

        @pl.loop(0, n_blocks, step=each)
        def _(block):
            if not arrived:
                pltpu.make_async_copy(
                    y_hbm.at[pl.ds(block, each)], y_ref.at[pl.ds(block, each)], sems.at[block // each]
                ).wait()
            total = moved_ref[...]
            for k in range(each):
                total = step(block + k, total)
            moved_ref[...] = total

        s = moved_ref[96:97, :]
        part = moved_ref[0:32, :] + moved_ref[32:64, :] + moved_ref[64:96, :]
        part = part / s
        for k in range(pieces):
            for d in range(4):
                block = part[8 * d : 8 * d + 8, HALF * k : HALF * (k + 1)]
                out_ref[:, 4 * k + d] = jnp.broadcast_to(block[None], (out_ref.shape[0], 8, HALF))
        return as_dense(s)

    def peaks(block, top):
        for t in range(width // TILE):
            s = jnp.dot(chunk_of(block, t)[1], row_ref[...], preferred_element_type=F32)
            top = jnp.maximum(top, jnp.max(s.reshape(TILE // 8, 8, count), axis=0))
        return top

    shift_ref[...] = e_ref[pl.ds(group * pieces, pieces), :]
    s = maps(False)

    @pl.when(outside(s))
    def _():
        row_ref[96:112, :] = xr_ref[128:144, cols]
        top = lax.fori_loop(0, n_blocks, peaks, jnp.full((8, count), -jnp.inf, F32))
        shift_ref[...] = as_dense(-jnp.max(top, axis=0, keepdims=True))
        maps(True)


def end_kernel(
    dims, e_ref, h_ref, xsq_ref, ysq_ref, src_ref, tgt_ref, f_ref, g_ref, si_ref, ti_ref
):
    f_ref[...] = LN2 * e_ref[...] + xsq_ref[...]
    g_ref[...] = LN2 * h_ref[...] + ysq_ref[...]
    n, blocks = src_ref.shape[:2]
    for p in range(n):
        for at in range(blocks):
            d, cell = 8 * (at % 4), HALF * (p * blocks // 4 + at // 4)
            si_ref[d : d + 8, cell : cell + HALF] = src_ref[p, at]
    n, cells = tgt_ref.shape[0], ti_ref.shape[1] // HALF
    groups = n * dims // DIM
    for p in range(n):
        top, at = dims * (p // groups), 0
        for cell in range(p % groups, cells, groups):
            for d in range(top, top + dims, 4):
                ti_ref[d : d + 4, HALF * cell : HALF * (cell + 1)] = tgt_ref[p, at]
                at += 1


def shape(*dims, dtype=F32):
    return jax.ShapeDtypeStruct(dims, dtype)


def call(kernel, ins, outs, scratch=(), name=None, hbm=()):
    return pl.pallas_call(
        kernel,
        out_shape=outs,
        in_specs=[HBM if k in hbm else VMEM for k in range(len(ins))],
        out_specs=jax.tree.map(lambda _: VMEM, outs),
        scratch_shapes=list(scratch),
        compiler_params=pltpu.CompilerParams(vmem_limit_bytes=32 * 2**20),
        name=name,
    )(*ins)


def local(x, y):
    ns, nt = x.shape[1], y.shape[1]
    n_row, n_col = lax.axis_size("row"), lax.axis_size("col")
    rs, rt = ns // HALF, nt // HALF
    all_src, all_tgt = ns * n_row, nt * n_col
    dims = DIM // min(n_row, 8)
    groups = n_row * dims // DIM
    blocks = nt * DIM // n_row // 512
    near = min(n_col, 4)
    quarter = ns // near

    def scratch(m, n, rows=1):
        return (pltpu.VMEM((m, HALF), BF), pltpu.VMEM((1, n), F32), pltpu.VMEM((rows, n), F32))

    def over(axis, v, groups=None):
        return lax.all_to_all(v, axis, 0, 0, axis_index_groups=groups)

    every_y = lax.all_gather(y, "col")

    xt, yt, xr, yr, xsq, ysq, parts = call(
        start_kernel,
        (jnp.concatenate([x, y], axis=1),),
        (
            shape(ns, DEPTH, dtype=BF),
            shape(nt, DEPTH, dtype=BF),
            shape(DEPTH, ns, dtype=BF),
            shape(DEPTH, nt, dtype=BF),
            shape(rs, HALF),
            shape(rt, HALF),
            shape(n_col, rs // 8, 8, HALF),
        ),
        scratch(nt, ns),
        name="start",
    )
    h = None
    for step in range(ITERS - 1):
        parts = over("col", parts)
        kernel = functools.partial(lse_kernel, all_tgt, 0, 3)
        ins = (parts, xt, yr)
        if h is None:
            base = kernel
            kernel = lambda p, c, r, *refs: base(p, c, r, None, *refs)
        else:
            ins += (h,)
        e, parts = call(
            kernel,
            ins,
            (shape(rs, HALF), shape(n_row, rt // 4, 4, HALF)),
            scratch(ns, nt),
            name="cols",
        )
        parts = over("row", parts)
        h, parts = call(
            functools.partial(lse_kernel, all_src, 3, 0),
            (parts, yt, xr, e),
            (shape(rt, HALF), shape(n_col, rs // 8, 8, HALF)),
            scratch(nt, ns),
            name="rows",
        )
    parts = over("col", parts)
    e, parts = call(
        functools.partial(tgt_part_kernel, all_tgt, dims),
        (parts, xt, yr, xr, h),
        (shape(rs, HALF), shape(n_row, rt // 4 + blocks, 4, HALF)),
        scratch(ns, nt, HALF),
        name="tgt_part",
    )
    parts = over("row", parts)
    h, every_h = call(
        functools.partial(tgt_join_kernel, all_src),
        (parts,),
        (shape(rt, HALF), shape(n_col, rt // 4, 4, HALF)),
        name="tgt_join",
    )
    every_h, every_y = lax.optimization_barrier((every_h, every_y))
    every_h = over("col", every_h)
    parts, every_h = lax.optimization_barrier((parts, every_h))
    tgt = call(
        functools.partial(tgt_share_kernel, dims, groups),
        (parts,),
        shape(n_row, blocks, 4, HALF),
        name="tgt_share",
    )
    tgt = over("row", tgt)
    src = call(
        src_map_kernel,
        (every_h, pltpu.with_memory_space_constraint(every_y, pltpu.HBM), xr, e),
        shape(near, 4 * quarter // HALF, 8, HALF),
        src_scratch(quarter, n_col, nt)
        + (pltpu.VMEM((n_col, DIM, nt), F32), pltpu.SemaphoreType.DMA((n_col,))),
        name="src_map",
        hbm=(1,),
    )
    src, tgt = lax.optimization_barrier((src, tgt))
    src = over("col", src, [[near * k + j for j in range(near)] for k in range(n_col // near)])
    f, g, si, ti = call(
        functools.partial(end_kernel, dims),
        (e, h, xsq, ysq, src, tgt),
        (shape(rs, HALF), shape(rt, HALF), shape(*x.shape), shape(*y.shape)),
        name="end",
    )
    return f.reshape(ns), g.reshape(nt), si, ti


def solution(mesh):
    in_specs = (P(None, "row"), P(None, "col"))
    out_specs = (P("row"), P("col"), P(None, "row"), P(None, "col"))
    return jax.shard_map(local, mesh=mesh, in_specs=in_specs, out_specs=out_specs, check_vma=False)
```

```python
import functools
import math

import jax
import jax.numpy as jnp
from jax import lax
from jax.experimental import pallas as pl
from jax.experimental.pallas import tpu as pltpu
from jax.sharding import PartitionSpec as P

ITERS = 3
LOG2E = math.log2(math.e)
LN2 = math.log(2.0)
DEPTH = 256
HALF = 128
DIM = 32
TILE = 256
CHUNK = 256
PROBE = 64
LOW, HIGH = 2.0**-90, 2.0**100
BF, F32 = jnp.bfloat16, jnp.float32
VMEM = pl.BlockSpec(memory_space=pltpu.VMEM)


def rounded(v):
    return v.astype(BF).astype(F32)


def split(v):
    a = rounded(v)
    b = rounded(v - a)
    return a, b, rounded(v - a - b)


def as_row(v):
    return jnp.concatenate([v[r : r + 1, :] for r in range(v.shape[0])], axis=1)


def as_dense(v):
    return jnp.concatenate(
        [v[:, HALF * r : HALF * (r + 1)] for r in range(v.shape[1] // HALF)], axis=0
    )


def potential_rows(v, first):
    a, b, c = split(v)
    row = lax.broadcasted_iota(jnp.int32, (8, v.shape[1]), 0)
    ones = jnp.where((row < 6) & ((row < first) | (row >= first + 3)), 1.0, 0.0).astype(F32)
    out = jnp.where(row == first, a, ones)
    out = jnp.where(row == first + 1, b, out)
    return jnp.where(row == first + 2, c, out)


def row_block(v, first):
    rows = potential_rows(v, first)
    return jnp.concatenate([rows, jnp.zeros_like(rows)], axis=0).astype(BF)


def operand(v, order1, order2, first):
    pieces = split(v)
    n = v.shape[1]
    zero = jnp.zeros((32, n), F32)
    rows = potential_rows(jnp.zeros((1, n), F32), first)
    return jnp.concatenate(
        [pieces[k] for k in order1]
        + [zero, rows, zero[:8]]
        + [pieces[k] for k in order2]
        + [zero[:16]],
        axis=0,
    )


SRC = dict(order1=(0, 0, 1), order2=(0, 2, 1), first=0)
TGT = dict(order1=(0, 1, 0), order2=(2, 0, 1), first=3)


def column_half(v, first, static_ref):
    rows = potential_rows(v, first)
    n = v.shape[1]
    keep = lax.broadcasted_iota(jnp.int32, (8, n), 0)
    rows = jnp.where((keep >= first) & (keep < first + 3), rows, 0.0)
    wide = jnp.concatenate([rows, jnp.zeros((HALF - 8, n), F32)], axis=0)
    return static_ref[:, HALF:] + jnp.transpose(wide.astype(BF))


def tile_of(row_ref, block, start):
    cols = pl.ds(start, TILE)
    return jnp.concatenate(
        [row_ref[:HALF, cols], block, row_ref[HALF + 16 :, cols]], axis=0
    )


def scores(col_ref, half_ref, start, rhs, count=CHUNK):
    rows = pl.ds(start, count)
    lhs = jnp.concatenate([col_ref[rows, :HALF], half_ref[rows, :]], axis=1)
    return jnp.dot(lhs, rhs, preferred_element_type=F32)


def sums(col_ref, half_ref, row_ref, shift_ref, s_ref, first):
    count, n = col_ref.shape[0], row_ref.shape[1]
    for t in range(n // TILE):
        cols = slice(t * TILE, (t + 1) * TILE)
        rhs = tile_of(row_ref, row_block(shift_ref[:, cols], first), t * TILE)
        acc = jnp.zeros((8, TILE), F32)
        for c in range(count // CHUNK):
            s = scores(col_ref, half_ref, c * CHUNK, rhs)
            acc += jnp.sum(jnp.exp2(s).reshape(CHUNK // 8, 8, TILE), axis=0)
        s_ref[:, cols] = jnp.sum(acc, axis=0, keepdims=True)


def fold(col_ref, half_ref, row_ref, shift_ref, out_ref, first, shifted, start, step, end):
    @pl.loop(0, row_ref.shape[1] // TILE)
    def _(t):
        at = pl.multiple_of(t * TILE, TILE)
        cols = pl.ds(at, TILE)
        shift = shift_ref[:, cols] if shifted else jnp.zeros((1, TILE), F32)
        rhs = tile_of(row_ref, row_block(shift, first), at)

        def chunk(c, acc):
            c = pl.multiple_of(c * CHUNK, CHUNK)
            return step(c, acc, scores(col_ref, half_ref, c, rhs))

        out_ref[:, cols] = end(lax.fori_loop(0, col_ref.shape[0] // CHUNK, chunk, start))


def peaks(col_ref, half_ref, row_ref, shift_ref, first):
    fold(
        col_ref, half_ref, row_ref, shift_ref, shift_ref, first, False,
        jnp.full((8, TILE), -jnp.inf, F32),
        lambda c, acc, s: jnp.maximum(acc, jnp.max(s.reshape(CHUNK // 8, 8, TILE), axis=0)),
        lambda acc: -jnp.max(acc, axis=0, keepdims=True),
    )


def slow_sums(col_ref, half_ref, row_ref, shift_ref, s_ref, first):
    fold(
        col_ref, half_ref, row_ref, shift_ref, s_ref, first, True,
        jnp.zeros((8, TILE), F32),
        lambda c, acc, s: acc + jnp.sum(jnp.exp2(s).reshape(CHUNK // 8, 8, TILE), axis=0),
        lambda acc: jnp.sum(acc, axis=0, keepdims=True),
    )


def probe(col_ref, half_ref, row_ref, shift_ref, first):
    for t in range(row_ref.shape[1] // TILE):
        cols = slice(t * TILE, (t + 1) * TILE)
        rhs = tile_of(row_ref, row_block(jnp.zeros((1, TILE), F32), first), t * TILE)
        s = scores(col_ref, half_ref, 0, rhs, PROBE)
        shift_ref[:, cols] = -jnp.max(s, axis=0, keepdims=True)


def outside(s):
    return jnp.any(jnp.logical_not((s > LOW) & (s < HIGH)))


def guarded(compute, redo, finish, sum_ref, col_ref, half_ref, row_ref, shift_ref, first):
    compute()
    s = as_dense(sum_ref[...])
    finish(s)

    @pl.when(outside(s))
    def _():
        peaks(col_ref, half_ref, row_ref, shift_ref, first)
        redo()
        finish(as_dense(sum_ref[...]))


def joined(parts):
    peak = jnp.max(parts, axis=0)
    return peak + jnp.log2(jnp.sum(jnp.exp2(parts - peak[None]), axis=0))


def joined_rows(total, parts_ref, new_ref):
    new = math.log2(total) - joined(parts_ref[...])
    step = new.shape[1]
    for k in range(new.shape[0]):
        new_ref[step * k : step * (k + 1), :] = new[k]


def send_logs(out_ref, log):
    n, step = out_ref.shape[0], out_ref.shape[2]
    for k in range(log.shape[0] // step):
        rows = log[step * k : step * (k + 1)]
        out_ref[:, k] = jnp.broadcast_to(rows[None], (n, step, HALF))


def start_kernel(
    xy_ref,
    xt_ref, yt_ref, xr_ref, yr_ref, xsq_ref, ysq_ref, out_ref,
    half_ref, shift_ref, s_ref,
):
    x = xy_ref[:, : xr_ref.shape[1]]
    xr = operand(x * (2.0 * LOG2E), **SRC)
    xr_ref[...] = xr.astype(BF)
    xt_ref[...] = jnp.transpose(xr.astype(BF))
    xsq_ref[...] = as_dense(jnp.sum(x * x, axis=0, keepdims=True))
    y = xy_ref[:, xr_ref.shape[1] :]
    yr = operand(y, **TGT)
    yr_ref[...] = yr.astype(BF)
    yt_ref[...] = jnp.transpose(yr.astype(BF))
    ysq = jnp.sum(y * y, axis=0, keepdims=True)
    ysq_ref[...] = as_dense(ysq)
    half_ref[...] = column_half(ysq * -LOG2E, 3, yt_ref)
    args = (yt_ref, half_ref, xr_ref, shift_ref)
    probe(*args, 0)
    lse(out_ref, *args, s_ref, 0)


def lse(out_ref, col_ref, half_ref, row_ref, shift_ref, s_ref, first):
    args = (col_ref, half_ref, row_ref, shift_ref)
    guarded(
        lambda: sums(*args, s_ref, first),
        lambda: slow_sums(*args, s_ref, first),
        lambda s: send_logs(out_ref, jnp.log2(s) - as_dense(shift_ref[...])),
        s_ref,
        *args,
        first,
    )


def lse_kernel(
    total, col_first, row_first,
    parts_ref, col_ref, row_ref, old_ref,
    new_ref, out_ref,
    half_ref, shift_ref, s_ref,
):
    joined_rows(total, parts_ref, new_ref)
    half_ref[...] = column_half(as_row(new_ref[...]), col_first, col_ref)
    args = (col_ref, half_ref, row_ref, shift_ref)
    if old_ref is None:
        probe(*args, row_first)
    else:
        shift_ref[...] = as_row(old_ref[...])
    lse(out_ref, *args, s_ref, row_first)


def weighted(score, values):
    w = jnp.exp2(score)
    high = w.astype(BF)
    low = (w - high.astype(F32)).astype(BF)
    return jnp.dot(values, high, preferred_element_type=F32) + jnp.dot(
        values, low, preferred_element_type=F32
    )


def maps(col_ref, half_ref, row_ref, shift_ref, values_ref, moved_ref, first):
    count, n = col_ref.shape[0], row_ref.shape[1]
    for t in range(n // TILE):
        cols = slice(t * TILE, (t + 1) * TILE)
        rhs = tile_of(row_ref, row_block(shift_ref[:, cols], first), t * TILE)
        total = jnp.zeros((HALF, TILE), F32)
        for c in range(count // CHUNK):
            values = values_ref[HALF:, c * CHUNK : (c + 1) * CHUNK]
            total += weighted(scores(col_ref, half_ref, c * CHUNK, rhs), values)
        moved_ref[:, cols] = total


def slow_maps(col_ref, half_ref, row_ref, shift_ref, values_ref, moved_ref, first):
    fold(
        col_ref, half_ref, row_ref, shift_ref, moved_ref, first, True,
        jnp.zeros((HALF, TILE), F32),
        lambda c, acc, s: acc + weighted(s, values_ref[HALF:, pl.ds(c, CHUNK)]),
        lambda acc: acc,
    )


def image(dims, scale, send, out_ref, col_ref, half_ref, row_ref, values_ref, shift_ref, moved_ref, first):
    one = first
    n, cells = out_ref.shape[0], row_ref.shape[1] // HALF
    groups = n * dims // DIM
    args = (col_ref, half_ref, row_ref, shift_ref)

    def finish(s):
        log = jnp.log2(s) - as_dense(shift_ref[...])
        base = send(out_ref, log, groups)
        part = moved_ref[16:48, :] + moved_ref[48:80, :] + moved_ref[80:112, :]
        part = part * (scale / as_row(s))
        for k in range(n):
            top, group = dims * (k // groups), k % groups
            at = base
            for cell in range(group, cells, groups):
                for d in range(top, top + dims, 4):
                    out_ref[k, at] = part[d : d + 4, HALF * cell : HALF * (cell + 1)]
                    at += 1

    guarded(
        lambda: maps(*args, values_ref, moved_ref, first),
        lambda: slow_maps(*args, values_ref, moved_ref, first),
        finish,
        moved_ref.at[one : one + 1, :],
        *args,
        first,
    )


def send_all_logs(out_ref, log, groups):
    send_logs(out_ref, log)
    return log.shape[0] // 4


def send_own_logs(out_ref, log, groups):
    n, each = out_ref.shape[0], log.shape[0] // groups
    blocks = -(-each // 4)
    for group in range(groups):
        rows = [log[c : c + 1] for c in range(group, log.shape[0], groups)]
        rows = rows + [jnp.zeros_like(rows[0])] * (4 * blocks - each)
        for b in range(blocks):
            block = jnp.concatenate(rows[4 * b : 4 * b + 4], axis=0)
            for k in range(group, n, groups):
                out_ref[k, b] = block
    return blocks


def tgt_part_kernel(
    total, dims,
    parts_ref, col_ref, row_ref, values_ref, old_ref,
    new_ref, out_ref,
    half_ref, shift_ref, moved_ref,
):
    joined_rows(total, parts_ref, new_ref)
    half_ref[...] = column_half(as_row(new_ref[...]), 0, col_ref)
    shift_ref[...] = as_row(old_ref[...])
    image(
        dims, 0.5 * LN2, send_all_logs, out_ref,
        col_ref, half_ref, row_ref, values_ref, shift_ref, moved_ref, 3,
    )


def src_part_kernel(
    dims,
    new_ref, col_ref, row_ref, values_ref, old_ref,
    out_ref,
    half_ref, shift_ref, moved_ref,
):
    half_ref[...] = column_half(as_row(new_ref[...]), 3, col_ref)
    shift_ref[...] = as_row(old_ref[...])
    image(
        dims, 1.0, send_own_logs, out_ref,
        col_ref, half_ref, row_ref, values_ref, shift_ref, moved_ref, 0,
    )


def share(parts_ref, out_ref, base, dims, logs_of):
    n, blocks = out_ref.shape[:2]
    each = dims // 4
    for c in range(blocks // each):
        logs = logs_of(c)
        weights = jnp.exp2(logs - jnp.max(logs, axis=0)[None])
        weights = weights / jnp.sum(weights, axis=0)[None]
        for u in range(each):
            at = c * each + u
            part = jnp.sum(parts_ref[:, base + at] * weights, axis=0)
            out_ref[:, at] = jnp.broadcast_to(part[None], (n, 4, HALF))


def tgt_join_kernel(total, dims, groups, parts_ref, new_ref, out_ref):
    logs_ref = parts_ref.at[:, : new_ref.shape[0] // 4]
    joined_rows(total, logs_ref, new_ref)
    group = lax.rem(lax.axis_index("row"), groups)

    def logs_of(c):
        cell = groups * c + group
        return logs_ref[:, cell // 4, pl.ds(lax.rem(cell, 4), 1), :]

    share(parts_ref, out_ref, new_ref.shape[0] // 4, dims, logs_of)


def src_join_kernel(dims, base, parts_ref, out_ref):
    out_ref[:, :base] = jnp.zeros((out_ref.shape[0], base, 4, HALF), F32)
    for c in range((parts_ref.shape[1] - base) * 4 // dims):
        rows = slice(c % 4, c % 4 + 1)
        log = joined(parts_ref[:, c // 4, rows, :])
        out_ref[:, c // 4, rows, :] = jnp.broadcast_to(log[None], (out_ref.shape[0], 1, HALF))
    src_share_kernel(dims, parts_ref, out_ref.at[:, base:])


def src_share_kernel(dims, parts_ref, out_ref):
    base = parts_ref.shape[1] - out_ref.shape[1]
    share(
        parts_ref, out_ref, base, dims, lambda c: parts_ref[:, c // 4, c % 4 : c % 4 + 1, :]
    )


def end_kernel(
    dims_of, e_ref, h_ref, xsq_ref, ysq_ref, src_ref, tgt_ref, f_ref, g_ref, si_ref, ti_ref
):
    f_ref[...] = LN2 * e_ref[...] + xsq_ref[...]
    g_ref[...] = LN2 * h_ref[...] + ysq_ref[...]
    for parts_ref, out_ref in ((src_ref, si_ref), (tgt_ref, ti_ref)):
        n, blocks = parts_ref.shape[:2]
        cells = out_ref.shape[1] // HALF
        dims = dims_of[0] if out_ref is si_ref else dims_of[1]
        groups = n * dims // DIM
        for k in range(n):
            top, at = dims * (k // groups), 0
            for cell in range(k % groups, cells, groups):
                for d in range(top, top + dims, 4):
                    out_ref[d : d + 4, HALF * cell : HALF * (cell + 1)] = parts_ref[k, at]
                    at += 1


def shape(*dims, dtype=F32):
    return jax.ShapeDtypeStruct(dims, dtype)


def call(kernel, ins, outs, scratch=(), name=None):
    return pl.pallas_call(
        kernel,
        out_shape=outs,
        in_specs=[VMEM] * len(ins),
        out_specs=jax.tree.map(lambda _: VMEM, outs),
        scratch_shapes=list(scratch),
        compiler_params=pltpu.CompilerParams(vmem_limit_bytes=32 * 2**20),
        name=name,
    )(*ins)


def local(x, y):
    ns, nt = x.shape[1], y.shape[1]
    n_row, n_col = lax.axis_size("row"), lax.axis_size("col")
    rs, rt = ns // HALF, nt // HALF
    all_src, all_tgt = ns * n_row, nt * n_col
    dim_tgt = DIM // min(n_row, 8)
    grp_tgt = n_row * dim_tgt // DIM
    blk_tgt = nt * DIM // n_row // 512
    near = min(n_col, 4)
    neighbours = [[near * k + j for j in range(near)] for k in range(n_col // near)]
    apart = [[near * k + j for k in range(n_col // near)] for j in range(near)]
    blk_src, log_src = ns * DIM // near // 512, -(-rs // near // 4)

    def scratch(m, n, rows=1):
        return (pltpu.VMEM((m, HALF), BF), pltpu.VMEM((1, n), F32), pltpu.VMEM((rows, n), F32))

    def over(axis, v, groups=None):
        return lax.all_to_all(v, axis, 0, 0, axis_index_groups=groups)

    xt, yt, xr, yr, xsq, ysq, parts = call(
        start_kernel,
        (jnp.concatenate([x, y], axis=1),),
        (
            shape(ns, DEPTH, dtype=BF),
            shape(nt, DEPTH, dtype=BF),
            shape(DEPTH, ns, dtype=BF),
            shape(DEPTH, nt, dtype=BF),
            shape(rs, HALF),
            shape(rt, HALF),
            shape(n_col, rs // 8, 8, HALF),
        ),
        scratch(nt, ns),
        name="start",
    )
    h = None
    for step in range(ITERS - 1):
        parts = over("col", parts)
        kernel = functools.partial(lse_kernel, all_tgt, 0, 3)
        ins = (parts, xt, yr)
        if h is None:
            base = kernel
            kernel = lambda p, c, r, *refs: base(p, c, r, None, *refs)
        else:
            ins += (h,)
        e, parts = call(
            kernel,
            ins,
            (shape(rs, HALF), shape(n_row, rt // 4, 4, HALF)),
            scratch(ns, nt),
            name="cols",
        )
        parts = over("row", parts)
        h, parts = call(
            functools.partial(lse_kernel, all_src, 3, 0),
            (parts, yt, xr, e),
            (shape(rt, HALF), shape(n_col, rs // 8, 8, HALF)),
            scratch(nt, ns),
            name="rows",
        )
    parts = over("col", parts)
    e, parts = call(
        functools.partial(tgt_part_kernel, all_tgt, dim_tgt),
        (parts, xt, yr, xr, h),
        (shape(rs, HALF), shape(n_row, rt // 4 + blk_tgt, 4, HALF)),
        scratch(ns, nt, HALF),
        name="tgt_part",
    )
    parts = over("row", parts)
    h, tgt = call(
        functools.partial(tgt_join_kernel, all_src, dim_tgt, grp_tgt),
        (parts,),
        (shape(rt, HALF), shape(n_row, blk_tgt, 4, HALF)),
        name="tgt_join",
    )
    tgt = over("row", tgt)
    parts = call(
        functools.partial(src_part_kernel, DIM),
        (h, yt, xr, yr, e),
        shape(near, log_src + blk_src, 4, HALF),
        scratch(nt, ns, HALF),
        name="src_part",
    )
    parts, tgt = lax.optimization_barrier((parts, tgt))
    parts = over("col", parts, neighbours)
    parts = call(
        functools.partial(src_join_kernel, DIM, log_src),
        (parts,),
        shape(n_col // near, log_src + blk_src, 4, HALF),
        name="src_join",
    )
    parts = over("col", parts, apart)
    src = call(
        functools.partial(src_share_kernel, DIM),
        (parts,),
        shape(near, blk_src, 4, HALF),
        name="src_share",
    )
    src = over("col", src, neighbours)
    f, g, si, ti = call(
        functools.partial(end_kernel, (DIM, dim_tgt)),
        (e, h, xsq, ysq, src, tgt),
        (shape(rs, HALF), shape(rt, HALF), shape(*x.shape), shape(*y.shape)),
        name="end",
    )
    return f.reshape(ns), g.reshape(nt), si, ti


def solution(mesh):
    in_specs = (P(None, "row"), P(None, "col"))
    out_specs = (P("row"), P("col"), P(None, "row"), P(None, "col"))
    return jax.shard_map(local, mesh=mesh, in_specs=in_specs, out_specs=out_specs, check_vma=False)
```

```python
import functools
import math

import jax
import jax.numpy as jnp
from jax import lax
from jax.experimental import pallas as pl
from jax.experimental.pallas import tpu as pltpu
from jax.sharding import PartitionSpec as P

ITERS = 3
LOG2E = math.log2(math.e)
LN2 = math.log(2.0)
DEPTH = 256
HALF = 128
DIM = 32
TILE = 256
CHUNK = 256
PROBE = 64
LOW, HIGH = 2.0**-90, 2.0**100
BF, F32 = jnp.bfloat16, jnp.float32
VMEM = pl.BlockSpec(memory_space=pltpu.VMEM)


def rounded(v):
    return v.astype(BF).astype(F32)


def split(v):
    a = rounded(v)
    b = rounded(v - a)
    return a, b, rounded(v - a - b)


def as_row(v):
    return jnp.concatenate([v[r : r + 1, :] for r in range(v.shape[0])], axis=1)


def as_dense(v):
    return jnp.concatenate(
        [v[:, HALF * r : HALF * (r + 1)] for r in range(v.shape[1] // HALF)], axis=0
    )


def potential_rows(v, first):
    a, b, c = split(v)
    row = lax.broadcasted_iota(jnp.int32, (8, v.shape[1]), 0)
    ones = jnp.where((row < 6) & ((row < first) | (row >= first + 3)), 1.0, 0.0).astype(F32)
    out = jnp.where(row == first, a, ones)
    out = jnp.where(row == first + 1, b, out)
    return jnp.where(row == first + 2, c, out)


def row_block(v, first):
    rows = potential_rows(v, first)
    return jnp.concatenate([rows, jnp.zeros_like(rows)], axis=0).astype(BF)


def operand(v, order1, order2, first):
    pieces = split(v)
    n = v.shape[1]
    zero = jnp.zeros((32, n), F32)
    rows = potential_rows(jnp.zeros((1, n), F32), first)
    return jnp.concatenate(
        [pieces[k] for k in order1]
        + [zero, rows, zero[:8]]
        + [pieces[k] for k in order2]
        + [zero[:16]],
        axis=0,
    )


SRC = dict(order1=(0, 0, 1), order2=(0, 2, 1), first=0)
TGT = dict(order1=(0, 1, 0), order2=(2, 0, 1), first=3)


def column_half(v, first, static_ref):
    rows = potential_rows(v, first)
    n = v.shape[1]
    keep = lax.broadcasted_iota(jnp.int32, (8, n), 0)
    rows = jnp.where((keep >= first) & (keep < first + 3), rows, 0.0)
    wide = jnp.concatenate([rows, jnp.zeros((HALF - 8, n), F32)], axis=0)
    return static_ref[:, HALF:] + jnp.transpose(wide.astype(BF))


def tile_of(row_ref, block, start):
    cols = pl.ds(start, TILE)
    return jnp.concatenate(
        [row_ref[:HALF, cols], block, row_ref[HALF + 16 :, cols]], axis=0
    )


def scores(col_ref, half_ref, start, rhs, count=CHUNK):
    rows = pl.ds(start, count)
    lhs = jnp.concatenate([col_ref[rows, :HALF], half_ref[rows, :]], axis=1)
    return jnp.dot(lhs, rhs, preferred_element_type=F32)


def sums(col_ref, half_ref, row_ref, shift_ref, s_ref, first):
    count, n = col_ref.shape[0], row_ref.shape[1]
    for t in range(n // TILE):
        cols = slice(t * TILE, (t + 1) * TILE)
        rhs = tile_of(row_ref, row_block(shift_ref[:, cols], first), t * TILE)
        acc = jnp.zeros((8, TILE), F32)
        for c in range(count // CHUNK):
            s = scores(col_ref, half_ref, c * CHUNK, rhs)
            acc += jnp.sum(jnp.exp2(s).reshape(CHUNK // 8, 8, TILE), axis=0)
        s_ref[:, cols] = jnp.sum(acc, axis=0, keepdims=True)


def fold(col_ref, half_ref, row_ref, shift_ref, out_ref, first, shifted, start, step, end):
    @pl.loop(0, row_ref.shape[1] // TILE)
    def _(t):
        at = pl.multiple_of(t * TILE, TILE)
        cols = pl.ds(at, TILE)
        shift = shift_ref[:, cols] if shifted else jnp.zeros((1, TILE), F32)
        rhs = tile_of(row_ref, row_block(shift, first), at)

        def chunk(c, acc):
            c = pl.multiple_of(c * CHUNK, CHUNK)
            return step(c, acc, scores(col_ref, half_ref, c, rhs))

        out_ref[:, cols] = end(lax.fori_loop(0, col_ref.shape[0] // CHUNK, chunk, start))


def peaks(col_ref, half_ref, row_ref, shift_ref, first):
    fold(
        col_ref, half_ref, row_ref, shift_ref, shift_ref, first, False,
        jnp.full((8, TILE), -jnp.inf, F32),
        lambda c, acc, s: jnp.maximum(acc, jnp.max(s.reshape(CHUNK // 8, 8, TILE), axis=0)),
        lambda acc: -jnp.max(acc, axis=0, keepdims=True),
    )


def slow_sums(col_ref, half_ref, row_ref, shift_ref, s_ref, first):
    fold(
        col_ref, half_ref, row_ref, shift_ref, s_ref, first, True,
        jnp.zeros((8, TILE), F32),
        lambda c, acc, s: acc + jnp.sum(jnp.exp2(s).reshape(CHUNK // 8, 8, TILE), axis=0),
        lambda acc: jnp.sum(acc, axis=0, keepdims=True),
    )


def probe(col_ref, half_ref, row_ref, shift_ref, first):
    for t in range(row_ref.shape[1] // TILE):
        cols = slice(t * TILE, (t + 1) * TILE)
        rhs = tile_of(row_ref, row_block(jnp.zeros((1, TILE), F32), first), t * TILE)
        s = scores(col_ref, half_ref, 0, rhs, PROBE)
        shift_ref[:, cols] = -jnp.max(s, axis=0, keepdims=True)


def outside(s):
    return jnp.any(jnp.logical_not((s > LOW) & (s < HIGH)))


def guarded(compute, redo, finish, sum_ref, col_ref, half_ref, row_ref, shift_ref, first):
    compute()
    s = as_dense(sum_ref[...])
    finish(s)

    @pl.when(outside(s))
    def _():
        peaks(col_ref, half_ref, row_ref, shift_ref, first)
        redo()
        finish(as_dense(sum_ref[...]))


def joined(parts):
    peak = jnp.max(parts, axis=0)
    return peak + jnp.log2(jnp.sum(jnp.exp2(parts - peak[None]), axis=0))


def joined_rows(total, parts_ref, new_ref):
    new = math.log2(total) - joined(parts_ref[...])
    step = new.shape[1]
    for k in range(new.shape[0]):
        new_ref[step * k : step * (k + 1), :] = new[k]


def send_logs(out_ref, log):
    n, step = out_ref.shape[0], out_ref.shape[2]
    for k in range(log.shape[0] // step):
        rows = log[step * k : step * (k + 1)]
        out_ref[:, k] = jnp.broadcast_to(rows[None], (n, step, HALF))


def start_kernel(
    xy_ref,
    xt_ref, yt_ref, xr_ref, yr_ref, xsq_ref, ysq_ref, out_ref,
    half_ref, shift_ref, s_ref,
):
    x = xy_ref[:, : xr_ref.shape[1]]
    xr = operand(x * (2.0 * LOG2E), **SRC)
    xr_ref[...] = xr.astype(BF)
    xt_ref[...] = jnp.transpose(xr.astype(BF))
    xsq_ref[...] = as_dense(jnp.sum(x * x, axis=0, keepdims=True))
    y = xy_ref[:, xr_ref.shape[1] :]
    yr = operand(y, **TGT)
    yr_ref[...] = yr.astype(BF)
    yt_ref[...] = jnp.transpose(yr.astype(BF))
    ysq = jnp.sum(y * y, axis=0, keepdims=True)
    ysq_ref[...] = as_dense(ysq)
    half_ref[...] = column_half(ysq * -LOG2E, 3, yt_ref)
    args = (yt_ref, half_ref, xr_ref, shift_ref)
    probe(*args, 0)
    lse(out_ref, *args, s_ref, 0)


def lse(out_ref, col_ref, half_ref, row_ref, shift_ref, s_ref, first):
    args = (col_ref, half_ref, row_ref, shift_ref)
    guarded(
        lambda: sums(*args, s_ref, first),
        lambda: slow_sums(*args, s_ref, first),
        lambda s: send_logs(out_ref, jnp.log2(s) - as_dense(shift_ref[...])),
        s_ref,
        *args,
        first,
    )


def lse_kernel(
    total, col_first, row_first,
    parts_ref, col_ref, row_ref, old_ref,
    new_ref, out_ref,
    half_ref, shift_ref, s_ref,
):
    joined_rows(total, parts_ref, new_ref)
    half_ref[...] = column_half(as_row(new_ref[...]), col_first, col_ref)
    args = (col_ref, half_ref, row_ref, shift_ref)
    if old_ref is None:
        probe(*args, row_first)
    else:
        shift_ref[...] = as_row(old_ref[...])
    lse(out_ref, *args, s_ref, row_first)


def weighted(score, values):
    w = jnp.exp2(score)
    high = w.astype(BF)
    low = (w - high.astype(F32)).astype(BF)
    return jnp.dot(values, high, preferred_element_type=F32) + jnp.dot(
        values, low, preferred_element_type=F32
    )


def maps(col_ref, half_ref, row_ref, shift_ref, values_ref, moved_ref, first):
    count, n = col_ref.shape[0], row_ref.shape[1]
    for t in range(n // TILE):
        cols = slice(t * TILE, (t + 1) * TILE)
        rhs = tile_of(row_ref, row_block(shift_ref[:, cols], first), t * TILE)
        total = jnp.zeros((HALF, TILE), F32)
        for c in range(count // CHUNK):
            values = values_ref[HALF:, c * CHUNK : (c + 1) * CHUNK]
            total += weighted(scores(col_ref, half_ref, c * CHUNK, rhs), values)
        moved_ref[:, cols] = total


def slow_maps(col_ref, half_ref, row_ref, shift_ref, values_ref, moved_ref, first):
    fold(
        col_ref, half_ref, row_ref, shift_ref, moved_ref, first, True,
        jnp.zeros((HALF, TILE), F32),
        lambda c, acc, s: acc + weighted(s, values_ref[HALF:, pl.ds(c, CHUNK)]),
        lambda acc: acc,
    )


def image(dims, scale, send, out_ref, col_ref, half_ref, row_ref, values_ref, shift_ref, moved_ref, first):
    one = first
    n, cells = out_ref.shape[0], row_ref.shape[1] // HALF
    groups = n * dims // DIM
    args = (col_ref, half_ref, row_ref, shift_ref)

    def finish(s):
        log = jnp.log2(s) - as_dense(shift_ref[...])
        base = send(out_ref, log, groups)
        part = moved_ref[16:48, :] + moved_ref[48:80, :] + moved_ref[80:112, :]
        part = part * (scale / as_row(s))
        for k in range(n):
            top, group = dims * (k // groups), k % groups
            at = base
            for cell in range(group, cells, groups):
                for d in range(top, top + dims, 4):
                    out_ref[k, at] = part[d : d + 4, HALF * cell : HALF * (cell + 1)]
                    at += 1

    guarded(
        lambda: maps(*args, values_ref, moved_ref, first),
        lambda: slow_maps(*args, values_ref, moved_ref, first),
        finish,
        moved_ref.at[one : one + 1, :],
        *args,
        first,
    )


def send_all_logs(out_ref, log, groups):
    send_logs(out_ref, log)
    return log.shape[0] // 4


def tgt_part_kernel(
    total, dims,
    parts_ref, col_ref, row_ref, values_ref, old_ref,
    new_ref, out_ref,
    half_ref, shift_ref, moved_ref,
):
    joined_rows(total, parts_ref, new_ref)
    half_ref[...] = column_half(as_row(new_ref[...]), 0, col_ref)
    shift_ref[...] = as_row(old_ref[...])
    image(
        dims, 0.5 * LN2, send_all_logs, out_ref,
        col_ref, half_ref, row_ref, values_ref, shift_ref, moved_ref, 3,
    )


def src_part_kernel(near, new_ref, col_ref, row_ref, values_ref, old_ref, *refs):
    outs, (half_ref, shift_ref, moved_ref, image_ref, log_ref) = refs[:near], refs[near:]
    half_ref[...] = column_half(as_row(new_ref[...]), 3, col_ref)
    shift_ref[...] = as_row(old_ref[...])
    args = (col_ref, half_ref, row_ref, shift_ref)
    mine = lax.rem(lax.axis_index("col"), near)
    each = log_ref.shape[0] // near
    base = -(-each // 4)

    def finish(s):
        log_ref[...] = jnp.log2(s) - as_dense(shift_ref[...])
        part = moved_ref[16:48, :] + moved_ref[48:80, :] + moved_ref[80:112, :]
        image_ref[...] = part / as_row(s)
        for k, out_ref in enumerate(outs):
            out_ref[:base] = jnp.zeros((base, 4, HALF), F32)
            for c in range(each):
                cell = near * c + (mine ^ k)
                lanes = pl.ds(pl.multiple_of(HALF * cell, HALF), HALF)
                out_ref[c // 4, c % 4 : c % 4 + 1, :] = log_ref[pl.ds(cell, 1), :]
                for u in range(DIM // 4):
                    out_ref[base + DIM // 4 * c + u] = image_ref[4 * u : 4 * u + 4, lanes]

    guarded(
        lambda: maps(*args, values_ref, moved_ref, 0),
        lambda: slow_maps(*args, values_ref, moved_ref, 0),
        finish,
        moved_ref.at[0:1, :],
        *args,
        0,
    )


def share(parts_ref, out_ref, base, dims, logs_of):
    n, blocks = out_ref.shape[:2]
    each = dims // 4
    for c in range(blocks // each):
        logs = logs_of(c)
        weights = jnp.exp2(logs - jnp.max(logs, axis=0)[None])
        weights = weights / jnp.sum(weights, axis=0)[None]
        for u in range(each):
            at = c * each + u
            part = jnp.sum(parts_ref[:, base + at] * weights, axis=0)
            out_ref[:, at] = jnp.broadcast_to(part[None], (n, 4, HALF))


def tgt_join_kernel(total, dims, groups, parts_ref, new_ref, out_ref):
    logs_ref = parts_ref.at[:, : new_ref.shape[0] // 4]
    joined_rows(total, logs_ref, new_ref)
    group = lax.rem(lax.axis_index("row"), groups)

    def logs_of(c):
        cell = groups * c + group
        return logs_ref[:, cell // 4, pl.ds(lax.rem(cell, 4), 1), :]

    share(parts_ref, out_ref, new_ref.shape[0] // 4, dims, logs_of)


def src_join_kernel(base, *refs):
    ins, (out_ref, parts_ref) = refs[:-2], refs[-2:]
    for k, ref in enumerate(ins):
        parts_ref[k] = ref[...]
    out_ref[:, :base] = jnp.zeros((out_ref.shape[0], base, 4, HALF), F32)
    for c in range((parts_ref.shape[1] - base) * 4 // DIM):
        rows = slice(c % 4, c % 4 + 1)
        log = joined(parts_ref[:, c // 4, rows, :])
        out_ref[:, c // 4, rows, :] = jnp.broadcast_to(log[None], (out_ref.shape[0], 1, HALF))
    src_share_kernel(DIM, parts_ref, out_ref.at[:, base:])


def src_share_kernel(dims, parts_ref, out_ref):
    base = parts_ref.shape[1] - out_ref.shape[1]
    share(
        parts_ref, out_ref, base, dims, lambda c: parts_ref[:, c // 4, c % 4 : c % 4 + 1, :]
    )


def end_kernel(
    dims_of, e_ref, h_ref, xsq_ref, ysq_ref, src_ref, tgt_ref, f_ref, g_ref, si_ref, ti_ref
):
    f_ref[...] = LN2 * e_ref[...] + xsq_ref[...]
    g_ref[...] = LN2 * h_ref[...] + ysq_ref[...]
    for parts_ref, out_ref in ((src_ref, si_ref), (tgt_ref, ti_ref)):
        n, blocks = parts_ref.shape[:2]
        cells = out_ref.shape[1] // HALF
        dims = dims_of[0] if out_ref is si_ref else dims_of[1]
        groups = n * dims // DIM
        for k in range(n):
            top, at = dims * (k // groups), 0
            for cell in range(k % groups, cells, groups):
                for d in range(top, top + dims, 4):
                    out_ref[d : d + 4, HALF * cell : HALF * (cell + 1)] = parts_ref[k, at]
                    at += 1


def shape(*dims, dtype=F32):
    return jax.ShapeDtypeStruct(dims, dtype)


def call(kernel, ins, outs, scratch=(), name=None):
    return pl.pallas_call(
        kernel,
        out_shape=outs,
        in_specs=[VMEM] * len(ins),
        out_specs=jax.tree.map(lambda _: VMEM, outs),
        scratch_shapes=list(scratch),
        compiler_params=pltpu.CompilerParams(vmem_limit_bytes=32 * 2**20),
        name=name,
    )(*ins)


def local(x, y):
    ns, nt = x.shape[1], y.shape[1]
    n_row, n_col = lax.axis_size("row"), lax.axis_size("col")
    rs, rt = ns // HALF, nt // HALF
    all_src, all_tgt = ns * n_row, nt * n_col
    dim_tgt = DIM // min(n_row, 8)
    grp_tgt = n_row * dim_tgt // DIM
    blk_tgt = nt * DIM // n_row // 512
    near = min(n_col, 4)
    neighbours = [[near * k + j for j in range(near)] for k in range(n_col // near)]
    apart = [[near * k + j for k in range(n_col // near)] for j in range(near)]
    blk_src, log_src = ns * DIM // near // 512, -(-rs // near // 4)

    def scratch(m, n, rows=1):
        return (pltpu.VMEM((m, HALF), BF), pltpu.VMEM((1, n), F32), pltpu.VMEM((rows, n), F32))

    def over(axis, v, groups=None):
        return lax.all_to_all(v, axis, 0, 0, axis_index_groups=groups)

    xt, yt, xr, yr, xsq, ysq, parts = call(
        start_kernel,
        (jnp.concatenate([x, y], axis=1),),
        (
            shape(ns, DEPTH, dtype=BF),
            shape(nt, DEPTH, dtype=BF),
            shape(DEPTH, ns, dtype=BF),
            shape(DEPTH, nt, dtype=BF),
            shape(rs, HALF),
            shape(rt, HALF),
            shape(n_col, rs // 8, 8, HALF),
        ),
        scratch(nt, ns),
        name="start",
    )
    h = None
    for step in range(ITERS - 1):
        parts = over("col", parts)
        kernel = functools.partial(lse_kernel, all_tgt, 0, 3)
        ins = (parts, xt, yr)
        if h is None:
            base = kernel
            kernel = lambda p, c, r, *refs: base(p, c, r, None, *refs)
        else:
            ins += (h,)
        e, parts = call(
            kernel,
            ins,
            (shape(rs, HALF), shape(n_row, rt // 4, 4, HALF)),
            scratch(ns, nt),
            name="cols",
        )
        parts = over("row", parts)
        h, parts = call(
            functools.partial(lse_kernel, all_src, 3, 0),
            (parts, yt, xr, e),
            (shape(rt, HALF), shape(n_col, rs // 8, 8, HALF)),
            scratch(nt, ns),
            name="rows",
        )
    parts = over("col", parts)
    e, parts = call(
        functools.partial(tgt_part_kernel, all_tgt, dim_tgt),
        (parts, xt, yr, xr, h),
        (shape(rs, HALF), shape(n_row, rt // 4 + blk_tgt, 4, HALF)),
        scratch(ns, nt, HALF),
        name="tgt_part",
    )
    parts = over("row", parts)
    h, tgt = call(
        functools.partial(tgt_join_kernel, all_src, dim_tgt, grp_tgt),
        (parts,),
        (shape(rt, HALF), shape(n_row, blk_tgt, 4, HALF)),
        name="tgt_join",
    )
    tgt = over("row", tgt)
    block = (log_src + blk_src, 4, HALF)
    parts = call(
        functools.partial(src_part_kernel, near),
        (h, yt, xr, yr, e),
        tuple(shape(*block) for _ in range(near)),
        scratch(nt, ns, HALF) + (pltpu.VMEM(x.shape, F32), pltpu.VMEM((rs, HALF), F32)),
        name="src_part",
    )
    parts = parts[:1] + tuple(
        lax.ppermute(
            parts[k], "col", [(i, near * (i // near) + ((i % near) ^ k)) for i in range(n_col)]
        )
        for k in range(1, near)
    )
    parts = call(
        functools.partial(src_join_kernel, log_src),
        parts,
        shape(n_col // near, *block),
        (pltpu.VMEM((near, *block), F32),),
        name="src_join",
    )
    parts, tgt = lax.optimization_barrier((parts, tgt))
    parts = over("col", parts, apart)
    src = call(
        functools.partial(src_share_kernel, DIM),
        (parts,),
        shape(near, blk_src, 4, HALF),
        name="src_share",
    )
    src = over("col", src, neighbours)
    f, g, si, ti = call(
        functools.partial(end_kernel, (DIM, dim_tgt)),
        (e, h, xsq, ysq, src, tgt),
        (shape(rs, HALF), shape(rt, HALF), shape(*x.shape), shape(*y.shape)),
        name="end",
    )
    return f.reshape(ns), g.reshape(nt), si, ti


def solution(mesh):
    in_specs = (P(None, "row"), P(None, "col"))
    out_specs = (P("row"), P("col"), P(None, "row"), P(None, "col"))
    return jax.shard_map(local, mesh=mesh, in_specs=in_specs, out_specs=out_specs, check_vma=False)
```

```python
import functools
import math

import jax
import jax.numpy as jnp
from jax import lax
from jax.experimental import pallas as pl
from jax.experimental.pallas import tpu as pltpu
from jax.sharding import PartitionSpec as P

ITERS = 3
LOG2E = math.log2(math.e)
LN2 = math.log(2.0)
DEPTH = 256
HALF = 128
DIM = 32
TILE = 256
CHUNK = 256
PROBE = 64
LOW, HIGH = 2.0**-90, 2.0**100
BF, F32 = jnp.bfloat16, jnp.float32
VMEM = pl.BlockSpec(memory_space=pltpu.VMEM)


def rounded(v):
    return v.astype(BF).astype(F32)


def split(v):
    a = rounded(v)
    b = rounded(v - a)
    return a, b, rounded(v - a - b)


def as_row(v):
    return jnp.concatenate([v[r : r + 1, :] for r in range(v.shape[0])], axis=1)


def as_dense(v):
    return jnp.concatenate(
        [v[:, HALF * r : HALF * (r + 1)] for r in range(v.shape[1] // HALF)], axis=0
    )


def potential_rows(v, first):
    a, b, c = split(v)
    row = lax.broadcasted_iota(jnp.int32, (8, v.shape[1]), 0)
    ones = jnp.where((row < 6) & ((row < first) | (row >= first + 3)), 1.0, 0.0).astype(F32)
    out = jnp.where(row == first, a, ones)
    out = jnp.where(row == first + 1, b, out)
    return jnp.where(row == first + 2, c, out)


def row_block(v, first):
    rows = potential_rows(v, first)
    return jnp.concatenate([rows, jnp.zeros_like(rows)], axis=0).astype(BF)


def operand(v, order1, order2, first):
    pieces = split(v)
    n = v.shape[1]
    zero = jnp.zeros((32, n), F32)
    rows = potential_rows(jnp.zeros((1, n), F32), first)
    return jnp.concatenate(
        [pieces[k] for k in order1]
        + [zero, rows, zero[:8]]
        + [pieces[k] for k in order2]
        + [zero[:16]],
        axis=0,
    )


SRC = dict(order1=(0, 0, 1), order2=(0, 2, 1), first=0)
TGT = dict(order1=(0, 1, 0), order2=(2, 0, 1), first=3)


def column_half(v, first, static_ref):
    rows = potential_rows(v, first)
    n = v.shape[1]
    keep = lax.broadcasted_iota(jnp.int32, (8, n), 0)
    rows = jnp.where((keep >= first) & (keep < first + 3), rows, 0.0)
    wide = jnp.concatenate([rows, jnp.zeros((HALF - 8, n), F32)], axis=0)
    return static_ref[:, HALF:] + jnp.transpose(wide.astype(BF))


def tile_of(row_ref, block, start):
    cols = pl.ds(start, TILE)
    return jnp.concatenate(
        [row_ref[:HALF, cols], block, row_ref[HALF + 16 :, cols]], axis=0
    )


def scores(col_ref, half_ref, start, rhs, count=CHUNK):
    rows = pl.ds(start, count)
    lhs = jnp.concatenate([col_ref[rows, :HALF], half_ref[rows, :]], axis=1)
    return jnp.dot(lhs, rhs, preferred_element_type=F32)


def sums(col_ref, half_ref, row_ref, shift_ref, s_ref, first):
    count, n = col_ref.shape[0], row_ref.shape[1]
    for t in range(n // TILE):
        cols = slice(t * TILE, (t + 1) * TILE)
        rhs = tile_of(row_ref, row_block(shift_ref[:, cols], first), t * TILE)
        acc = jnp.zeros((8, TILE), F32)
        for c in range(count // CHUNK):
            s = scores(col_ref, half_ref, c * CHUNK, rhs)
            acc += jnp.sum(jnp.exp2(s).reshape(CHUNK // 8, 8, TILE), axis=0)
        s_ref[:, cols] = jnp.sum(acc, axis=0, keepdims=True)


def fold(col_ref, half_ref, row_ref, shift_ref, out_ref, first, shifted, start, step, end):
    @pl.loop(0, row_ref.shape[1] // TILE)
    def _(t):
        at = pl.multiple_of(t * TILE, TILE)
        cols = pl.ds(at, TILE)
        shift = shift_ref[:, cols] if shifted else jnp.zeros((1, TILE), F32)
        rhs = tile_of(row_ref, row_block(shift, first), at)

        def chunk(c, acc):
            c = pl.multiple_of(c * CHUNK, CHUNK)
            return step(c, acc, scores(col_ref, half_ref, c, rhs))

        out_ref[:, cols] = end(lax.fori_loop(0, col_ref.shape[0] // CHUNK, chunk, start))


def peaks(col_ref, half_ref, row_ref, shift_ref, first):
    fold(
        col_ref, half_ref, row_ref, shift_ref, shift_ref, first, False,
        jnp.full((8, TILE), -jnp.inf, F32),
        lambda c, acc, s: jnp.maximum(acc, jnp.max(s.reshape(CHUNK // 8, 8, TILE), axis=0)),
        lambda acc: -jnp.max(acc, axis=0, keepdims=True),
    )


def slow_sums(col_ref, half_ref, row_ref, shift_ref, s_ref, first):
    fold(
        col_ref, half_ref, row_ref, shift_ref, s_ref, first, True,
        jnp.zeros((8, TILE), F32),
        lambda c, acc, s: acc + jnp.sum(jnp.exp2(s).reshape(CHUNK // 8, 8, TILE), axis=0),
        lambda acc: jnp.sum(acc, axis=0, keepdims=True),
    )


def probe(col_ref, half_ref, row_ref, shift_ref, first):
    for t in range(row_ref.shape[1] // TILE):
        cols = slice(t * TILE, (t + 1) * TILE)
        rhs = tile_of(row_ref, row_block(jnp.zeros((1, TILE), F32), first), t * TILE)
        s = scores(col_ref, half_ref, 0, rhs, PROBE)
        shift_ref[:, cols] = -jnp.max(s, axis=0, keepdims=True)


def outside(s):
    return jnp.any(jnp.logical_not((s > LOW) & (s < HIGH)))


def guarded(compute, redo, finish, sum_ref, col_ref, half_ref, row_ref, shift_ref, first):
    compute()
    s = as_dense(sum_ref[...])
    finish(s)

    @pl.when(outside(s))
    def _():
        peaks(col_ref, half_ref, row_ref, shift_ref, first)
        redo()
        finish(as_dense(sum_ref[...]))


def joined(parts):
    peak = jnp.max(parts, axis=0)
    return peak + jnp.log2(jnp.sum(jnp.exp2(parts - peak[None]), axis=0))


def joined_rows(total, parts_ref, new_ref):
    new = math.log2(total) - joined(parts_ref[...])
    step = new.shape[1]
    for k in range(new.shape[0]):
        new_ref[step * k : step * (k + 1), :] = new[k]


def send_logs(out_ref, log):
    n, step = out_ref.shape[0], out_ref.shape[2]
    for k in range(log.shape[0] // step):
        rows = log[step * k : step * (k + 1)]
        out_ref[:, k] = jnp.broadcast_to(rows[None], (n, step, HALF))


def start_kernel(
    xy_ref,
    xt_ref, yt_ref, xr_ref, yr_ref, xsq_ref, ysq_ref, out_ref,
    half_ref, shift_ref, s_ref,
):
    x = xy_ref[:, : xr_ref.shape[1]]
    xr = operand(x * (2.0 * LOG2E), **SRC)
    xr_ref[...] = xr.astype(BF)
    xt_ref[...] = jnp.transpose(xr.astype(BF))
    xsq_ref[...] = as_dense(jnp.sum(x * x, axis=0, keepdims=True))
    y = xy_ref[:, xr_ref.shape[1] :]
    yr = operand(y, **TGT)
    yr_ref[...] = yr.astype(BF)
    yt_ref[...] = jnp.transpose(yr.astype(BF))
    ysq = jnp.sum(y * y, axis=0, keepdims=True)
    ysq_ref[...] = as_dense(ysq)
    half_ref[...] = column_half(ysq * -LOG2E, 3, yt_ref)
    args = (yt_ref, half_ref, xr_ref, shift_ref)
    probe(*args, 0)
    lse(out_ref, *args, s_ref, 0)


def lse(out_ref, col_ref, half_ref, row_ref, shift_ref, s_ref, first):
    args = (col_ref, half_ref, row_ref, shift_ref)
    guarded(
        lambda: sums(*args, s_ref, first),
        lambda: slow_sums(*args, s_ref, first),
        lambda s: send_logs(out_ref, jnp.log2(s) - as_dense(shift_ref[...])),
        s_ref,
        *args,
        first,
    )


def lse_kernel(
    total, col_first, row_first,
    parts_ref, col_ref, row_ref, old_ref,
    new_ref, out_ref,
    half_ref, shift_ref, s_ref,
):
    joined_rows(total, parts_ref, new_ref)
    half_ref[...] = column_half(as_row(new_ref[...]), col_first, col_ref)
    args = (col_ref, half_ref, row_ref, shift_ref)
    if old_ref is None:
        probe(*args, row_first)
    else:
        shift_ref[...] = as_row(old_ref[...])
    lse(out_ref, *args, s_ref, row_first)


def weighted(score, values):
    w = jnp.exp2(score)
    high = w.astype(BF)
    low = (w - high.astype(F32)).astype(BF)
    return jnp.dot(values, high, preferred_element_type=F32) + jnp.dot(
        values, low, preferred_element_type=F32
    )


def maps(col_ref, half_ref, row_ref, shift_ref, values_ref, moved_ref, first):
    count, n = col_ref.shape[0], row_ref.shape[1]
    for t in range(n // TILE):
        cols = slice(t * TILE, (t + 1) * TILE)
        rhs = tile_of(row_ref, row_block(shift_ref[:, cols], first), t * TILE)
        total = jnp.zeros((HALF, TILE), F32)
        for c in range(count // CHUNK):
            values = values_ref[HALF:, c * CHUNK : (c + 1) * CHUNK]
            total += weighted(scores(col_ref, half_ref, c * CHUNK, rhs), values)
        moved_ref[:, cols] = total


def slow_maps(col_ref, half_ref, row_ref, shift_ref, values_ref, moved_ref, first):
    fold(
        col_ref, half_ref, row_ref, shift_ref, moved_ref, first, True,
        jnp.zeros((HALF, TILE), F32),
        lambda c, acc, s: acc + weighted(s, values_ref[HALF:, pl.ds(c, CHUNK)]),
        lambda acc: acc,
    )


def image(dims, scale, send, out_ref, col_ref, half_ref, row_ref, values_ref, shift_ref, moved_ref, first):
    one = first
    n, cells = out_ref.shape[0], row_ref.shape[1] // HALF
    groups = n * dims // DIM
    args = (col_ref, half_ref, row_ref, shift_ref)

    def finish(s):
        log = jnp.log2(s) - as_dense(shift_ref[...])
        base = send(out_ref, log, groups)
        part = moved_ref[16:48, :] + moved_ref[48:80, :] + moved_ref[80:112, :]
        part = part * (scale / as_row(s))
        for k in range(n):
            top, group = dims * (k // groups), k % groups
            at = base
            for cell in range(group, cells, groups):
                for d in range(top, top + dims, 4):
                    out_ref[k, at] = part[d : d + 4, HALF * cell : HALF * (cell + 1)]
                    at += 1

    guarded(
        lambda: maps(*args, values_ref, moved_ref, first),
        lambda: slow_maps(*args, values_ref, moved_ref, first),
        finish,
        moved_ref.at[one : one + 1, :],
        *args,
        first,
    )


def send_all_logs(out_ref, log, groups):
    send_logs(out_ref, log)
    return log.shape[0] // 4


def tgt_part_kernel(
    total, dims,
    parts_ref, col_ref, row_ref, values_ref, old_ref,
    new_ref, out_ref,
    half_ref, shift_ref, moved_ref,
):
    joined_rows(total, parts_ref, new_ref)
    half_ref[...] = column_half(as_row(new_ref[...]), 0, col_ref)
    shift_ref[...] = as_row(old_ref[...])
    image(
        dims, 0.5 * LN2, send_all_logs, out_ref,
        col_ref, half_ref, row_ref, values_ref, shift_ref, moved_ref, 3,
    )


def src_part_kernel(near, new_ref, col_ref, row_ref, values_ref, old_ref, *refs):
    out_refs, (half_ref, shift_ref, moved_ref, image_ref, log_ref) = refs[:-5], refs[-5:]
    outs = [(k, out_refs[k % 2].at[k // 2]) for k in range(near)]
    half_ref[...] = column_half(as_row(new_ref[...]), 3, col_ref)
    shift_ref[...] = as_row(old_ref[...])
    args = (col_ref, half_ref, row_ref, shift_ref)
    mine = lax.rem(lax.axis_index("col"), near)
    each = log_ref.shape[0] // near
    base = -(-each // 4)

    def finish(s):
        log_ref[...] = jnp.log2(s) - as_dense(shift_ref[...])
        part = moved_ref[16:48, :] + moved_ref[48:80, :] + moved_ref[80:112, :]
        image_ref[...] = part / as_row(s)
        for k, out_ref in outs:
            out_ref[:base] = jnp.zeros((base, 4, HALF), F32)
            for c in range(each):
                cell = near * c + (mine ^ k)
                lanes = pl.ds(pl.multiple_of(HALF * cell, HALF), HALF)
                out_ref[c // 4, c % 4 : c % 4 + 1, :] = log_ref[pl.ds(cell, 1), :]
                for u in range(DIM // 4):
                    out_ref[base + DIM // 4 * c + u] = image_ref[4 * u : 4 * u + 4, lanes]

    guarded(
        lambda: maps(*args, values_ref, moved_ref, 0),
        lambda: slow_maps(*args, values_ref, moved_ref, 0),
        finish,
        moved_ref.at[0:1, :],
        *args,
        0,
    )


def share(parts_ref, out_ref, base, dims, logs_of):
    n, blocks = out_ref.shape[:2]
    each = dims // 4
    for c in range(blocks // each):
        logs = logs_of(c)
        weights = jnp.exp2(logs - jnp.max(logs, axis=0)[None])
        weights = weights / jnp.sum(weights, axis=0)[None]
        for u in range(each):
            at = c * each + u
            part = jnp.sum(parts_ref[:, base + at] * weights, axis=0)
            out_ref[:, at] = jnp.broadcast_to(part[None], (n, 4, HALF))


def tgt_join_kernel(total, dims, groups, parts_ref, new_ref, out_ref):
    logs_ref = parts_ref.at[:, : new_ref.shape[0] // 4]
    joined_rows(total, logs_ref, new_ref)
    group = lax.rem(lax.axis_index("row"), groups)

    def logs_of(c):
        cell = groups * c + group
        return logs_ref[:, cell // 4, pl.ds(lax.rem(cell, 4), 1), :]

    share(parts_ref, out_ref, new_ref.shape[0] // 4, dims, logs_of)


def src_join_kernel(base, own, one_ref, other_ref, out_ref, parts_ref):
    for k in range(out_ref.shape[0] if own is None else 1):
        parts_ref[0] = one_ref[k if own is None else own]
        parts_ref[1] = other_ref[k]
        joined_ref = out_ref.at[k : k + 1] if own is None else out_ref
        n = joined_ref.shape[0]
        joined_ref[:, :base] = jnp.zeros((n, base, 4, HALF), F32)
        for c in range((parts_ref.shape[1] - base) * 4 // DIM):
            rows = slice(c % 4, c % 4 + 1)
            log = joined(parts_ref[:, c // 4, rows, :])
            joined_ref[:, c // 4, rows, :] = jnp.broadcast_to(log[None], (n, 1, HALF))
        src_share_kernel(DIM, parts_ref, joined_ref.at[:, base:])


def src_share_kernel(dims, parts_ref, out_ref):
    base = parts_ref.shape[1] - out_ref.shape[1]
    share(
        parts_ref, out_ref, base, dims, lambda c: parts_ref[:, c // 4, c % 4 : c % 4 + 1, :]
    )


def tgt_end_kernel(dims, e_ref, h_ref, xsq_ref, ysq_ref, tgt_ref, f_ref, g_ref, ti_ref):
    f_ref[...] = LN2 * e_ref[...] + xsq_ref[...]
    g_ref[...] = LN2 * h_ref[...] + ysq_ref[...]
    end_kernel(dims, tgt_ref, ti_ref)


def end_kernel(dims, parts_ref, out_ref):
    n, cells = parts_ref.shape[0], out_ref.shape[1] // HALF
    groups = n * dims // DIM
    for k in range(n):
        top, at = dims * (k // groups), 0
        for cell in range(k % groups, cells, groups):
            for d in range(top, top + dims, 4):
                out_ref[d : d + 4, HALF * cell : HALF * (cell + 1)] = parts_ref[k, at]
                at += 1


def shape(*dims, dtype=F32):
    return jax.ShapeDtypeStruct(dims, dtype)


def call(kernel, ins, outs, scratch=(), name=None):
    return pl.pallas_call(
        kernel,
        out_shape=outs,
        in_specs=[VMEM] * len(ins),
        out_specs=jax.tree.map(lambda _: VMEM, outs),
        scratch_shapes=list(scratch),
        compiler_params=pltpu.CompilerParams(vmem_limit_bytes=32 * 2**20),
        name=name,
    )(*ins)


def local(x, y):
    ns, nt = x.shape[1], y.shape[1]
    n_row, n_col = lax.axis_size("row"), lax.axis_size("col")
    rs, rt = ns // HALF, nt // HALF
    all_src, all_tgt = ns * n_row, nt * n_col
    dim_tgt = DIM // min(n_row, 8)
    grp_tgt = n_row * dim_tgt // DIM
    blk_tgt = nt * DIM // n_row // 512
    near = min(n_col, 4)
    neighbours = [[near * k + j for j in range(near)] for k in range(n_col // near)]
    apart = [[near * k + j for k in range(n_col // near)] for j in range(near)]
    blk_src, log_src = ns * DIM // near // 512, -(-rs // near // 4)

    def scratch(m, n, rows=1):
        return (pltpu.VMEM((m, HALF), BF), pltpu.VMEM((1, n), F32), pltpu.VMEM((rows, n), F32))

    def over(axis, v, groups=None):
        return lax.all_to_all(v, axis, 0, 0, axis_index_groups=groups)

    xt, yt, xr, yr, xsq, ysq, parts = call(
        start_kernel,
        (jnp.concatenate([x, y], axis=1),),
        (
            shape(ns, DEPTH, dtype=BF),
            shape(nt, DEPTH, dtype=BF),
            shape(DEPTH, ns, dtype=BF),
            shape(DEPTH, nt, dtype=BF),
            shape(rs, HALF),
            shape(rt, HALF),
            shape(n_col, rs // 8, 8, HALF),
        ),
        scratch(nt, ns),
        name="start",
    )
    h = None
    for step in range(ITERS - 1):
        parts = over("col", parts)
        kernel = functools.partial(lse_kernel, all_tgt, 0, 3)
        ins = (parts, xt, yr)
        if h is None:
            base = kernel
            kernel = lambda p, c, r, *refs: base(p, c, r, None, *refs)
        else:
            ins += (h,)
        e, parts = call(
            kernel,
            ins,
            (shape(rs, HALF), shape(n_row, rt // 4, 4, HALF)),
            scratch(ns, nt),
            name="cols",
        )
        parts = over("row", parts)
        h, parts = call(
            functools.partial(lse_kernel, all_src, 3, 0),
            (parts, yt, xr, e),
            (shape(rt, HALF), shape(n_col, rs // 8, 8, HALF)),
            scratch(nt, ns),
            name="rows",
        )
    parts = over("col", parts)
    e, parts = call(
        functools.partial(tgt_part_kernel, all_tgt, dim_tgt),
        (parts, xt, yr, xr, h),
        (shape(rs, HALF), shape(n_row, rt // 4 + blk_tgt, 4, HALF)),
        scratch(ns, nt, HALF),
        name="tgt_part",
    )
    parts = over("row", parts)
    h, tgt = call(
        functools.partial(tgt_join_kernel, all_src, dim_tgt, grp_tgt),
        (parts,),
        (shape(rt, HALF), shape(n_row, blk_tgt, 4, HALF)),
        name="tgt_join",
    )
    tgt = over("row", tgt)
    block = (log_src + blk_src, 4, HALF)
    pair = (pltpu.VMEM((2, *block), F32),)
    keep, send = call(
        functools.partial(src_part_kernel, near),
        (h, yt, xr, yr, e),
        (shape(2, *block), shape(2, *block)),
        scratch(nt, ns, HALF) + (pltpu.VMEM(x.shape, F32), pltpu.VMEM((rs, HALF), F32)),
        name="src_part",
    )
    parts = call(
        functools.partial(src_join_kernel, log_src, None),
        (keep, lax.ppermute(send, "col", [(i, i ^ 1) for i in range(n_col)])),
        shape(2, *block),
        pair,
        name="src_join",
    )
    came = lax.ppermute(parts[1:], "col", [(i, i ^ 2) for i in range(n_col)])
    f, g, ti = call(
        functools.partial(tgt_end_kernel, dim_tgt),
        (e, h, xsq, ysq, tgt),
        (shape(rs, HALF), shape(rt, HALF), shape(*y.shape)),
        name="tgt_end",
    )
    came, f, g, ti = lax.optimization_barrier((came, f, g, ti))
    parts = call(
        functools.partial(src_join_kernel, log_src, 0),
        (parts, came),
        shape(n_col // near, *block),
        pair,
        name="src_join2",
    )
    parts = over("col", parts, apart)
    src = call(
        functools.partial(src_share_kernel, DIM),
        (parts,),
        shape(near, blk_src, 4, HALF),
        name="src_share",
    )
    src = over("col", src, neighbours)
    si = call(functools.partial(end_kernel, DIM), (src,), shape(*x.shape), name="src_end")
    return f.reshape(ns), g.reshape(nt), si, ti


def solution(mesh):
    in_specs = (P(None, "row"), P(None, "col"))
    out_specs = (P("row"), P("col"), P(None, "row"), P(None, "col"))
    return jax.shard_map(local, mesh=mesh, in_specs=in_specs, out_specs=out_specs, check_vma=False)
```

```python
import functools
import math

import jax
import jax.numpy as jnp
from jax import lax
from jax.experimental import pallas as pl
from jax.experimental.pallas import tpu as pltpu
from jax.sharding import PartitionSpec as P

ITERS = 3
LOG2E = math.log2(math.e)
LN2 = math.log(2.0)
DEPTH = 256
HALF = 128
DIM = 32
NEAR = 4
TILE = 256
CHUNK = 256
PROBE = 64
LOW, HIGH = 2.0**-90, 2.0**100
BF, F32 = jnp.bfloat16, jnp.float32
VMEM = pl.BlockSpec(memory_space=pltpu.VMEM)


def rounded(v):
    return v.astype(BF).astype(F32)


def split(v):
    a = rounded(v)
    b = rounded(v - a)
    return a, b, rounded(v - a - b)


def as_row(v):
    return jnp.concatenate([v[r : r + 1, :] for r in range(v.shape[0])], axis=1)


def as_dense(v):
    return jnp.concatenate(
        [v[:, HALF * r : HALF * (r + 1)] for r in range(v.shape[1] // HALF)], axis=0
    )


def potential_rows(v, first):
    a, b, c = split(v)
    row = lax.broadcasted_iota(jnp.int32, (8, v.shape[1]), 0)
    ones = jnp.where((row < 6) & ((row < first) | (row >= first + 3)), 1.0, 0.0).astype(F32)
    out = jnp.where(row == first, a, ones)
    out = jnp.where(row == first + 1, b, out)
    return jnp.where(row == first + 2, c, out)


def row_block(v, first):
    rows = potential_rows(v, first)
    return jnp.concatenate([rows, jnp.zeros_like(rows)], axis=0).astype(BF)


def operand(v, order1, order2, first):
    pieces = split(v)
    n = v.shape[1]
    zero = jnp.zeros((32, n), F32)
    rows = potential_rows(jnp.zeros((1, n), F32), first)
    return jnp.concatenate(
        [pieces[k] for k in order1]
        + [zero, rows, zero[:8]]
        + [pieces[k] for k in order2]
        + [zero[:16]],
        axis=0,
    )


SRC = dict(order1=(0, 0, 1), order2=(0, 2, 1), first=0)
TGT = dict(order1=(0, 1, 0), order2=(2, 0, 1), first=3)


def column_half(v, first, static_ref):
    rows = potential_rows(v, first)
    n = v.shape[1]
    keep = lax.broadcasted_iota(jnp.int32, (8, n), 0)
    rows = jnp.where((keep >= first) & (keep < first + 3), rows, 0.0)
    wide = jnp.concatenate([rows, jnp.zeros((HALF - 8, n), F32)], axis=0)
    return static_ref[:, HALF:] + jnp.transpose(wide.astype(BF))


def tile_of(row_ref, block, start):
    cols = pl.ds(start, TILE)
    return jnp.concatenate(
        [row_ref[:HALF, cols], block, row_ref[HALF + 16 :, cols]], axis=0
    )


def scores(col_ref, half_ref, start, rhs, count=CHUNK):
    rows = pl.ds(start, count)
    lhs = jnp.concatenate([col_ref[rows, :HALF], half_ref[rows, :]], axis=1)
    return jnp.dot(lhs, rhs, preferred_element_type=F32)


def sums(col_ref, half_ref, row_ref, shift_ref, s_ref, first):
    count, n = col_ref.shape[0], row_ref.shape[1]
    for t in range(n // TILE):
        cols = slice(t * TILE, (t + 1) * TILE)
        rhs = tile_of(row_ref, row_block(shift_ref[:, cols], first), t * TILE)
        acc = jnp.zeros((8, TILE), F32)
        for c in range(count // CHUNK):
            s = scores(col_ref, half_ref, c * CHUNK, rhs)
            acc += jnp.sum(jnp.exp2(s).reshape(CHUNK // 8, 8, TILE), axis=0)
        s_ref[:, cols] = jnp.sum(acc, axis=0, keepdims=True)


def fold(col_ref, half_ref, row_ref, shift_ref, out_ref, first, shifted, start, step, end):
    @pl.loop(0, row_ref.shape[1] // TILE)
    def _(t):
        at = pl.multiple_of(t * TILE, TILE)
        cols = pl.ds(at, TILE)
        shift = shift_ref[:, cols] if shifted else jnp.zeros((1, TILE), F32)
        rhs = tile_of(row_ref, row_block(shift, first), at)

        def chunk(c, acc):
            c = pl.multiple_of(c * CHUNK, CHUNK)
            return step(c, acc, scores(col_ref, half_ref, c, rhs))

        out_ref[:, cols] = end(lax.fori_loop(0, col_ref.shape[0] // CHUNK, chunk, start))


def peaks(col_ref, half_ref, row_ref, shift_ref, first):
    fold(
        col_ref, half_ref, row_ref, shift_ref, shift_ref, first, False,
        jnp.full((8, TILE), -jnp.inf, F32),
        lambda c, acc, s: jnp.maximum(acc, jnp.max(s.reshape(CHUNK // 8, 8, TILE), axis=0)),
        lambda acc: -jnp.max(acc, axis=0, keepdims=True),
    )


def slow_sums(col_ref, half_ref, row_ref, shift_ref, s_ref, first):
    fold(
        col_ref, half_ref, row_ref, shift_ref, s_ref, first, True,
        jnp.zeros((8, TILE), F32),
        lambda c, acc, s: acc + jnp.sum(jnp.exp2(s).reshape(CHUNK // 8, 8, TILE), axis=0),
        lambda acc: jnp.sum(acc, axis=0, keepdims=True),
    )


def probe(col_ref, half_ref, row_ref, shift_ref, first):
    for t in range(row_ref.shape[1] // TILE):
        cols = slice(t * TILE, (t + 1) * TILE)
        rhs = tile_of(row_ref, row_block(jnp.zeros((1, TILE), F32), first), t * TILE)
        s = scores(col_ref, half_ref, 0, rhs, PROBE)
        shift_ref[:, cols] = -jnp.max(s, axis=0, keepdims=True)


def outside(s):
    return jnp.any(jnp.logical_not((s > LOW) & (s < HIGH)))


def guarded(compute, redo, finish, sum_ref, col_ref, half_ref, row_ref, shift_ref, first):
    compute()
    s = as_dense(sum_ref[...])
    finish(s)

    @pl.when(outside(s))
    def _():
        peaks(col_ref, half_ref, row_ref, shift_ref, first)
        redo()
        finish(as_dense(sum_ref[...]))


def joined(parts):
    peak = jnp.max(parts, axis=0)
    return peak + jnp.log2(jnp.sum(jnp.exp2(parts - peak[None]), axis=0))


def joined_rows(total, parts_ref, new_ref):
    new = math.log2(total) - joined(parts_ref[...])
    step = new.shape[1]
    for k in range(new.shape[0]):
        new_ref[step * k : step * (k + 1), :] = new[k]


def send_logs(out_ref, log):
    n, step = out_ref.shape[0], out_ref.shape[2]
    for k in range(log.shape[0] // step):
        rows = log[step * k : step * (k + 1)]
        out_ref[:, k] = jnp.broadcast_to(rows[None], (n, step, HALF))


def start_kernel(
    xy_ref,
    xt_ref, yt_ref, xr_ref, yr_ref, xsq_ref, ysq_ref, out_ref,
    half_ref, shift_ref, s_ref,
):
    x = xy_ref[:, : xr_ref.shape[1]]
    xr = operand(x * (2.0 * LOG2E), **SRC)
    xr_ref[...] = xr.astype(BF)
    xt_ref[...] = jnp.transpose(xr.astype(BF))
    xsq_ref[...] = as_dense(jnp.sum(x * x, axis=0, keepdims=True))
    y = xy_ref[:, xr_ref.shape[1] :]
    yr = operand(y, **TGT)
    yr_ref[...] = yr.astype(BF)
    yt_ref[...] = jnp.transpose(yr.astype(BF))
    ysq = jnp.sum(y * y, axis=0, keepdims=True)
    ysq_ref[...] = as_dense(ysq)
    half_ref[...] = column_half(ysq * -LOG2E, 3, yt_ref)
    args = (yt_ref, half_ref, xr_ref, shift_ref)
    probe(*args, 0)
    lse(out_ref, *args, s_ref, 0)


def lse(out_ref, col_ref, half_ref, row_ref, shift_ref, s_ref, first):
    args = (col_ref, half_ref, row_ref, shift_ref)
    guarded(
        lambda: sums(*args, s_ref, first),
        lambda: slow_sums(*args, s_ref, first),
        lambda s: send_logs(out_ref, jnp.log2(s) - as_dense(shift_ref[...])),
        s_ref,
        *args,
        first,
    )


def lse_kernel(
    total, col_first, row_first,
    parts_ref, col_ref, row_ref, old_ref,
    new_ref, out_ref,
    half_ref, shift_ref, s_ref,
):
    joined_rows(total, parts_ref, new_ref)
    half_ref[...] = column_half(as_row(new_ref[...]), col_first, col_ref)
    args = (col_ref, half_ref, row_ref, shift_ref)
    if old_ref is None:
        probe(*args, row_first)
    else:
        shift_ref[...] = as_row(old_ref[...])
    lse(out_ref, *args, s_ref, row_first)


def weighted(score, values):
    w = jnp.exp2(score)
    high = w.astype(BF)
    low = (w - high.astype(F32)).astype(BF)
    return jnp.dot(values, high, preferred_element_type=F32) + jnp.dot(
        values, low, preferred_element_type=F32
    )


def maps(col_ref, half_ref, row_ref, shift_ref, values_ref, moved_ref, first):
    count, n = col_ref.shape[0], row_ref.shape[1]
    for t in range(n // TILE):
        cols = slice(t * TILE, (t + 1) * TILE)
        rhs = tile_of(row_ref, row_block(shift_ref[:, cols], first), t * TILE)
        total = jnp.zeros((HALF, TILE), F32)
        for c in range(count // CHUNK):
            values = values_ref[HALF:, c * CHUNK : (c + 1) * CHUNK]
            total += weighted(scores(col_ref, half_ref, c * CHUNK, rhs), values)
        moved_ref[:, cols] = total


def slow_maps(col_ref, half_ref, row_ref, shift_ref, values_ref, moved_ref, first):
    fold(
        col_ref, half_ref, row_ref, shift_ref, moved_ref, first, True,
        jnp.zeros((HALF, TILE), F32),
        lambda c, acc, s: acc + weighted(s, values_ref[HALF:, pl.ds(c, CHUNK)]),
        lambda acc: acc,
    )


def image(dims, scale, send, out_ref, col_ref, half_ref, row_ref, values_ref, shift_ref, moved_ref, first):
    one = first
    n, cells = out_ref.shape[0], row_ref.shape[1] // HALF
    groups = n * dims // DIM
    args = (col_ref, half_ref, row_ref, shift_ref)

    def finish(s):
        log = jnp.log2(s) - as_dense(shift_ref[...])
        base = send(out_ref, log, groups)
        part = moved_ref[16:48, :] + moved_ref[48:80, :] + moved_ref[80:112, :]
        part = part * (scale / as_row(s))
        for k in range(n):
            top, group = dims * (k // groups), k % groups
            at = base
            for cell in range(group, cells, groups):
                for d in range(top, top + dims, 4):
                    out_ref[k, at] = part[d : d + 4, HALF * cell : HALF * (cell + 1)]
                    at += 1

    guarded(
        lambda: maps(*args, values_ref, moved_ref, first),
        lambda: slow_maps(*args, values_ref, moved_ref, first),
        finish,
        moved_ref.at[one : one + 1, :],
        *args,
        first,
    )


def send_all_logs(out_ref, log, groups):
    send_logs(out_ref, log)
    return log.shape[0] // 4


def tgt_part_kernel(
    total, dims,
    parts_ref, col_ref, row_ref, values_ref, old_ref,
    new_ref, out_ref,
    half_ref, shift_ref, moved_ref,
):
    joined_rows(total, parts_ref, new_ref)
    half_ref[...] = column_half(as_row(new_ref[...]), 0, col_ref)
    shift_ref[...] = as_row(old_ref[...])
    image(
        dims, 0.5 * LN2, send_all_logs, out_ref,
        col_ref, half_ref, row_ref, values_ref, shift_ref, moved_ref, 3,
    )


def src_part_kernel(
    flip, half_in, e_ref, row_ref, values_ref, col_ref, h_ref,
    out_ref, half_ref,
    rows_ref, shift_ref, moved_ref,
):
    if half_in is None:
        half_ref[...] = column_half(as_row(h_ref[...]), 3, col_ref)
    else:
        half_ref = half_in
    mine = lax.rem(lax.axis_index("col"), NEAR)
    count = rows_ref.shape[1] // 2
    cells = count // HALF
    for k in range(2):
        part = mine ^ (flip ^ 2 * k)
        at = slice(count * k, count * (k + 1))
        rows_ref[:, at] = row_ref[:, pl.ds(pl.multiple_of(count * part, count), count)]
        shift_ref[:, at] = as_row(e_ref[pl.ds(cells * part, cells), :])
    args = (col_ref, half_ref, rows_ref, shift_ref)

    def finish(s):
        log = jnp.log2(s) - as_dense(shift_ref[...])
        part = moved_ref[16:48, :] + moved_ref[48:80, :] + moved_ref[80:112, :]
        part = part / as_row(s)
        for k in range(2):
            out_ref[k, 0] = jnp.concatenate(
                [log[cells * k : cells * (k + 1)], jnp.zeros((4 - cells, HALF), F32)], axis=0
            )
            for c in range(cells):
                cell = cells * k + c
                for u in range(DIM // 4):
                    out_ref[k, 1 + DIM // 4 * c + u] = part[
                        4 * u : 4 * u + 4, HALF * cell : HALF * (cell + 1)
                    ]

    guarded(
        lambda: maps(*args, values_ref, moved_ref, 0),
        lambda: slow_maps(*args, values_ref, moved_ref, 0),
        finish,
        moved_ref.at[0:1, :],
        *args,
        0,
    )


def src_send_kernel(h_ref, col_ref, row_ref, values_ref, e_ref, out_ref, half_ref, *scratch):
    src_part_kernel(1, None, e_ref, row_ref, values_ref, col_ref, h_ref, out_ref, half_ref, *scratch)


def src_keep_kernel(half_ref, col_ref, row_ref, values_ref, e_ref, out_ref, *scratch):
    src_part_kernel(0, half_ref, e_ref, row_ref, values_ref, col_ref, None, out_ref, None, *scratch)


def share(parts_ref, out_ref, base, dims, logs_of):
    n, blocks = out_ref.shape[:2]
    each = dims // 4
    for c in range(blocks // each):
        logs = logs_of(c)
        weights = jnp.exp2(logs - jnp.max(logs, axis=0)[None])
        weights = weights / jnp.sum(weights, axis=0)[None]
        for u in range(each):
            at = c * each + u
            part = jnp.sum(parts_ref[:, base + at] * weights, axis=0)
            out_ref[:, at] = jnp.broadcast_to(part[None], (n, 4, HALF))


def tgt_join_kernel(total, dims, groups, parts_ref, new_ref, out_ref):
    logs_ref = parts_ref.at[:, : new_ref.shape[0] // 4]
    joined_rows(total, logs_ref, new_ref)
    group = lax.rem(lax.axis_index("row"), groups)

    def logs_of(c):
        cell = groups * c + group
        return logs_ref[:, cell // 4, pl.ds(lax.rem(cell, 4), 1), :]

    share(parts_ref, out_ref, new_ref.shape[0] // 4, dims, logs_of)


def src_join_kernel(base, own, one_ref, other_ref, out_ref, parts_ref):
    for k in range(out_ref.shape[0] if own is None else 1):
        parts_ref[0] = one_ref[k if own is None else own]
        parts_ref[1] = other_ref[k]
        joined_ref = out_ref.at[k : k + 1] if own is None else out_ref
        n = joined_ref.shape[0]
        joined_ref[:, :base] = jnp.zeros((n, base, 4, HALF), F32)
        for c in range((parts_ref.shape[1] - base) * 4 // DIM):
            rows = slice(c % 4, c % 4 + 1)
            log = joined(parts_ref[:, c // 4, rows, :])
            joined_ref[:, c // 4, rows, :] = jnp.broadcast_to(log[None], (n, 1, HALF))
        src_share_kernel(DIM, parts_ref, joined_ref.at[:, base:])


def src_share_kernel(dims, parts_ref, out_ref):
    base = parts_ref.shape[1] - out_ref.shape[1]
    share(
        parts_ref, out_ref, base, dims, lambda c: parts_ref[:, c // 4, c % 4 : c % 4 + 1, :]
    )


def tgt_end_kernel(dims, e_ref, h_ref, xsq_ref, ysq_ref, tgt_ref, f_ref, g_ref, ti_ref):
    f_ref[...] = LN2 * e_ref[...] + xsq_ref[...]
    g_ref[...] = LN2 * h_ref[...] + ysq_ref[...]
    end_kernel(dims, tgt_ref, ti_ref)


def end_kernel(dims, parts_ref, out_ref):
    n, cells = parts_ref.shape[0], out_ref.shape[1] // HALF
    groups = n * dims // DIM
    for k in range(n):
        top, at = dims * (k // groups), 0
        if dims == DIM:
            span = range(k * cells // n, (k + 1) * cells // n)
        else:
            span = range(k % groups, cells, groups)
        for cell in span:
            for d in range(top, top + dims, 4):
                out_ref[d : d + 4, HALF * cell : HALF * (cell + 1)] = parts_ref[k, at]
                at += 1


def shape(*dims, dtype=F32):
    return jax.ShapeDtypeStruct(dims, dtype)


def call(kernel, ins, outs, scratch=(), name=None, cost=None):
    return pl.pallas_call(
        kernel,
        out_shape=outs,
        in_specs=[VMEM] * len(ins),
        out_specs=jax.tree.map(lambda _: VMEM, outs),
        scratch_shapes=list(scratch),
        compiler_params=pltpu.CompilerParams(vmem_limit_bytes=32 * 2**20),
        name=name,
        cost_estimate=cost,
    )(*ins)


def local(x, y):
    ns, nt = x.shape[1], y.shape[1]
    n_row, n_col = lax.axis_size("row"), lax.axis_size("col")
    rs, rt = ns // HALF, nt // HALF
    all_src, all_tgt = ns * n_row, nt * n_col
    dim_tgt = DIM // min(n_row, 8)
    grp_tgt = n_row * dim_tgt // DIM
    blk_tgt = nt * DIM // n_row // 512
    near = NEAR
    neighbours = [[near * k + j for j in range(near)] for k in range(n_col // near)]
    apart = [[near * k + j for k in range(n_col // near)] for j in range(near)]
    blk_src, log_src = ns * DIM // near // 512, -(-rs // near // 4)

    def scratch(m, n, rows=1):
        return (pltpu.VMEM((m, HALF), BF), pltpu.VMEM((1, n), F32), pltpu.VMEM((rows, n), F32))

    def over(axis, v, groups=None):
        return lax.all_to_all(v, axis, 0, 0, axis_index_groups=groups)

    xt, yt, xr, yr, xsq, ysq, parts = call(
        start_kernel,
        (jnp.concatenate([x, y], axis=1),),
        (
            shape(ns, DEPTH, dtype=BF),
            shape(nt, DEPTH, dtype=BF),
            shape(DEPTH, ns, dtype=BF),
            shape(DEPTH, nt, dtype=BF),
            shape(rs, HALF),
            shape(rt, HALF),
            shape(n_col, rs // 8, 8, HALF),
        ),
        scratch(nt, ns),
        name="start",
    )
    h = None
    for step in range(ITERS - 1):
        parts = over("col", parts)
        kernel = functools.partial(lse_kernel, all_tgt, 0, 3)
        ins = (parts, xt, yr)
        if h is None:
            base = kernel
            kernel = lambda p, c, r, *refs: base(p, c, r, None, *refs)
        else:
            ins += (h,)
        e, parts = call(
            kernel,
            ins,
            (shape(rs, HALF), shape(n_row, rt // 4, 4, HALF)),
            scratch(ns, nt),
            name="cols",
        )
        parts = over("row", parts)
        h, parts = call(
            functools.partial(lse_kernel, all_src, 3, 0),
            (parts, yt, xr, e),
            (shape(rt, HALF), shape(n_col, rs // 8, 8, HALF)),
            scratch(nt, ns),
            name="rows",
        )
    parts = over("col", parts)
    e, parts = call(
        functools.partial(tgt_part_kernel, all_tgt, dim_tgt),
        (parts, xt, yr, xr, h),
        (shape(rs, HALF), shape(n_row, rt // 4 + blk_tgt, 4, HALF)),
        scratch(ns, nt, HALF),
        name="tgt_part",
    )
    parts = over("row", parts)
    h, tgt = call(
        functools.partial(tgt_join_kernel, all_src, dim_tgt, grp_tgt),
        (parts,),
        (shape(rt, HALF), shape(n_row, blk_tgt, 4, HALF)),
        name="tgt_join",
    )
    tgt = over("row", tgt)
    block = (log_src + blk_src, 4, HALF)
    pair = (pltpu.VMEM((2, *block), F32),)
    half = shape(2, *block)
    src_scratch = (
        pltpu.VMEM((DEPTH, ns // 2), BF),
        pltpu.VMEM((1, ns // 2), F32),
        pltpu.VMEM((HALF, ns // 2), F32),
    )
    work = pl.CostEstimate(flops=2 * 2**29, bytes_accessed=2**21, transcendentals=2**20)
    send, half_h = call(
        src_send_kernel,
        (h, yt, xr, yr, e),
        (half, shape(nt, HALF, dtype=BF)),
        src_scratch,
        name="src_send",
        cost=work,
    )
    send = lax.ppermute(send, "col", [(i, i ^ 1) for i in range(n_col)])
    keep = call(
        src_keep_kernel, (half_h, yt, xr, yr, e), half, src_scratch, name="src_keep", cost=work
    )
    parts = call(
        functools.partial(src_join_kernel, log_src, None),
        (keep, send),
        shape(2, *block),
        pair,
        name="src_join",
    )
    came = lax.ppermute(parts[1:], "col", [(i, i ^ 2) for i in range(n_col)])
    f, g, ti = call(
        functools.partial(tgt_end_kernel, dim_tgt),
        (e, h, xsq, ysq, tgt),
        (shape(rs, HALF), shape(rt, HALF), shape(*y.shape)),
        name="tgt_end",
    )
    came, f, g, ti = lax.optimization_barrier((came, f, g, ti))
    parts = call(
        functools.partial(src_join_kernel, log_src, 0),
        (parts, came),
        shape(n_col // near, *block),
        pair,
        name="src_join2",
    )
    parts = over("col", parts, apart)
    src = call(
        functools.partial(src_share_kernel, DIM),
        (parts,),
        shape(near, blk_src, 4, HALF),
        name="src_share",
    )
    src = over("col", src, neighbours)
    si = call(functools.partial(end_kernel, DIM), (src,), shape(*x.shape), name="src_end")
    return f.reshape(ns), g.reshape(nt), si, ti


def solution(mesh):
    in_specs = (P(None, "row"), P(None, "col"))
    out_specs = (P("row"), P("col"), P(None, "row"), P(None, "col"))
    return jax.shard_map(local, mesh=mesh, in_specs=in_specs, out_specs=out_specs, check_vma=False)
```

```python
import functools
import math

import jax
import jax.numpy as jnp
from jax import lax
from jax.experimental import pallas as pl
from jax.experimental.pallas import tpu as pltpu
from jax.sharding import PartitionSpec as P

ITERS = 3
LOG2E = math.log2(math.e)
LN2 = math.log(2.0)
DEPTH = 256
HALF = 128
DIM = 32
NEAR = 4
TILE = 256
CHUNK = 256
PROBE = 64
LOW, HIGH = 2.0**-90, 2.0**100
BF, F32 = jnp.bfloat16, jnp.float32
VMEM = pl.BlockSpec(memory_space=pltpu.VMEM)
HBM = pl.BlockSpec(memory_space=pltpu.HBM)


def rounded(v):
    return v.astype(BF).astype(F32)


def split(v):
    a = rounded(v)
    b = rounded(v - a)
    return a, b, rounded(v - a - b)


def as_row(v):
    return jnp.concatenate([v[r : r + 1, :] for r in range(v.shape[0])], axis=1)


def as_dense(v):
    return jnp.concatenate(
        [v[:, HALF * r : HALF * (r + 1)] for r in range(v.shape[1] // HALF)], axis=0
    )


def potential_rows(v, first):
    a, b, c = split(v)
    row = lax.broadcasted_iota(jnp.int32, (8, v.shape[1]), 0)
    ones = jnp.where((row < 6) & ((row < first) | (row >= first + 3)), 1.0, 0.0).astype(F32)
    out = jnp.where(row == first, a, ones)
    out = jnp.where(row == first + 1, b, out)
    return jnp.where(row == first + 2, c, out)


def row_block(v, first):
    rows = potential_rows(v, first)
    return jnp.concatenate([rows, jnp.zeros_like(rows)], axis=0).astype(BF)


def operand(v, order1, order2, first):
    pieces = split(v)
    n = v.shape[1]
    zero = jnp.zeros((32, n), F32)
    rows = potential_rows(jnp.zeros((1, n), F32), first)
    return jnp.concatenate(
        [pieces[k] for k in order1]
        + [zero, rows, zero[:8]]
        + [pieces[k] for k in order2]
        + [zero[:16]],
        axis=0,
    )


SRC = dict(order1=(0, 0, 1), order2=(0, 2, 1), first=0)
TGT = dict(order1=(0, 1, 0), order2=(2, 0, 1), first=3)


def column_half(v, first, static_ref):
    rows = potential_rows(v, first)
    n = v.shape[1]
    keep = lax.broadcasted_iota(jnp.int32, (8, n), 0)
    rows = jnp.where((keep >= first) & (keep < first + 3), rows, 0.0)
    wide = jnp.concatenate([rows, jnp.zeros((HALF - 8, n), F32)], axis=0)
    return static_ref[:, HALF:] + jnp.transpose(wide.astype(BF))


def tile_of(row_ref, block, start):
    cols = pl.ds(start, TILE)
    return jnp.concatenate(
        [row_ref[:HALF, cols], block, row_ref[HALF + 16 :, cols]], axis=0
    )


def scores(col_ref, half_ref, start, rhs, count=CHUNK):
    rows = pl.ds(start, count)
    lhs = jnp.concatenate([col_ref[rows, :HALF], half_ref[rows, :]], axis=1)
    return jnp.dot(lhs, rhs, preferred_element_type=F32)


def sums(col_ref, half_ref, row_ref, shift_ref, s_ref, first):
    count, n = col_ref.shape[0], row_ref.shape[1]
    for t in range(n // TILE):
        cols = slice(t * TILE, (t + 1) * TILE)
        rhs = tile_of(row_ref, row_block(shift_ref[:, cols], first), t * TILE)
        acc = jnp.zeros((8, TILE), F32)
        for c in range(count // CHUNK):
            s = scores(col_ref, half_ref, c * CHUNK, rhs)
            acc += jnp.sum(jnp.exp2(s).reshape(CHUNK // 8, 8, TILE), axis=0)
        s_ref[:, cols] = jnp.sum(acc, axis=0, keepdims=True)


def fold(col_ref, half_ref, row_ref, shift_ref, out_ref, first, shifted, start, step, end):
    @pl.loop(0, row_ref.shape[1] // TILE)
    def _(t):
        at = pl.multiple_of(t * TILE, TILE)
        cols = pl.ds(at, TILE)
        shift = shift_ref[:, cols] if shifted else jnp.zeros((1, TILE), F32)
        rhs = tile_of(row_ref, row_block(shift, first), at)

        def chunk(c, acc):
            c = pl.multiple_of(c * CHUNK, CHUNK)
            return step(c, acc, scores(col_ref, half_ref, c, rhs))

        out_ref[:, cols] = end(lax.fori_loop(0, col_ref.shape[0] // CHUNK, chunk, start))


def peaks(col_ref, half_ref, row_ref, shift_ref, first):
    fold(
        col_ref, half_ref, row_ref, shift_ref, shift_ref, first, False,
        jnp.full((8, TILE), -jnp.inf, F32),
        lambda c, acc, s: jnp.maximum(acc, jnp.max(s.reshape(CHUNK // 8, 8, TILE), axis=0)),
        lambda acc: -jnp.max(acc, axis=0, keepdims=True),
    )


def slow_sums(col_ref, half_ref, row_ref, shift_ref, s_ref, first):
    fold(
        col_ref, half_ref, row_ref, shift_ref, s_ref, first, True,
        jnp.zeros((8, TILE), F32),
        lambda c, acc, s: acc + jnp.sum(jnp.exp2(s).reshape(CHUNK // 8, 8, TILE), axis=0),
        lambda acc: jnp.sum(acc, axis=0, keepdims=True),
    )


def probe(col_ref, half_ref, row_ref, shift_ref, first):
    for t in range(row_ref.shape[1] // TILE):
        cols = slice(t * TILE, (t + 1) * TILE)
        rhs = tile_of(row_ref, row_block(jnp.zeros((1, TILE), F32), first), t * TILE)
        s = scores(col_ref, half_ref, 0, rhs, PROBE)
        shift_ref[:, cols] = -jnp.max(s, axis=0, keepdims=True)


def outside(s):
    return jnp.any(jnp.logical_not((s > LOW) & (s < HIGH)))


def guarded(compute, redo, finish, sum_ref, col_ref, half_ref, row_ref, shift_ref, first):
    compute()
    s = as_dense(sum_ref[...])
    finish(s)

    @pl.when(outside(s))
    def _():
        peaks(col_ref, half_ref, row_ref, shift_ref, first)
        redo()
        finish(as_dense(sum_ref[...]))


def joined(parts):
    peak = jnp.max(parts, axis=0)
    return peak + jnp.log2(jnp.sum(jnp.exp2(parts - peak[None]), axis=0))


def joined_rows(total, parts_ref, new_ref):
    new = math.log2(total) - joined(parts_ref[...])
    step = new.shape[1]
    for k in range(new.shape[0]):
        new_ref[step * k : step * (k + 1), :] = new[k]


def send_logs(out_ref, log):
    n, step = out_ref.shape[0], out_ref.shape[2]
    for k in range(log.shape[0] // step):
        rows = log[step * k : step * (k + 1)]
        out_ref[:, k] = jnp.broadcast_to(rows[None], (n, step, HALF))


def start_kernel(
    xy_ref,
    xt_ref, yt_ref, xr_ref, yr_ref, xsq_ref, ysq_ref, out_ref,
    half_ref, shift_ref, s_ref,
):
    x = xy_ref[:, : xr_ref.shape[1]]
    xr = operand(x * (2.0 * LOG2E), **SRC)
    xr_ref[...] = xr.astype(BF)
    xt_ref[...] = jnp.transpose(xr.astype(BF))
    xsq_ref[...] = as_dense(jnp.sum(x * x, axis=0, keepdims=True))
    y = xy_ref[:, xr_ref.shape[1] :]
    yr = operand(y, **TGT)
    yr_ref[...] = yr.astype(BF)
    yt_ref[...] = jnp.transpose(yr.astype(BF))
    ysq = jnp.sum(y * y, axis=0, keepdims=True)
    ysq_ref[...] = as_dense(ysq)
    half_ref[...] = column_half(ysq * -LOG2E, 3, yt_ref)
    args = (yt_ref, half_ref, xr_ref, shift_ref)
    probe(*args, 0)
    lse(out_ref, *args, s_ref, 0)


def lse(out_ref, col_ref, half_ref, row_ref, shift_ref, s_ref, first):
    args = (col_ref, half_ref, row_ref, shift_ref)
    guarded(
        lambda: sums(*args, s_ref, first),
        lambda: slow_sums(*args, s_ref, first),
        lambda s: send_logs(out_ref, jnp.log2(s) - as_dense(shift_ref[...])),
        s_ref,
        *args,
        first,
    )


def lse_kernel(
    total, col_first, row_first,
    parts_ref, col_ref, row_ref, old_ref,
    new_ref, out_ref,
    half_ref, shift_ref, s_ref,
):
    joined_rows(total, parts_ref, new_ref)
    half_ref[...] = column_half(as_row(new_ref[...]), col_first, col_ref)
    args = (col_ref, half_ref, row_ref, shift_ref)
    if old_ref is None:
        probe(*args, row_first)
    else:
        shift_ref[...] = as_row(old_ref[...])
    lse(out_ref, *args, s_ref, row_first)


def weighted(score, values):
    w = jnp.exp2(score)
    high = w.astype(BF)
    low = (w - high.astype(F32)).astype(BF)
    return jnp.dot(values, high, preferred_element_type=F32) + jnp.dot(
        values, low, preferred_element_type=F32
    )


def maps(col_ref, half_ref, row_ref, shift_ref, values_ref, moved_ref, first):
    count, n = col_ref.shape[0], row_ref.shape[1]
    for t in range(n // TILE):
        cols = slice(t * TILE, (t + 1) * TILE)
        rhs = tile_of(row_ref, row_block(shift_ref[:, cols], first), t * TILE)
        total = jnp.zeros((HALF, TILE), F32)
        for c in range(count // CHUNK):
            values = values_ref[HALF:, c * CHUNK : (c + 1) * CHUNK]
            total += weighted(scores(col_ref, half_ref, c * CHUNK, rhs), values)
        moved_ref[:, cols] = total


def slow_maps(col_ref, half_ref, row_ref, shift_ref, values_ref, moved_ref, first):
    fold(
        col_ref, half_ref, row_ref, shift_ref, moved_ref, first, True,
        jnp.zeros((HALF, TILE), F32),
        lambda c, acc, s: acc + weighted(s, values_ref[HALF:, pl.ds(c, CHUNK)]),
        lambda acc: acc,
    )


def image(dims, scale, send, out_ref, col_ref, half_ref, row_ref, values_ref, shift_ref, moved_ref, first):
    one = first
    n, cells = out_ref.shape[0], row_ref.shape[1] // HALF
    groups = n * dims // DIM
    args = (col_ref, half_ref, row_ref, shift_ref)

    def finish(s):
        log = jnp.log2(s) - as_dense(shift_ref[...])
        base = send(out_ref, log, groups)
        part = moved_ref[16:48, :] + moved_ref[48:80, :] + moved_ref[80:112, :]
        part = part * (scale / as_row(s))
        for k in range(n):
            top, group = dims * (k // groups), k % groups
            at = base
            for cell in range(group, cells, groups):
                for d in range(top, top + dims, 4):
                    out_ref[k, at] = part[d : d + 4, HALF * cell : HALF * (cell + 1)]
                    at += 1

    guarded(
        lambda: maps(*args, values_ref, moved_ref, first),
        lambda: slow_maps(*args, values_ref, moved_ref, first),
        finish,
        moved_ref.at[one : one + 1, :],
        *args,
        first,
    )


def send_all_logs(out_ref, log, groups):
    send_logs(out_ref, log)
    return log.shape[0] // 4


def tgt_part_kernel(
    total, dims,
    parts_ref, col_ref, row_ref, values_ref, old_ref,
    new_ref, out_ref,
    half_ref, shift_ref, moved_ref,
):
    joined_rows(total, parts_ref, new_ref)
    half_ref[...] = column_half(as_row(new_ref[...]), 0, col_ref)
    shift_ref[...] = as_row(old_ref[...])
    image(
        dims, 0.5 * LN2, send_all_logs, out_ref,
        col_ref, half_ref, row_ref, values_ref, shift_ref, moved_ref, 3,
    )


def src_part(
    flip, half_ref, col_ref, row_ref, values_ref, e_ref, out_ref, rows_ref, shift_ref, moved_ref
):
    mine = lax.rem(lax.axis_index("col"), NEAR)
    count = rows_ref.shape[1] // 2
    cells = count // HALF
    for k in range(2):
        part = mine ^ (flip ^ 2 * k)
        at = slice(count * k, count * (k + 1))
        rows_ref[:, at] = row_ref[:, pl.ds(pl.multiple_of(count * part, count), count)]
        shift_ref[:, at] = as_row(e_ref[pl.ds(cells * part, cells), :])
    args = (col_ref, half_ref, rows_ref, shift_ref)

    def finish(s):
        log = jnp.log2(s) - as_dense(shift_ref[...])
        part = moved_ref[16:48, :] + moved_ref[48:80, :] + moved_ref[80:112, :]
        part = part / as_row(s)
        for k in range(2):
            out_ref[k, 0] = jnp.concatenate(
                [log[cells * k : cells * (k + 1)], jnp.zeros((4 - cells, HALF), F32)], axis=0
            )
            for c in range(cells):
                cell = cells * k + c
                for u in range(DIM // 4):
                    out_ref[k, 1 + DIM // 4 * c + u] = part[
                        4 * u : 4 * u + 4, HALF * cell : HALF * (cell + 1)
                    ]

    guarded(
        lambda: maps(*args, values_ref, moved_ref, 0),
        lambda: slow_maps(*args, values_ref, moved_ref, 0),
        finish,
        moved_ref.at[0:1, :],
        *args,
        0,
    )


def src_send_kernel(
    total, dims, groups,
    parts_ref, col_ref, row_ref, values_ref, e_ref,
    new_ref, half_ref, out_ref, tgt_out,
    tgt_ref, sem, *scratch,
):
    tgt_share(dims, groups, parts_ref, tgt_ref)
    copy = pltpu.make_async_copy(tgt_ref, tgt_out, sem)
    copy.start()
    joined_rows(total, parts_ref.at[:, : new_ref.shape[0] // 4], new_ref)
    half_ref[...] = column_half(as_row(new_ref[...]), 3, col_ref)
    src_part(1, half_ref, col_ref, row_ref, values_ref, e_ref, out_ref, *scratch)
    copy.wait()


def src_keep_kernel(half_ref, col_ref, row_ref, values_ref, e_ref, out_ref, *scratch):
    src_part(0, half_ref, col_ref, row_ref, values_ref, e_ref, out_ref, *scratch)


def share(parts_ref, out_ref, base, dims, logs_of):
    n, blocks = out_ref.shape[:2]
    each = dims // 4
    for c in range(blocks // each):
        logs = logs_of(c)
        weights = jnp.exp2(logs - jnp.max(logs, axis=0)[None])
        weights = weights / jnp.sum(weights, axis=0)[None]
        for u in range(each):
            at = c * each + u
            part = jnp.sum(parts_ref[:, base + at] * weights, axis=0)
            out_ref[:, at] = jnp.broadcast_to(part[None], (n, 4, HALF))


def tgt_share(dims, groups, parts_ref, out_ref):
    base = parts_ref.shape[1] - out_ref.shape[1]
    group = lax.rem(lax.axis_index("row"), groups)

    def logs_of(c):
        cell = groups * c + group
        return parts_ref[:, cell // 4, pl.ds(lax.rem(cell, 4), 1), :]

    share(parts_ref, out_ref, base, dims, logs_of)


def src_join_kernel(base, own, one_ref, other_ref, out_ref, parts_ref):
    for k in range(out_ref.shape[0] if own is None else 1):
        parts_ref[0] = one_ref[k if own is None else own]
        parts_ref[1] = other_ref[k]
        joined_ref = out_ref.at[k : k + 1] if own is None else out_ref
        n = joined_ref.shape[0]
        joined_ref[:, :base] = jnp.zeros((n, base, 4, HALF), F32)
        for c in range((parts_ref.shape[1] - base) * 4 // DIM):
            rows = slice(c % 4, c % 4 + 1)
            log = joined(parts_ref[:, c // 4, rows, :])
            joined_ref[:, c // 4, rows, :] = jnp.broadcast_to(log[None], (n, 1, HALF))
        src_share_kernel(DIM, parts_ref, joined_ref.at[:, base:])


def src_share_kernel(dims, parts_ref, out_ref):
    base = parts_ref.shape[1] - out_ref.shape[1]
    share(
        parts_ref, out_ref, base, dims, lambda c: parts_ref[:, c // 4, c % 4 : c % 4 + 1, :]
    )


def tgt_end_kernel(dims, e_ref, h_ref, xsq_ref, ysq_ref, tgt_ref, f_ref, g_ref, ti_ref):
    f_ref[...] = LN2 * e_ref[...] + xsq_ref[...]
    g_ref[...] = LN2 * h_ref[...] + ysq_ref[...]
    end_kernel(dims, tgt_ref, ti_ref)


def end_kernel(dims, parts_ref, out_ref):
    n, cells = parts_ref.shape[0], out_ref.shape[1] // HALF
    groups = n * dims // DIM
    for k in range(n):
        top, at = dims * (k // groups), 0
        if dims == DIM:
            span = range(k * cells // n, (k + 1) * cells // n)
        else:
            span = range(k % groups, cells, groups)
        for cell in span:
            for d in range(top, top + dims, 4):
                out_ref[d : d + 4, HALF * cell : HALF * (cell + 1)] = parts_ref[k, at]
                at += 1


def shape(*dims, dtype=F32):
    return jax.ShapeDtypeStruct(dims, dtype)


def call(kernel, ins, outs, scratch=(), name=None, cost=None, out_specs=None):
    return pl.pallas_call(
        kernel,
        out_shape=outs,
        in_specs=[VMEM] * len(ins),
        out_specs=out_specs or jax.tree.map(lambda _: VMEM, outs),
        scratch_shapes=list(scratch),
        compiler_params=pltpu.CompilerParams(vmem_limit_bytes=32 * 2**20),
        name=name,
        cost_estimate=cost,
    )(*ins)


def local(x, y):
    ns, nt = x.shape[1], y.shape[1]
    n_row, n_col = lax.axis_size("row"), lax.axis_size("col")
    rs, rt = ns // HALF, nt // HALF
    all_src, all_tgt = ns * n_row, nt * n_col
    dim_tgt = DIM // min(n_row, 8)
    grp_tgt = n_row * dim_tgt // DIM
    blk_tgt = nt * DIM // n_row // 512
    near = NEAR
    neighbours = [[near * k + j for j in range(near)] for k in range(n_col // near)]
    apart = [[near * k + j for k in range(n_col // near)] for j in range(near)]
    blk_src, log_src = ns * DIM // near // 512, -(-rs // near // 4)

    def scratch(m, n, rows=1):
        return (pltpu.VMEM((m, HALF), BF), pltpu.VMEM((1, n), F32), pltpu.VMEM((rows, n), F32))

    def over(axis, v, groups=None):
        return lax.all_to_all(v, axis, 0, 0, axis_index_groups=groups)

    xt, yt, xr, yr, xsq, ysq, parts = call(
        start_kernel,
        (jnp.concatenate([x, y], axis=1),),
        (
            shape(ns, DEPTH, dtype=BF),
            shape(nt, DEPTH, dtype=BF),
            shape(DEPTH, ns, dtype=BF),
            shape(DEPTH, nt, dtype=BF),
            shape(rs, HALF),
            shape(rt, HALF),
            shape(n_col, rs // 8, 8, HALF),
        ),
        scratch(nt, ns),
        name="start",
    )
    h = None
    for step in range(ITERS - 1):
        parts = over("col", parts)
        kernel = functools.partial(lse_kernel, all_tgt, 0, 3)
        ins = (parts, xt, yr)
        if h is None:
            base = kernel
            kernel = lambda p, c, r, *refs: base(p, c, r, None, *refs)
        else:
            ins += (h,)
        e, parts = call(
            kernel,
            ins,
            (shape(rs, HALF), shape(n_row, rt // 4, 4, HALF)),
            scratch(ns, nt),
            name="cols",
        )
        parts = over("row", parts)
        h, parts = call(
            functools.partial(lse_kernel, all_src, 3, 0),
            (parts, yt, xr, e),
            (shape(rt, HALF), shape(n_col, rs // 8, 8, HALF)),
            scratch(nt, ns),
            name="rows",
        )
    parts = over("col", parts)
    e, parts = call(
        functools.partial(tgt_part_kernel, all_tgt, dim_tgt),
        (parts, xt, yr, xr, h),
        (shape(rs, HALF), shape(n_row, rt // 4 + blk_tgt, 4, HALF)),
        scratch(ns, nt, HALF),
        name="tgt_part",
    )
    parts = over("row", parts)
    block = (log_src + blk_src, 4, HALF)
    pair = (pltpu.VMEM((2, *block), F32),)
    half = shape(2, *block)
    src_scratch = (
        pltpu.VMEM((DEPTH, ns // 2), BF),
        pltpu.VMEM((1, ns // 2), F32),
        pltpu.VMEM((HALF, ns // 2), F32),
    )
    work = pl.CostEstimate(flops=2 * 2**29, bytes_accessed=2**21, transcendentals=2**20)
    h, half_h, send, tgt = call(
        functools.partial(src_send_kernel, all_src, dim_tgt, grp_tgt),
        (parts, yt, xr, yr, e),
        (shape(rt, HALF), shape(nt, HALF, dtype=BF), half, shape(n_row, blk_tgt, 4, HALF)),
        (pltpu.VMEM((n_row, blk_tgt, 4, HALF), F32), pltpu.SemaphoreType.DMA) + src_scratch,
        name="src_send",
        cost=work,
        out_specs=(VMEM, VMEM, VMEM, HBM),
    )
    tgt = over("row", tgt)
    send = lax.ppermute(send, "col", [(i, i ^ 1) for i in range(n_col)])
    keep = call(
        src_keep_kernel, (half_h, yt, xr, yr, e), half, src_scratch, name="src_keep", cost=work
    )
    parts = call(
        functools.partial(src_join_kernel, log_src, None),
        (keep, send),
        shape(2, *block),
        pair,
        name="src_join",
    )
    came = lax.ppermute(parts[1:], "col", [(i, i ^ 2) for i in range(n_col)])
    f, g, ti = call(
        functools.partial(tgt_end_kernel, dim_tgt),
        (e, h, xsq, ysq, tgt),
        (shape(rs, HALF), shape(rt, HALF), shape(*y.shape)),
        name="tgt_end",
    )
    came, f, g, ti = lax.optimization_barrier((came, f, g, ti))
    parts = call(
        functools.partial(src_join_kernel, log_src, 0),
        (parts, came),
        shape(n_col // near, *block),
        pair,
        name="src_join2",
    )
    parts = over("col", parts, apart)
    src = call(
        functools.partial(src_share_kernel, DIM),
        (parts,),
        shape(near, blk_src, 4, HALF),
        name="src_share",
    )
    src = over("col", src, neighbours)
    si = call(functools.partial(end_kernel, DIM), (src,), shape(*x.shape), name="src_end")
    return f.reshape(ns), g.reshape(nt), si, ti


def solution(mesh):
    in_specs = (P(None, "row"), P(None, "col"))
    out_specs = (P("row"), P("col"), P(None, "row"), P(None, "col"))
    return jax.shard_map(local, mesh=mesh, in_specs=in_specs, out_specs=out_specs, check_vma=False)
```

```python
import functools
import math

import jax
import jax.numpy as jnp
from jax import lax
from jax.experimental import pallas as pl
from jax.experimental.pallas import tpu as pltpu
from jax.sharding import PartitionSpec as P

ITERS = 3
LOG2E = math.log2(math.e)
LN2 = math.log(2.0)
DEPTH = 256
HALF = 128
DIM = 32
NEAR = 4
TILE = 256
CHUNK = 256
PROBE = 64
LOW, HIGH = 2.0**-90, 2.0**100
BF, F32 = jnp.bfloat16, jnp.float32
VMEM = pl.BlockSpec(memory_space=pltpu.VMEM)
HBM = pl.BlockSpec(memory_space=pltpu.HBM)


def rounded(v):
    return v.astype(BF).astype(F32)


def split(v):
    a = rounded(v)
    b = rounded(v - a)
    return a, b, rounded(v - a - b)


def as_row(v):
    return jnp.concatenate([v[r : r + 1, :] for r in range(v.shape[0])], axis=1)


def as_dense(v):
    return jnp.concatenate(
        [v[:, HALF * r : HALF * (r + 1)] for r in range(v.shape[1] // HALF)], axis=0
    )


def potential_rows(v, first):
    a, b, c = split(v)
    row = lax.broadcasted_iota(jnp.int32, (8, v.shape[1]), 0)
    ones = jnp.where((row < 6) & ((row < first) | (row >= first + 3)), 1.0, 0.0).astype(F32)
    out = jnp.where(row == first, a, ones)
    out = jnp.where(row == first + 1, b, out)
    return jnp.where(row == first + 2, c, out)


def row_block(v, first):
    rows = potential_rows(v, first)
    return jnp.concatenate([rows, jnp.zeros_like(rows)], axis=0).astype(BF)


def operand(v, order1, order2, first):
    pieces = split(v)
    n = v.shape[1]
    zero = jnp.zeros((32, n), F32)
    rows = potential_rows(jnp.zeros((1, n), F32), first)
    return jnp.concatenate(
        [pieces[k] for k in order1]
        + [zero, rows, zero[:8]]
        + [pieces[k] for k in order2]
        + [zero[:16]],
        axis=0,
    )


SRC = dict(order1=(0, 0, 1), order2=(0, 2, 1), first=0)
TGT = dict(order1=(0, 1, 0), order2=(2, 0, 1), first=3)


def column_half(v, first, static_ref):
    rows = potential_rows(v, first)
    n = v.shape[1]
    keep = lax.broadcasted_iota(jnp.int32, (8, n), 0)
    rows = jnp.where((keep >= first) & (keep < first + 3), rows, 0.0)
    wide = jnp.concatenate([rows, jnp.zeros((HALF - 8, n), F32)], axis=0)
    return static_ref[:, HALF:] + jnp.transpose(wide.astype(BF))


def tile_of(row_ref, block, start):
    cols = pl.ds(start, TILE)
    return jnp.concatenate(
        [row_ref[:HALF, cols], block, row_ref[HALF + 16 :, cols]], axis=0
    )


def scores(col_ref, half_ref, start, rhs, count=CHUNK):
    rows = pl.ds(start, count)
    lhs = jnp.concatenate([col_ref[rows, :HALF], half_ref[rows, :]], axis=1)
    return jnp.dot(lhs, rhs, preferred_element_type=F32)


def sums(col_ref, half_ref, row_ref, shift_ref, s_ref, first):
    count, n = col_ref.shape[0], row_ref.shape[1]
    for t in range(n // TILE):
        cols = slice(t * TILE, (t + 1) * TILE)
        rhs = tile_of(row_ref, row_block(shift_ref[:, cols], first), t * TILE)
        acc = jnp.zeros((8, TILE), F32)
        for c in range(count // CHUNK):
            s = scores(col_ref, half_ref, c * CHUNK, rhs)
            acc += jnp.sum(jnp.exp2(s).reshape(CHUNK // 8, 8, TILE), axis=0)
        s_ref[:, cols] = jnp.sum(acc, axis=0, keepdims=True)


def fold(col_ref, half_ref, row_ref, shift_ref, out_ref, first, shifted, start, step, end):
    @pl.loop(0, row_ref.shape[1] // TILE)
    def _(t):
        at = pl.multiple_of(t * TILE, TILE)
        cols = pl.ds(at, TILE)
        shift = shift_ref[:, cols] if shifted else jnp.zeros((1, TILE), F32)
        rhs = tile_of(row_ref, row_block(shift, first), at)

        def chunk(c, acc):
            c = pl.multiple_of(c * CHUNK, CHUNK)
            return step(c, acc, scores(col_ref, half_ref, c, rhs))

        out_ref[:, cols] = end(lax.fori_loop(0, col_ref.shape[0] // CHUNK, chunk, start))


def peaks(col_ref, half_ref, row_ref, shift_ref, first):
    fold(
        col_ref, half_ref, row_ref, shift_ref, shift_ref, first, False,
        jnp.full((8, TILE), -jnp.inf, F32),
        lambda c, acc, s: jnp.maximum(acc, jnp.max(s.reshape(CHUNK // 8, 8, TILE), axis=0)),
        lambda acc: -jnp.max(acc, axis=0, keepdims=True),
    )


def slow_sums(col_ref, half_ref, row_ref, shift_ref, s_ref, first):
    fold(
        col_ref, half_ref, row_ref, shift_ref, s_ref, first, True,
        jnp.zeros((8, TILE), F32),
        lambda c, acc, s: acc + jnp.sum(jnp.exp2(s).reshape(CHUNK // 8, 8, TILE), axis=0),
        lambda acc: jnp.sum(acc, axis=0, keepdims=True),
    )


def probe(col_ref, half_ref, row_ref, shift_ref, first):
    for t in range(row_ref.shape[1] // TILE):
        cols = slice(t * TILE, (t + 1) * TILE)
        rhs = tile_of(row_ref, row_block(jnp.zeros((1, TILE), F32), first), t * TILE)
        s = scores(col_ref, half_ref, 0, rhs, PROBE)
        shift_ref[:, cols] = -jnp.max(s, axis=0, keepdims=True)


def outside(s):
    return jnp.any(jnp.logical_not((s > LOW) & (s < HIGH)))


def guarded(compute, redo, finish, sum_ref, col_ref, half_ref, row_ref, shift_ref, first):
    compute()
    s = as_dense(sum_ref[...])
    finish(s)

    @pl.when(outside(s))
    def _():
        peaks(col_ref, half_ref, row_ref, shift_ref, first)
        redo()
        finish(as_dense(sum_ref[...]))


def joined(parts):
    peak = jnp.max(parts, axis=0)
    return peak + jnp.log2(jnp.sum(jnp.exp2(parts - peak[None]), axis=0))


def joined_rows(total, parts_ref, new_ref):
    new = math.log2(total) - joined(parts_ref[...])
    step = new.shape[1]
    for k in range(new.shape[0]):
        new_ref[step * k : step * (k + 1), :] = new[k]


def send_logs(out_ref, log):
    n, step = out_ref.shape[0], out_ref.shape[2]
    for k in range(log.shape[0] // step):
        rows = log[step * k : step * (k + 1)]
        out_ref[:, k] = jnp.broadcast_to(rows[None], (n, step, HALF))


def start_kernel(
    xy_ref,
    xt_ref, yt_ref, xr_ref, yr_ref, xsq_ref, ysq_ref, out_ref,
    half_ref, shift_ref, s_ref,
):
    x = xy_ref[:, : xr_ref.shape[1]]
    xr = operand(x * (2.0 * LOG2E), **SRC)
    xr_ref[...] = xr.astype(BF)
    xt_ref[...] = jnp.transpose(xr.astype(BF))
    xsq_ref[...] = as_dense(jnp.sum(x * x, axis=0, keepdims=True))
    y = xy_ref[:, xr_ref.shape[1] :]
    yr = operand(y, **TGT)
    yr_ref[...] = yr.astype(BF)
    yt_ref[...] = jnp.transpose(yr.astype(BF))
    ysq = jnp.sum(y * y, axis=0, keepdims=True)
    ysq_ref[...] = as_dense(ysq)
    half_ref[...] = column_half(ysq * -LOG2E, 3, yt_ref)
    args = (yt_ref, half_ref, xr_ref, shift_ref)
    probe(*args, 0)
    lse(out_ref, *args, s_ref, 0)


def lse(out_ref, col_ref, half_ref, row_ref, shift_ref, s_ref, first):
    args = (col_ref, half_ref, row_ref, shift_ref)
    guarded(
        lambda: sums(*args, s_ref, first),
        lambda: slow_sums(*args, s_ref, first),
        lambda s: send_logs(out_ref, jnp.log2(s) - as_dense(shift_ref[...])),
        s_ref,
        *args,
        first,
    )


def lse_kernel(
    total, col_first, row_first,
    parts_ref, col_ref, row_ref, old_ref,
    new_ref, out_ref,
    half_ref, shift_ref, s_ref,
):
    joined_rows(total, parts_ref, new_ref)
    half_ref[...] = column_half(as_row(new_ref[...]), col_first, col_ref)
    args = (col_ref, half_ref, row_ref, shift_ref)
    if old_ref is None:
        probe(*args, row_first)
    else:
        shift_ref[...] = as_row(old_ref[...])
    lse(out_ref, *args, s_ref, row_first)


def weighted(score, values):
    w = jnp.exp2(score)
    high = w.astype(BF)
    low = (w - high.astype(F32)).astype(BF)
    return jnp.dot(values, high, preferred_element_type=F32) + jnp.dot(
        values, low, preferred_element_type=F32
    )


def maps(col_ref, half_ref, row_ref, shift_ref, values_ref, moved_ref, first):
    count, n = col_ref.shape[0], row_ref.shape[1]
    for t in range(n // TILE):
        cols = slice(t * TILE, (t + 1) * TILE)
        rhs = tile_of(row_ref, row_block(shift_ref[:, cols], first), t * TILE)
        total = jnp.zeros((HALF, TILE), F32)
        for c in range(count // CHUNK):
            values = values_ref[HALF:, c * CHUNK : (c + 1) * CHUNK]
            total += weighted(scores(col_ref, half_ref, c * CHUNK, rhs), values)
        moved_ref[:, cols] = total


def slow_maps(col_ref, half_ref, row_ref, shift_ref, values_ref, moved_ref, first):
    fold(
        col_ref, half_ref, row_ref, shift_ref, moved_ref, first, True,
        jnp.zeros((HALF, TILE), F32),
        lambda c, acc, s: acc + weighted(s, values_ref[HALF:, pl.ds(c, CHUNK)]),
        lambda acc: acc,
    )


def image(dims, scale, send, out_ref, col_ref, half_ref, row_ref, values_ref, shift_ref, moved_ref, first):
    one = first
    n, cells = out_ref.shape[0], row_ref.shape[1] // HALF
    groups = n * dims // DIM
    args = (col_ref, half_ref, row_ref, shift_ref)

    def finish(s):
        log = jnp.log2(s) - as_dense(shift_ref[...])
        base = send(out_ref, log, groups)
        part = moved_ref[16:48, :] + moved_ref[48:80, :] + moved_ref[80:112, :]
        part = part * (scale / as_row(s))
        for k in range(n):
            top, group = dims * (k // groups), k % groups
            at = base
            for cell in range(group, cells, groups):
                for d in range(top, top + dims, 4):
                    out_ref[k, at] = part[d : d + 4, HALF * cell : HALF * (cell + 1)]
                    at += 1

    guarded(
        lambda: maps(*args, values_ref, moved_ref, first),
        lambda: slow_maps(*args, values_ref, moved_ref, first),
        finish,
        moved_ref.at[one : one + 1, :],
        *args,
        first,
    )


def send_all_logs(out_ref, log, groups):
    send_logs(out_ref, log)
    return log.shape[0] // 4


def tgt_part_kernel(
    total, dims,
    parts_ref, col_ref, row_ref, values_ref, old_ref,
    new_ref, out_ref,
    half_ref, shift_ref, moved_ref,
):
    joined_rows(total, parts_ref, new_ref)
    half_ref[...] = column_half(as_row(new_ref[...]), 0, col_ref)
    shift_ref[...] = as_row(old_ref[...])
    image(
        dims, 0.5 * LN2, send_all_logs, out_ref,
        col_ref, half_ref, row_ref, values_ref, shift_ref, moved_ref, 3,
    )


def src_part(
    flip, half_ref, col_ref, row_ref, values_ref, e_ref, out_ref, rows_ref, shift_ref, moved_ref
):
    mine = lax.rem(lax.axis_index("col"), NEAR)
    count = rows_ref.shape[1] // 2
    cells = count // HALF
    for k in range(2):
        part = mine ^ (flip ^ 2 * k)
        at = slice(count * k, count * (k + 1))
        rows_ref[:, at] = row_ref[:, pl.ds(pl.multiple_of(count * part, count), count)]
        shift_ref[:, at] = as_row(e_ref[pl.ds(cells * part, cells), :])
    args = (col_ref, half_ref, rows_ref, shift_ref)

    def finish(s):
        log = jnp.log2(s) - as_dense(shift_ref[...])
        part = moved_ref[16:48, :] + moved_ref[48:80, :] + moved_ref[80:112, :]
        part = part / as_row(s)
        for k in range(2):
            out_ref[k, 0] = jnp.concatenate(
                [log[cells * k : cells * (k + 1)], jnp.zeros((4 - cells, HALF), F32)], axis=0
            )
            for c in range(cells):
                cell = cells * k + c
                for u in range(DIM // 4):
                    out_ref[k, 1 + DIM // 4 * c + u] = part[
                        4 * u : 4 * u + 4, HALF * cell : HALF * (cell + 1)
                    ]

    guarded(
        lambda: maps(*args, values_ref, moved_ref, 0),
        lambda: slow_maps(*args, values_ref, moved_ref, 0),
        finish,
        moved_ref.at[0:1, :],
        *args,
        0,
    )


def src_send_kernel(
    total, dims, groups,
    parts_ref, col_ref, row_ref, values_ref, e_ref,
    new_ref, half_ref, out_ref, tgt_out,
    tgt_ref, sem, *scratch,
):
    tgt_share(dims, groups, parts_ref, tgt_ref)
    copy = pltpu.make_async_copy(tgt_ref, tgt_out, sem)
    copy.start()
    joined_rows(total, parts_ref.at[:, : new_ref.shape[0] // 4], new_ref)
    half_ref[...] = column_half(as_row(new_ref[...]), 3, col_ref)
    src_part(1, half_ref, col_ref, row_ref, values_ref, e_ref, out_ref, *scratch)
    copy.wait()


def src_keep_kernel(half_ref, col_ref, row_ref, values_ref, e_ref, out_ref, *scratch):
    src_part(0, half_ref, col_ref, row_ref, values_ref, e_ref, out_ref, *scratch)


def share(parts_ref, out_ref, base, dims, logs_of):
    n, blocks = out_ref.shape[:2]
    each = dims // 4
    for c in range(blocks // each):
        logs = logs_of(c)
        weights = jnp.exp2(logs - jnp.max(logs, axis=0)[None])
        whole = 1.0 / jnp.sum(weights, axis=0)
        for u in range(each):
            at = c * each + u
            part = jnp.sum(parts_ref[:, base + at] * weights, axis=0) * whole
            out_ref[:, at] = jnp.broadcast_to(part[None], (n, 4, HALF))


def tgt_share(dims, groups, parts_ref, out_ref):
    base = parts_ref.shape[1] - out_ref.shape[1]
    group = lax.rem(lax.axis_index("row"), groups)

    def logs_of(c):
        cell = groups * c + group
        return parts_ref[:, cell // 4, pl.ds(lax.rem(cell, 4), 1), :]

    share(parts_ref, out_ref, base, dims, logs_of)


def src_join_kernel(base, own, one_ref, other_ref, out_ref, parts_ref):
    for k in range(out_ref.shape[0] if own is None else 1):
        parts_ref[0] = one_ref[k if own is None else own]
        parts_ref[1] = other_ref[k]
        joined_ref = out_ref.at[k : k + 1] if own is None else out_ref
        n = joined_ref.shape[0]
        joined_ref[:, :base] = jnp.zeros((n, base, 4, HALF), F32)
        for c in range((parts_ref.shape[1] - base) * 4 // DIM):
            rows = slice(c % 4, c % 4 + 1)
            log = joined(parts_ref[:, c // 4, rows, :])
            joined_ref[:, c // 4, rows, :] = jnp.broadcast_to(log[None], (n, 1, HALF))
        src_share_kernel(DIM, parts_ref, joined_ref.at[:, base:])


def src_share_kernel(dims, parts_ref, out_ref):
    base = parts_ref.shape[1] - out_ref.shape[1]
    share(
        parts_ref, out_ref, base, dims, lambda c: parts_ref[:, c // 4, c % 4 : c % 4 + 1, :]
    )


def tgt_end_kernel(dims, e_ref, h_ref, xsq_ref, ysq_ref, tgt_ref, f_ref, g_ref, ti_ref):
    f_ref[...] = LN2 * e_ref[...] + xsq_ref[...]
    g_ref[...] = LN2 * h_ref[...] + ysq_ref[...]
    end_kernel(dims, tgt_ref, ti_ref)


def end_kernel(dims, parts_ref, out_ref):
    n, cells = parts_ref.shape[0], out_ref.shape[1] // HALF
    groups = n * dims // DIM
    for k in range(n):
        top, at = dims * (k // groups), 0
        if dims == DIM:
            span = range(k * cells // n, (k + 1) * cells // n)
        else:
            span = range(k % groups, cells, groups)
        for cell in span:
            for d in range(top, top + dims, 4):
                out_ref[d : d + 4, HALF * cell : HALF * (cell + 1)] = parts_ref[k, at]
                at += 1


def shape(*dims, dtype=F32):
    return jax.ShapeDtypeStruct(dims, dtype)


def call(kernel, ins, outs, scratch=(), name=None, cost=None, out_specs=None):
    return pl.pallas_call(
        kernel,
        out_shape=outs,
        in_specs=[VMEM] * len(ins),
        out_specs=out_specs or jax.tree.map(lambda _: VMEM, outs),
        scratch_shapes=list(scratch),
        compiler_params=pltpu.CompilerParams(vmem_limit_bytes=32 * 2**20),
        name=name,
        cost_estimate=cost,
    )(*ins)


def local(x, y):
    ns, nt = x.shape[1], y.shape[1]
    n_row, n_col = lax.axis_size("row"), lax.axis_size("col")
    rs, rt = ns // HALF, nt // HALF
    all_src, all_tgt = ns * n_row, nt * n_col
    dim_tgt = DIM // min(n_row, 8)
    grp_tgt = n_row * dim_tgt // DIM
    blk_tgt = nt * DIM // n_row // 512
    near = NEAR
    neighbours = [[near * k + j for j in range(near)] for k in range(n_col // near)]
    apart = [[near * k + j for k in range(n_col // near)] for j in range(near)]
    blk_src, log_src = ns * DIM // near // 512, -(-rs // near // 4)

    def scratch(m, n, rows=1):
        return (pltpu.VMEM((m, HALF), BF), pltpu.VMEM((1, n), F32), pltpu.VMEM((rows, n), F32))

    def over(axis, v, groups=None):
        return lax.all_to_all(v, axis, 0, 0, axis_index_groups=groups)

    xt, yt, xr, yr, xsq, ysq, parts = call(
        start_kernel,
        (jnp.concatenate([x, y], axis=1),),
        (
            shape(ns, DEPTH, dtype=BF),
            shape(nt, DEPTH, dtype=BF),
            shape(DEPTH, ns, dtype=BF),
            shape(DEPTH, nt, dtype=BF),
            shape(rs, HALF),
            shape(rt, HALF),
            shape(n_col, rs // 8, 8, HALF),
        ),
        scratch(nt, ns),
        name="start",
    )
    h = None
    for step in range(ITERS - 1):
        parts = over("col", parts)
        kernel = functools.partial(lse_kernel, all_tgt, 0, 3)
        ins = (parts, xt, yr)
        if h is None:
            base = kernel
            kernel = lambda p, c, r, *refs: base(p, c, r, None, *refs)
        else:
            ins += (h,)
        e, parts = call(
            kernel,
            ins,
            (shape(rs, HALF), shape(n_row, rt // 4, 4, HALF)),
            scratch(ns, nt),
            name="cols",
        )
        parts = over("row", parts)
        h, parts = call(
            functools.partial(lse_kernel, all_src, 3, 0),
            (parts, yt, xr, e),
            (shape(rt, HALF), shape(n_col, rs // 8, 8, HALF)),
            scratch(nt, ns),
            name="rows",
        )
    parts = over("col", parts)
    e, parts = call(
        functools.partial(tgt_part_kernel, all_tgt, dim_tgt),
        (parts, xt, yr, xr, h),
        (shape(rs, HALF), shape(n_row, rt // 4 + blk_tgt, 4, HALF)),
        scratch(ns, nt, HALF),
        name="tgt_part",
    )
    parts = over("row", parts)
    block = (log_src + blk_src, 4, HALF)
    pair = (pltpu.VMEM((2, *block), F32),)
    half = shape(2, *block)
    src_scratch = (
        pltpu.VMEM((DEPTH, ns // 2), BF),
        pltpu.VMEM((1, ns // 2), F32),
        pltpu.VMEM((HALF, ns // 2), F32),
    )
    work = pl.CostEstimate(flops=2 * 2**29, bytes_accessed=2**21, transcendentals=2**20)
    h, half_h, send, tgt = call(
        functools.partial(src_send_kernel, all_src, dim_tgt, grp_tgt),
        (parts, yt, xr, yr, e),
        (shape(rt, HALF), shape(nt, HALF, dtype=BF), half, shape(n_row, blk_tgt, 4, HALF)),
        (pltpu.VMEM((n_row, blk_tgt, 4, HALF), F32), pltpu.SemaphoreType.DMA) + src_scratch,
        name="src_send",
        cost=work,
        out_specs=(VMEM, VMEM, VMEM, HBM),
    )
    tgt = over("row", tgt)
    send = lax.ppermute(send, "col", [(i, i ^ 1) for i in range(n_col)])
    keep = call(
        src_keep_kernel, (half_h, yt, xr, yr, e), half, src_scratch, name="src_keep", cost=work
    )
    parts = call(
        functools.partial(src_join_kernel, log_src, None),
        (keep, send),
        shape(2, *block),
        pair,
        name="src_join",
    )
    came = lax.ppermute(parts[1:], "col", [(i, i ^ 2) for i in range(n_col)])
    f, g, ti = call(
        functools.partial(tgt_end_kernel, dim_tgt),
        (e, h, xsq, ysq, tgt),
        (shape(rs, HALF), shape(rt, HALF), shape(*y.shape)),
        name="tgt_end",
    )
    came, f, g, ti = lax.optimization_barrier((came, f, g, ti))
    parts = call(
        functools.partial(src_join_kernel, log_src, 0),
        (parts, came),
        shape(n_col // near, *block),
        pair,
        name="src_join2",
    )
    parts = over("col", parts, apart)
    src = call(
        functools.partial(src_share_kernel, DIM),
        (parts,),
        shape(near, blk_src, 4, HALF),
        name="src_share",
    )
    src = over("col", src, neighbours)
    si = call(functools.partial(end_kernel, DIM), (src,), shape(*x.shape), name="src_end")
    return f.reshape(ns), g.reshape(nt), si, ti


def solution(mesh):
    in_specs = (P(None, "row"), P(None, "col"))
    out_specs = (P("row"), P("col"), P(None, "row"), P(None, "col"))
    return jax.shard_map(local, mesh=mesh, in_specs=in_specs, out_specs=out_specs, check_vma=False)
```

```python
import functools
import math

import jax
import jax.numpy as jnp
from jax import lax
from jax.experimental import pallas as pl
from jax.experimental.pallas import tpu as pltpu
from jax.sharding import PartitionSpec as P

ITERS = 3
LOG2E = math.log2(math.e)
LN2 = math.log(2.0)
DEPTH = 256
HALF = 128
DIM = 32
NEAR = 4
TILE = 256
CHUNK = 256
PROBE = 64
LOW, HIGH = 2.0**-90, 2.0**100
BF, F32 = jnp.bfloat16, jnp.float32
VMEM = pl.BlockSpec(memory_space=pltpu.VMEM)
HBM = pl.BlockSpec(memory_space=pltpu.HBM)


def rounded(v):
    return v.astype(BF).astype(F32)


def split(v):
    a = rounded(v)
    b = rounded(v - a)
    return a, b, rounded(v - a - b)


def as_row(v):
    return jnp.concatenate([v[r : r + 1, :] for r in range(v.shape[0])], axis=1)


def as_dense(v):
    return jnp.concatenate(
        [v[:, HALF * r : HALF * (r + 1)] for r in range(v.shape[1] // HALF)], axis=0
    )


def potential_rows(v, first):
    a, b, c = split(v)
    row = lax.broadcasted_iota(jnp.int32, (8, v.shape[1]), 0)
    ones = jnp.where((row < 6) & ((row < first) | (row >= first + 3)), 1.0, 0.0).astype(F32)
    out = jnp.where(row == first, a, ones)
    out = jnp.where(row == first + 1, b, out)
    return jnp.where(row == first + 2, c, out)


def row_block(v, first):
    rows = potential_rows(v, first)
    return jnp.concatenate([rows, jnp.zeros_like(rows)], axis=0).astype(BF)


def operand(v, order1, order2, first):
    pieces = split(v)
    n = v.shape[1]
    zero = jnp.zeros((32, n), F32)
    rows = potential_rows(jnp.zeros((1, n), F32), first)
    return jnp.concatenate(
        [pieces[k] for k in order1]
        + [zero, rows, zero[:8]]
        + [pieces[k] for k in order2]
        + [zero[:16]],
        axis=0,
    )


SRC = dict(order1=(0, 0, 1), order2=(0, 2, 1), first=0)
TGT = dict(order1=(0, 1, 0), order2=(2, 0, 1), first=3)


def column_half(v, first, static_ref):
    rows = potential_rows(v, first)
    n = v.shape[1]
    keep = lax.broadcasted_iota(jnp.int32, (8, n), 0)
    rows = jnp.where((keep >= first) & (keep < first + 3), rows, 0.0)
    wide = jnp.concatenate([rows, jnp.zeros((HALF - 8, n), F32)], axis=0)
    return static_ref[:, HALF:] + jnp.transpose(wide.astype(BF))


def tile_of(row_ref, block, start):
    cols = pl.ds(start, TILE)
    return jnp.concatenate(
        [row_ref[:HALF, cols], block, row_ref[HALF + 16 :, cols]], axis=0
    )


def scores(col_ref, half_ref, start, rhs, count=CHUNK):
    rows = pl.ds(start, count)
    lhs = jnp.concatenate([col_ref[rows, :HALF], half_ref[rows, :]], axis=1)
    return jnp.dot(lhs, rhs, preferred_element_type=F32)


def sums(col_ref, half_ref, row_ref, shift_ref, s_ref, first):
    count, n = col_ref.shape[0], row_ref.shape[1]
    for t in range(n // TILE):
        cols = slice(t * TILE, (t + 1) * TILE)
        rhs = tile_of(row_ref, row_block(shift_ref[:, cols], first), t * TILE)
        acc = jnp.zeros((8, TILE), F32)
        for c in range(count // CHUNK):
            s = scores(col_ref, half_ref, c * CHUNK, rhs)
            acc += jnp.sum(jnp.exp2(s).reshape(CHUNK // 8, 8, TILE), axis=0)
        s_ref[:, cols] = jnp.sum(acc, axis=0, keepdims=True)


def fold(col_ref, half_ref, row_ref, shift_ref, out_ref, first, shifted, start, step, end):
    @pl.loop(0, row_ref.shape[1] // TILE)
    def _(t):
        at = pl.multiple_of(t * TILE, TILE)
        cols = pl.ds(at, TILE)
        shift = shift_ref[:, cols] if shifted else jnp.zeros((1, TILE), F32)
        rhs = tile_of(row_ref, row_block(shift, first), at)

        def chunk(c, acc):
            c = pl.multiple_of(c * CHUNK, CHUNK)
            return step(c, acc, scores(col_ref, half_ref, c, rhs))

        out_ref[:, cols] = end(lax.fori_loop(0, col_ref.shape[0] // CHUNK, chunk, start))


def peaks(col_ref, half_ref, row_ref, shift_ref, first):
    fold(
        col_ref, half_ref, row_ref, shift_ref, shift_ref, first, False,
        jnp.full((8, TILE), -jnp.inf, F32),
        lambda c, acc, s: jnp.maximum(acc, jnp.max(s.reshape(CHUNK // 8, 8, TILE), axis=0)),
        lambda acc: -jnp.max(acc, axis=0, keepdims=True),
    )


def slow_sums(col_ref, half_ref, row_ref, shift_ref, s_ref, first):
    fold(
        col_ref, half_ref, row_ref, shift_ref, s_ref, first, True,
        jnp.zeros((8, TILE), F32),
        lambda c, acc, s: acc + jnp.sum(jnp.exp2(s).reshape(CHUNK // 8, 8, TILE), axis=0),
        lambda acc: jnp.sum(acc, axis=0, keepdims=True),
    )


def probe(col_ref, half_ref, row_ref, shift_ref, first):
    for t in range(row_ref.shape[1] // TILE):
        cols = slice(t * TILE, (t + 1) * TILE)
        rhs = tile_of(row_ref, row_block(jnp.zeros((1, TILE), F32), first), t * TILE)
        s = scores(col_ref, half_ref, 0, rhs, PROBE)
        shift_ref[:, cols] = -jnp.max(s, axis=0, keepdims=True)


def outside(s):
    return jnp.any(jnp.logical_not((s > LOW) & (s < HIGH)))


def guarded(compute, redo, finish, sum_ref, col_ref, half_ref, row_ref, shift_ref, first):
    compute()
    s = as_dense(sum_ref[...])
    finish(s)

    @pl.when(outside(s))
    def _():
        peaks(col_ref, half_ref, row_ref, shift_ref, first)
        redo()
        finish(as_dense(sum_ref[...]))


def joined(parts):
    peak = jnp.max(parts, axis=0)
    return peak + jnp.log2(jnp.sum(jnp.exp2(parts - peak[None]), axis=0))


def joined_rows(total, parts_ref, new_ref):
    new = math.log2(total) - joined(parts_ref[...])
    step = new.shape[1]
    for k in range(new.shape[0]):
        new_ref[step * k : step * (k + 1), :] = new[k]


def send_logs(out_ref, log):
    n, step = out_ref.shape[0], out_ref.shape[2]
    for k in range(log.shape[0] // step):
        rows = log[step * k : step * (k + 1)]
        out_ref[:, k] = jnp.broadcast_to(rows[None], (n, step, HALF))


def start_kernel(
    xy_ref,
    xt_ref, yt_ref, xr_ref, yr_ref, xsq_ref, ysq_ref, out_ref,
    half_ref, shift_ref, s_ref,
):
    x = xy_ref[:, : xr_ref.shape[1]]
    xr = operand(x * (2.0 * LOG2E), **SRC)
    xr_ref[...] = xr.astype(BF)
    xt_ref[...] = jnp.transpose(xr.astype(BF))
    xsq_ref[...] = as_dense(jnp.sum(x * x, axis=0, keepdims=True))
    y = xy_ref[:, xr_ref.shape[1] :]
    yr = operand(y, **TGT)
    yr_ref[...] = yr.astype(BF)
    yt_ref[...] = jnp.transpose(yr.astype(BF))
    ysq = jnp.sum(y * y, axis=0, keepdims=True)
    ysq_ref[...] = as_dense(ysq)
    half_ref[...] = column_half(ysq * -LOG2E, 3, yt_ref)
    args = (yt_ref, half_ref, xr_ref, shift_ref)
    probe(*args, 0)
    lse(out_ref, *args, s_ref, 0)


def lse(out_ref, col_ref, half_ref, row_ref, shift_ref, s_ref, first):
    args = (col_ref, half_ref, row_ref, shift_ref)
    guarded(
        lambda: sums(*args, s_ref, first),
        lambda: slow_sums(*args, s_ref, first),
        lambda s: send_logs(out_ref, jnp.log2(s) - as_dense(shift_ref[...])),
        s_ref,
        *args,
        first,
    )


def lse_kernel(
    total, col_first, row_first,
    parts_ref, col_ref, row_ref, old_ref,
    new_ref, out_ref,
    half_ref, shift_ref, s_ref,
):
    joined_rows(total, parts_ref, new_ref)
    half_ref[...] = column_half(as_row(new_ref[...]), col_first, col_ref)
    args = (col_ref, half_ref, row_ref, shift_ref)
    if old_ref is None:
        probe(*args, row_first)
    else:
        shift_ref[...] = as_row(old_ref[...])
    lse(out_ref, *args, s_ref, row_first)


def weighted(score, values):
    w = jnp.exp2(score)
    high = w.astype(BF)
    low = (w - high.astype(F32)).astype(BF)
    return jnp.dot(values, high, preferred_element_type=F32) + jnp.dot(
        values, low, preferred_element_type=F32
    )


def maps(col_ref, half_ref, row_ref, shift_ref, values_ref, moved_ref, first, beside=None):
    count, n = col_ref.shape[0], row_ref.shape[1]
    for t in range(n // TILE):
        cols = slice(t * TILE, (t + 1) * TILE)
        rhs = tile_of(row_ref, row_block(shift_ref[:, cols], first), t * TILE)
        total = jnp.zeros((HALF, TILE), F32)
        for c in range(count // CHUNK):
            values = values_ref[HALF:, c * CHUNK : (c + 1) * CHUNK]
            total += weighted(scores(col_ref, half_ref, c * CHUNK, rhs), values)
        moved_ref[:, cols] = total
        if beside and t == 0:
            beside()


def slow_maps(col_ref, half_ref, row_ref, shift_ref, values_ref, moved_ref, first):
    fold(
        col_ref, half_ref, row_ref, shift_ref, moved_ref, first, True,
        jnp.zeros((HALF, TILE), F32),
        lambda c, acc, s: acc + weighted(s, values_ref[HALF:, pl.ds(c, CHUNK)]),
        lambda acc: acc,
    )


def image(dims, scale, send, out_ref, col_ref, half_ref, row_ref, values_ref, shift_ref, moved_ref, first):
    one = first
    n, cells = out_ref.shape[0], row_ref.shape[1] // HALF
    groups = n * dims // DIM
    args = (col_ref, half_ref, row_ref, shift_ref)

    def finish(s):
        log = jnp.log2(s) - as_dense(shift_ref[...])
        base = send(out_ref, log, groups)
        part = moved_ref[16:48, :] + moved_ref[48:80, :] + moved_ref[80:112, :]
        part = part * (scale / as_row(s))
        for k in range(n):
            top, group = dims * (k // groups), k % groups
            at = base
            for cell in range(group, cells, groups):
                for d in range(top, top + dims, 4):
                    out_ref[k, at] = part[d : d + 4, HALF * cell : HALF * (cell + 1)]
                    at += 1

    guarded(
        lambda: maps(*args, values_ref, moved_ref, first),
        lambda: slow_maps(*args, values_ref, moved_ref, first),
        finish,
        moved_ref.at[one : one + 1, :],
        *args,
        first,
    )


def send_all_logs(out_ref, log, groups):
    send_logs(out_ref, log)
    return log.shape[0] // 4


def tgt_part_kernel(
    total, dims,
    parts_ref, col_ref, row_ref, values_ref, old_ref,
    new_ref, out_ref,
    half_ref, shift_ref, moved_ref,
):
    joined_rows(total, parts_ref, new_ref)
    half_ref[...] = column_half(as_row(new_ref[...]), 0, col_ref)
    shift_ref[...] = as_row(old_ref[...])
    image(
        dims, 0.5 * LN2, send_all_logs, out_ref,
        col_ref, half_ref, row_ref, values_ref, shift_ref, moved_ref, 3,
    )


def src_part(
    flip, half_ref, col_ref, row_ref, values_ref, e_ref, out_ref, rows_ref, shift_ref, moved_ref,
    beside=None,
):
    mine = lax.rem(lax.axis_index("col"), NEAR)
    count = rows_ref.shape[1] // 2
    cells = count // HALF
    for k in range(2):
        part = mine ^ (flip ^ 2 * k)
        at = slice(count * k, count * (k + 1))
        rows_ref[:, at] = row_ref[:, pl.ds(pl.multiple_of(count * part, count), count)]
        shift_ref[:, at] = as_row(e_ref[pl.ds(cells * part, cells), :])
    args = (col_ref, half_ref, rows_ref, shift_ref)

    def finish(s):
        log = jnp.log2(s) - as_dense(shift_ref[...])
        part = moved_ref[16:48, :] + moved_ref[48:80, :] + moved_ref[80:112, :]
        part = part / as_row(s)
        for k in range(2):
            out_ref[k, 0] = jnp.concatenate(
                [log[cells * k : cells * (k + 1)], jnp.zeros((4 - cells, HALF), F32)], axis=0
            )
            for c in range(cells):
                cell = cells * k + c
                for u in range(DIM // 4):
                    out_ref[k, 1 + DIM // 4 * c + u] = part[
                        4 * u : 4 * u + 4, HALF * cell : HALF * (cell + 1)
                    ]

    guarded(
        lambda: maps(*args, values_ref, moved_ref, 0, beside),
        lambda: slow_maps(*args, values_ref, moved_ref, 0),
        finish,
        moved_ref.at[0:1, :],
        *args,
        0,
    )


def src_send_kernel(
    total, dims, groups,
    parts_ref, col_ref, row_ref, values_ref, e_ref,
    new_ref, half_ref, out_ref, tgt_out,
    tgt_ref, sem, *scratch,
):
    copy = pltpu.make_async_copy(tgt_ref, tgt_out, sem)
    joined_rows(total, parts_ref.at[:, : new_ref.shape[0] // 4], new_ref)
    half_ref[...] = column_half(as_row(new_ref[...]), 3, col_ref)
    tgt_share(dims, groups, parts_ref, tgt_ref)
    src_part(1, half_ref, col_ref, row_ref, values_ref, e_ref, out_ref, *scratch, copy.start)
    copy.wait()


def src_keep_kernel(half_ref, col_ref, row_ref, values_ref, e_ref, out_ref, *scratch):
    src_part(0, half_ref, col_ref, row_ref, values_ref, e_ref, out_ref, *scratch)


def share(parts_ref, out_ref, base, dims, logs_of):
    n, blocks = out_ref.shape[:2]
    each = dims // 4
    for c in range(blocks // each):
        logs = logs_of(c)
        weights = jnp.exp2(logs - jnp.max(logs, axis=0)[None])
        whole = 1.0 / jnp.sum(weights, axis=0)
        for u in range(each):
            at = c * each + u
            part = jnp.sum(parts_ref[:, base + at] * weights, axis=0) * whole
            out_ref[:, at] = jnp.broadcast_to(part[None], (n, 4, HALF))


def tgt_share(dims, groups, parts_ref, out_ref):
    base = parts_ref.shape[1] - out_ref.shape[1]
    group = lax.rem(lax.axis_index("row"), groups)

    def logs_of(c):
        cell = groups * c + group
        return parts_ref[:, cell // 4, pl.ds(lax.rem(cell, 4), 1), :]

    share(parts_ref, out_ref, base, dims, logs_of)


def src_join_kernel(base, own, one_ref, other_ref, out_ref, parts_ref):
    for k in range(out_ref.shape[0] if own is None else 1):
        parts_ref[0] = one_ref[k if own is None else own]
        parts_ref[1] = other_ref[k]
        joined_ref = out_ref.at[k : k + 1] if own is None else out_ref
        n = joined_ref.shape[0]
        joined_ref[:, :base] = jnp.zeros((n, base, 4, HALF), F32)
        for c in range((parts_ref.shape[1] - base) * 4 // DIM):
            rows = slice(c % 4, c % 4 + 1)
            log = joined(parts_ref[:, c // 4, rows, :])
            joined_ref[:, c // 4, rows, :] = jnp.broadcast_to(log[None], (n, 1, HALF))
        src_share_kernel(DIM, parts_ref, joined_ref.at[:, base:])


def src_share_kernel(dims, parts_ref, out_ref):
    base = parts_ref.shape[1] - out_ref.shape[1]
    share(
        parts_ref, out_ref, base, dims, lambda c: parts_ref[:, c // 4, c % 4 : c % 4 + 1, :]
    )


def tgt_end_kernel(dims, e_ref, h_ref, xsq_ref, ysq_ref, tgt_ref, f_ref, g_ref, ti_ref):
    f_ref[...] = LN2 * e_ref[...] + xsq_ref[...]
    g_ref[...] = LN2 * h_ref[...] + ysq_ref[...]
    end_kernel(dims, tgt_ref, ti_ref)


def end_kernel(dims, parts_ref, out_ref):
    n, cells = parts_ref.shape[0], out_ref.shape[1] // HALF
    groups = n * dims // DIM
    for k in range(n):
        top, at = dims * (k // groups), 0
        if dims == DIM:
            span = range(k * cells // n, (k + 1) * cells // n)
        else:
            span = range(k % groups, cells, groups)
        for cell in span:
            for d in range(top, top + dims, 4):
                out_ref[d : d + 4, HALF * cell : HALF * (cell + 1)] = parts_ref[k, at]
                at += 1


def shape(*dims, dtype=F32):
    return jax.ShapeDtypeStruct(dims, dtype)


def call(kernel, ins, outs, scratch=(), name=None, cost=None, out_specs=None):
    return pl.pallas_call(
        kernel,
        out_shape=outs,
        in_specs=[VMEM] * len(ins),
        out_specs=out_specs or jax.tree.map(lambda _: VMEM, outs),
        scratch_shapes=list(scratch),
        compiler_params=pltpu.CompilerParams(vmem_limit_bytes=32 * 2**20),
        name=name,
        cost_estimate=cost,
    )(*ins)


def local(x, y):
    ns, nt = x.shape[1], y.shape[1]
    n_row, n_col = lax.axis_size("row"), lax.axis_size("col")
    rs, rt = ns // HALF, nt // HALF
    all_src, all_tgt = ns * n_row, nt * n_col
    dim_tgt = DIM // min(n_row, 8)
    grp_tgt = n_row * dim_tgt // DIM
    blk_tgt = nt * DIM // n_row // 512
    near = NEAR
    neighbours = [[near * k + j for j in range(near)] for k in range(n_col // near)]
    apart = [[near * k + j for k in range(n_col // near)] for j in range(near)]
    blk_src, log_src = ns * DIM // near // 512, -(-rs // near // 4)

    def scratch(m, n, rows=1):
        return (pltpu.VMEM((m, HALF), BF), pltpu.VMEM((1, n), F32), pltpu.VMEM((rows, n), F32))

    def over(axis, v, groups=None):
        return lax.all_to_all(v, axis, 0, 0, axis_index_groups=groups)

    xt, yt, xr, yr, xsq, ysq, parts = call(
        start_kernel,
        (jnp.concatenate([x, y], axis=1),),
        (
            shape(ns, DEPTH, dtype=BF),
            shape(nt, DEPTH, dtype=BF),
            shape(DEPTH, ns, dtype=BF),
            shape(DEPTH, nt, dtype=BF),
            shape(rs, HALF),
            shape(rt, HALF),
            shape(n_col, rs // 8, 8, HALF),
        ),
        scratch(nt, ns),
        name="start",
    )
    h = None
    for step in range(ITERS - 1):
        parts = over("col", parts)
        kernel = functools.partial(lse_kernel, all_tgt, 0, 3)
        ins = (parts, xt, yr)
        if h is None:
            base = kernel
            kernel = lambda p, c, r, *refs: base(p, c, r, None, *refs)
        else:
            ins += (h,)
        e, parts = call(
            kernel,
            ins,
            (shape(rs, HALF), shape(n_row, rt // 4, 4, HALF)),
            scratch(ns, nt),
            name="cols",
        )
        parts = over("row", parts)
        h, parts = call(
            functools.partial(lse_kernel, all_src, 3, 0),
            (parts, yt, xr, e),
            (shape(rt, HALF), shape(n_col, rs // 8, 8, HALF)),
            scratch(nt, ns),
            name="rows",
        )
    parts = over("col", parts)
    e, parts = call(
        functools.partial(tgt_part_kernel, all_tgt, dim_tgt),
        (parts, xt, yr, xr, h),
        (shape(rs, HALF), shape(n_row, rt // 4 + blk_tgt, 4, HALF)),
        scratch(ns, nt, HALF),
        name="tgt_part",
    )
    parts = over("row", parts)
    block = (log_src + blk_src, 4, HALF)
    pair = (pltpu.VMEM((2, *block), F32),)
    half = shape(2, *block)
    src_scratch = (
        pltpu.VMEM((DEPTH, ns // 2), BF),
        pltpu.VMEM((1, ns // 2), F32),
        pltpu.VMEM((HALF, ns // 2), F32),
    )
    work = pl.CostEstimate(flops=2 * 2**29, bytes_accessed=2**21, transcendentals=2**20)
    h, half_h, send, tgt = call(
        functools.partial(src_send_kernel, all_src, dim_tgt, grp_tgt),
        (parts, yt, xr, yr, e),
        (shape(rt, HALF), shape(nt, HALF, dtype=BF), half, shape(n_row, blk_tgt, 4, HALF)),
        (pltpu.VMEM((n_row, blk_tgt, 4, HALF), F32), pltpu.SemaphoreType.DMA) + src_scratch,
        name="src_send",
        cost=work,
        out_specs=(VMEM, VMEM, VMEM, HBM),
    )
    tgt = over("row", tgt)
    send = lax.ppermute(send, "col", [(i, i ^ 1) for i in range(n_col)])
    keep = call(
        src_keep_kernel, (half_h, yt, xr, yr, e), half, src_scratch, name="src_keep", cost=work
    )
    parts = call(
        functools.partial(src_join_kernel, log_src, None),
        (keep, send),
        shape(2, *block),
        pair,
        name="src_join",
    )
    came = lax.ppermute(parts[1:], "col", [(i, i ^ 2) for i in range(n_col)])
    f, g, ti = call(
        functools.partial(tgt_end_kernel, dim_tgt),
        (e, h, xsq, ysq, tgt),
        (shape(rs, HALF), shape(rt, HALF), shape(*y.shape)),
        name="tgt_end",
    )
    came, f, g, ti = lax.optimization_barrier((came, f, g, ti))
    parts = call(
        functools.partial(src_join_kernel, log_src, 0),
        (parts, came),
        shape(n_col // near, *block),
        pair,
        name="src_join2",
    )
    parts = over("col", parts, apart)
    src = call(
        functools.partial(src_share_kernel, DIM),
        (parts,),
        shape(near, blk_src, 4, HALF),
        name="src_share",
    )
    src = over("col", src, neighbours)
    si = call(functools.partial(end_kernel, DIM), (src,), shape(*x.shape), name="src_end")
    return f.reshape(ns), g.reshape(nt), si, ti


def solution(mesh):
    in_specs = (P(None, "row"), P(None, "col"))
    out_specs = (P("row"), P("col"), P(None, "row"), P(None, "col"))
    return jax.shard_map(local, mesh=mesh, in_specs=in_specs, out_specs=out_specs, check_vma=False)
```
